128 devices in a mesh: lat: 8 (over z, x_lo), lon: 16 (over y, x_hi, core).
Axes of the slice: x: 4 (x_hi: 2, x_lo: 2; x = x_hi * 2 + x_lo), y: 4, z: 4, core: 2. Of those that a mesh axis runs over, the one named last changes fastest.
Arguments:
- inputs: bfloat16 [256, 2048, 128], P('lat', 'lon'), may hold values from -8 to 8
- cotangent: bfloat16 [256, 2048, 128], P('lat', 'lon'), may hold values from -8 to 8
- w_in: bfloat16 [3, 3, 128, 128], replicated, may hold values from -0.1875 to 0.1875
- w_out: bfloat16 [3, 3, 128, 128], replicated, may hold values from -0.1875 to 0.1875
- w_qkv: bfloat16 [3, 128, 128], replicated, may hold values from -1 to 1
- w_proj: bfloat16 [128, 128], replicated, may hold values from -0.5 to 0.5
Outputs:
- outputs: bfloat16 [256, 2048, 128], P('lat', 'lon')
- grad_inputs: bfloat16 [256, 2048, 128], P('lat', 'lon')
- grad_w_in: float32 [3, 3, 128, 128], replicated
- grad_w_out: float32 [3, 3, 128, 128], replicated
- grad_w_qkv: float32 [3, 128, 128], replicated
- grad_w_proj: float32 [128, 128], replicated
The draws below stay inside these ranges and needn't reach their ends.
All inputs are finite; a program needn't handle non-finite values.
Results may differ from the reference program's by a relative error of at most 0.03.
Values may be sent and summed in bfloat16 or wider, within the bound.
No kernel may reach another device: no remote copies, remote signals or barrier semaphores. Data moves between devices by JAX's collectives and lax.ppermute only.
A program may use at most 128 MiB of HBM per device.

```python
import jax
import jax.numpy as jnp
from jax import lax

C = 128
HEADS = 2
HEAD_DIM = 64
PATCH = 16
NLAT = 256
NLON = 2048


def block_field(key, spread):
    coarse_grid = jax.random.normal(key, (NLAT // PATCH, 1, NLON // PATCH, 1, C), jnp.float32)
    whole_grid = jnp.broadcast_to(coarse_grid, (NLAT // PATCH, PATCH, NLON // PATCH, PATCH, C))
    return spread * whole_grid.reshape(NLAT, NLON, C)


def draw_inputs(key, part):
    key = jax.random.fold_in(key, 11)
    rough_key, block_key = jax.random.split(key)
    rough_part = jax.random.normal(rough_key, (NLAT, NLON, C), jnp.float32)
    whole_field = rough_part + block_field(block_key, 1.5)
    return jnp.clip(whole_field, -8.0, 8.0).astype(jnp.bfloat16)


def draw_cotangent(key, part):
    key = jax.random.fold_in(key, 23)
    rough_key, block_key = jax.random.split(key)
    rough_part = jax.random.normal(rough_key, (NLAT, NLON, C), jnp.float32)
    whole_field = rough_part + block_field(block_key, 0.5)
    return jnp.clip(whole_field, -8.0, 8.0).astype(jnp.bfloat16)


def normal_values(rng, dims, scale, bound, held_as=jnp.bfloat16):
    array = jax.random.normal(rng, dims, jnp.float32) * scale
    return jnp.minimum(jnp.maximum(array, -bound), bound).astype(held_as)


def setup_inputs(seed: int = 0) -> dict:
    keys = jax.random.split(jax.random.key(seed), 7)
    inputs = draw_inputs(jax.random.fold_in(keys[6], 71), 0)
    cotangent = draw_cotangent(jax.random.fold_in(keys[6], 71), 0)
    w_in = normal_values(keys[2], (3, 3, C, C), (9 * C) ** -0.5, 0.1875)
    w_out = normal_values(keys[3], (3, 3, C, C), (9 * C) ** -0.5, 0.1875)
    w_qkv = normal_values(keys[4], (3, C, C), (C // 3) ** -0.5, 1.0)
    w_proj = normal_values(keys[5], (C, C), C ** -0.5, 0.5)
    return dict(inputs=inputs, cotangent=cotangent, w_in=w_in, w_out=w_out, w_qkv=w_qkv, w_proj=w_proj)


def pad_cells(field):
    rows = jnp.pad(field, ((1, 1), (0, 0), (0, 0)))
    return jnp.pad(rows, ((0, 0), (1, 1), (0, 0)), mode="wrap")


def conv_forward(padded, weight, row_count, col_count):
    chans = padded.shape[2]
    total = jnp.zeros((row_count * col_count, weight.shape[3]), jnp.float32)
    for row_off in range(3):
        for col_off in range(3):
            piece = padded[row_off:row_off + row_count, col_off:col_off + col_count].reshape(-1, chans)
            total = total + jnp.dot(piece, weight[row_off, col_off], preferred_element_type=jnp.float32)
    return total


def conv_inward(padded, weight, row_count, col_count):
    chans = padded.shape[2]
    total = jnp.zeros((row_count * col_count, weight.shape[2]), jnp.float32)
    for row_off in range(3):
        for col_off in range(3):
            piece = padded[2 - row_off:2 - row_off + row_count, 2 - col_off:2 - col_off + col_count].reshape(-1, chans)
            total = total + jnp.dot(piece, weight[row_off, col_off].T, preferred_element_type=jnp.float32)
    return total


def conv_weights(padded, grad_flat, row_count, col_count):
    chans = padded.shape[2]
    blocks = []
    for row_off in range(3):
        for col_off in range(3):
            piece = padded[row_off:row_off + row_count, col_off:col_off + col_count].reshape(-1, chans)
            blocks.append(lax.dot_general(piece, grad_flat, (((0,), (0,)), ((), ())), preferred_element_type=jnp.float32))
    return jnp.stack(blocks).reshape(3, 3, chans, grad_flat.shape[1])


def block_sum(flat, row_count, col_count):
    grid = flat.reshape(row_count // PATCH, PATCH, col_count // PATCH, PATCH, -1)
    return jnp.sum(grid, axis=(1, 3)).reshape(-1, grid.shape[4])


def spread_out(coarse, row_count, col_count):
    grid = coarse.reshape(row_count // PATCH, 1, col_count // PATCH, 1, -1)
    grid = jnp.broadcast_to(grid, (row_count // PATCH, PATCH, col_count // PATCH, PATCH, grid.shape[4]))
    return grid.reshape(row_count * col_count, -1)


def reference(inputs, cotangent, w_in, w_out, w_qkv, w_proj):
    row_count, col_count, chans = inputs.shape
    score_scale = HEAD_DIM ** -0.5
    highest = lax.Precision.HIGHEST
    in_pad = pad_cells(inputs)
    hidden = conv_forward(in_pad, w_in, row_count, col_count)
    activated = jax.nn.silu(hidden).astype(jnp.bfloat16)
    tokens = (block_sum(activated.astype(jnp.float32), row_count, col_count) / (PATCH * PATCH)).astype(jnp.bfloat16)
    queries = jnp.dot(tokens, w_qkv[0], preferred_element_type=jnp.float32).astype(jnp.bfloat16)
    key_all = jnp.dot(tokens, w_qkv[1], preferred_element_type=jnp.float32).astype(jnp.bfloat16)
    value_all = jnp.dot(tokens, w_qkv[2], preferred_element_type=jnp.float32).astype(jnp.bfloat16)
    query_h = queries.reshape(-1, HEADS, HEAD_DIM).astype(jnp.float32)
    key_h = key_all.reshape(-1, HEADS, HEAD_DIM).astype(jnp.float32)
    value_h = value_all.reshape(-1, HEADS, HEAD_DIM).astype(jnp.float32)
    scores = jnp.einsum("qhd,khd->hqk", query_h, key_h) * score_scale
    attn_prob = jax.nn.softmax(scores, axis=-1)
    prob_low = attn_prob.astype(jnp.bfloat16)
    mixed = jnp.einsum("hqk,khd->qhd", prob_low.astype(jnp.float32), value_h).reshape(-1, chans).astype(jnp.bfloat16)
    coarse = tokens.astype(jnp.float32) + jnp.dot(mixed, w_proj, preferred_element_type=jnp.float32)
    merged = (activated.astype(jnp.float32) + spread_out(coarse, row_count, col_count)).astype(jnp.bfloat16)
    merged_pad = pad_cells(merged.reshape(row_count, col_count, chans))
    outputs = conv_forward(merged_pad, w_out, row_count, col_count).astype(jnp.bfloat16)
    grad_pad = pad_cells(cotangent)
    grad_merged = conv_inward(grad_pad, w_out, row_count, col_count)
    grad_w_out = conv_weights(merged_pad, cotangent.reshape(-1, chans), row_count, col_count)
    grad_coarse = block_sum(grad_merged, row_count, col_count)
    coarse_low = grad_coarse.astype(jnp.bfloat16)
    grad_w_proj = lax.dot_general(mixed, coarse_low, (((0,), (0,)), ((), ())), preferred_element_type=jnp.float32)
    grad_mixed = jnp.dot(coarse_low, w_proj.T, preferred_element_type=jnp.float32).astype(jnp.bfloat16)
    mixed_h = grad_mixed.reshape(-1, HEADS, HEAD_DIM).astype(jnp.float32)
    grad_prob = jnp.einsum("qhd,khd->hqk", mixed_h, value_h)
    grad_score = (attn_prob * (grad_prob - jnp.sum(attn_prob * grad_prob, axis=-1, keepdims=True)) * score_scale).astype(jnp.bfloat16).astype(jnp.float32)
    grad_q = jnp.einsum("hqk,khd->qhd", grad_score, key_h).reshape(-1, chans)
    grad_k = jnp.einsum("hqk,qhd->khd", grad_score, query_h).reshape(-1, chans)
    grad_v = jnp.einsum("hqk,qhd->khd", prob_low.astype(jnp.float32), mixed_h).reshape(-1, chans)
    wide_qkv = w_qkv.astype(jnp.float32)
    grad_tokens = grad_coarse + jnp.dot(grad_q, wide_qkv[0].T, precision=highest)
    grad_tokens = grad_tokens + jnp.dot(grad_k, wide_qkv[1].T, precision=highest) + jnp.dot(grad_v, wide_qkv[2].T, precision=highest)
    tokens_wide = tokens.astype(jnp.float32)
    grad_w_qkv = jnp.stack([jnp.dot(tokens_wide.T, grad_q, precision=highest), jnp.dot(tokens_wide.T, grad_k, precision=highest), jnp.dot(tokens_wide.T, grad_v, precision=highest)])
    sigma = jax.nn.sigmoid(hidden)
    grad_act = grad_merged + spread_out(grad_tokens, row_count, col_count) / (PATCH * PATCH)
    grad_hidden = (grad_act * sigma * (1.0 + hidden * (1.0 - sigma))).astype(jnp.bfloat16)
    hidden_pad = pad_cells(grad_hidden.reshape(row_count, col_count, chans))
    grad_inputs = conv_inward(hidden_pad, w_in, row_count, col_count).astype(jnp.bfloat16)
    grad_w_in = conv_weights(in_pad, grad_hidden, row_count, col_count)
    shape = (row_count, col_count, chans)
    return outputs.reshape(shape), grad_inputs.reshape(shape), grad_w_in, grad_w_out, grad_w_qkv, grad_w_proj
```

```python
import jax
import jax.numpy as jnp
from jax import lax
from jax.sharding import PartitionSpec as P

HEADS = 2
HEAD_DIM = 64
PATCH = 16
DEVICES = 128


def with_halo(shard, sides, width, wrap):
    for axis, dim in sides:
        count, length = (lax.axis_size(axis), shard.shape[dim])
        up = [(i, (i + 1) % count) for i in range(count if wrap else count - 1)]
        down = [(j, i) for i, j in up]
        last = lax.slice_in_dim(shard, length - width, length, axis=dim)
        initial = lax.slice_in_dim(shard, 0, width, axis=dim)
        before = lax.ppermute(last, axis, up)
        after = lax.ppermute(initial, axis, down)
        shard = jnp.concatenate([before, shard, after], axis=dim)
    return shard


def gather_all(local):
    copies = jnp.broadcast_to(local[None], (DEVICES,) + local.shape)
    copies = copies.reshape((-1,) + local.shape[1:])
    return lax.all_to_all(copies, ("lat", "lon"), 0, 0, tiled=True)


def scatter_sum(partial):
    moved = lax.all_to_all(partial.astype(jnp.bfloat16), ("lat", "lon"), 0, 0, tiled=True)
    moved = moved.reshape(DEVICES, -1, partial.shape[1])
    return jnp.sum(moved.astype(jnp.float32), axis=0)


def pad_cells(field):
    rows = with_halo(field, (("lat", 0),), 1, False)
    return with_halo(rows, (("lon", 1),), 1, True)


def conv_forward(padded, weight, row_count, col_count):
    chans = padded.shape[2]
    total = jnp.zeros((row_count * col_count, weight.shape[3]), jnp.float32)
    for row_off in range(3):
        for col_off in range(3):
            piece = padded[row_off : row_off + row_count, col_off : col_off + col_count].reshape(
                -1, chans
            )
            total = total + jnp.dot(
                piece, weight[row_off, col_off], preferred_element_type=jnp.float32
            )
    return total


def conv_inward(padded, weight, row_count, col_count):
    chans = padded.shape[2]
    total = jnp.zeros((row_count * col_count, weight.shape[2]), jnp.float32)
    for row_off in range(3):
        for col_off in range(3):
            piece = padded[
                2 - row_off : 2 - row_off + row_count, 2 - col_off : 2 - col_off + col_count
            ].reshape(-1, chans)
            total = total + jnp.dot(
                piece, weight[row_off, col_off].T, preferred_element_type=jnp.float32
            )
    return total


def conv_weights(padded, grad_flat, row_count, col_count):
    chans = padded.shape[2]
    blocks = []
    for row_off in range(3):
        for col_off in range(3):
            piece = padded[row_off : row_off + row_count, col_off : col_off + col_count].reshape(
                -1, chans
            )
            blocks.append(
                lax.dot_general(
                    piece, grad_flat, (((0,), (0,)), ((), ())), preferred_element_type=jnp.float32
                )
            )
    return jnp.stack(blocks).reshape(3, 3, chans, grad_flat.shape[1])


def block_sum(flat, row_count, col_count):
    grid = flat.reshape(row_count // PATCH, PATCH, col_count // PATCH, PATCH, -1)
    return jnp.sum(grid, axis=(1, 3)).reshape(-1, grid.shape[4])


def spread_out(coarse, row_count, col_count):
    grid = coarse.reshape(row_count // PATCH, 1, col_count // PATCH, 1, -1)
    grid = jnp.broadcast_to(
        grid, (row_count // PATCH, PATCH, col_count // PATCH, PATCH, grid.shape[4])
    )
    return grid.reshape(row_count * col_count, -1)


def body(inputs, cotangent, w_in, w_out, w_qkv, w_proj):
    row_count, col_count, chans = inputs.shape
    score_scale = HEAD_DIM ** (-0.5)
    highest = lax.Precision.HIGHEST
    in_pad = pad_cells(inputs)
    hidden = conv_forward(in_pad, w_in, row_count, col_count)
    activated = jax.nn.silu(hidden).astype(jnp.bfloat16)
    tokens = (
        block_sum(activated.astype(jnp.float32), row_count, col_count) / (PATCH * PATCH)
    ).astype(jnp.bfloat16)
    queries = jnp.dot(tokens, w_qkv[0], preferred_element_type=jnp.float32).astype(jnp.bfloat16)
    key_local = jnp.dot(tokens, w_qkv[1], preferred_element_type=jnp.float32).astype(jnp.bfloat16)
    value_local = jnp.dot(tokens, w_qkv[2], preferred_element_type=jnp.float32).astype(jnp.bfloat16)
    both = gather_all(jnp.concatenate([key_local, value_local], axis=1))
    key_all, value_all = (both[:, :chans], both[:, chans:])
    query_h = queries.reshape(-1, HEADS, HEAD_DIM)
    key_h = key_all.reshape(-1, HEADS, HEAD_DIM)
    value_h = value_all.reshape(-1, HEADS, HEAD_DIM)
    scores = (
        jnp.einsum("qhd,khd->hqk", query_h, key_h, preferred_element_type=jnp.float32) * score_scale
    )
    attn_prob = jax.nn.softmax(scores, axis=-1)
    prob_low = attn_prob.astype(jnp.bfloat16)
    mixed = (
        jnp.einsum("hqk,khd->qhd", prob_low, value_h, preferred_element_type=jnp.float32)
        .reshape(-1, chans)
        .astype(jnp.bfloat16)
    )
    coarse = tokens.astype(jnp.float32) + jnp.dot(mixed, w_proj, preferred_element_type=jnp.float32)
    merged = (activated.astype(jnp.float32) + spread_out(coarse, row_count, col_count)).astype(
        jnp.bfloat16
    )
    merged_pad = pad_cells(merged.reshape(row_count, col_count, chans))
    outputs = conv_forward(merged_pad, w_out, row_count, col_count).astype(jnp.bfloat16)
    grad_pad = pad_cells(cotangent)
    grad_merged = conv_inward(grad_pad, w_out, row_count, col_count)
    grad_w_out = conv_weights(merged_pad, cotangent.reshape(-1, chans), row_count, col_count)
    grad_coarse = block_sum(grad_merged, row_count, col_count)
    coarse_low = grad_coarse.astype(jnp.bfloat16)
    grad_w_proj = lax.dot_general(
        mixed, coarse_low, (((0,), (0,)), ((), ())), preferred_element_type=jnp.float32
    )
    grad_mixed = jnp.dot(coarse_low, w_proj.T, preferred_element_type=jnp.float32).astype(
        jnp.bfloat16
    )
    mixed_h = grad_mixed.reshape(-1, HEADS, HEAD_DIM)
    grad_prob = jnp.einsum("qhd,khd->hqk", mixed_h, value_h, preferred_element_type=jnp.float32)
    grad_score = (
        attn_prob
        * (grad_prob - jnp.sum(attn_prob * grad_prob, axis=-1, keepdims=True))
        * score_scale
    ).astype(jnp.bfloat16)
    grad_q = jnp.einsum(
        "hqk,khd->qhd", grad_score, key_h, preferred_element_type=jnp.float32
    ).reshape(-1, chans)
    part_k = jnp.einsum(
        "hqk,qhd->khd", grad_score, query_h, preferred_element_type=jnp.float32
    ).reshape(-1, chans)
    part_v = jnp.einsum(
        "hqk,qhd->khd", prob_low, mixed_h, preferred_element_type=jnp.float32
    ).reshape(-1, chans)
    wide_qkv = w_qkv.astype(jnp.float32)
    tokens_wide = tokens.astype(jnp.float32)
    grad_tokens = grad_coarse + jnp.dot(grad_q, wide_qkv[0].T, precision=highest)
    grad_kv = scatter_sum(jnp.concatenate([part_k, part_v], axis=1))
    grad_k, grad_v = (grad_kv[:, :chans], grad_kv[:, chans:])
    grad_tokens = (
        grad_tokens
        + jnp.dot(grad_k, wide_qkv[1].T, precision=highest)
        + jnp.dot(grad_v, wide_qkv[2].T, precision=highest)
    )
    grad_wk = jnp.dot(tokens_wide.T, grad_k, precision=highest)
    grad_wv = jnp.dot(tokens_wide.T, grad_v, precision=highest)
    grad_wq = jnp.dot(tokens_wide.T, grad_q, precision=highest)
    grad_w_qkv = jnp.stack([grad_wq, grad_wk, grad_wv])
    sigma = jax.nn.sigmoid(hidden)
    grad_act = grad_merged + spread_out(grad_tokens, row_count, col_count) / (PATCH * PATCH)
    grad_hidden = (grad_act * sigma * (1.0 + hidden * (1.0 - sigma))).astype(jnp.bfloat16)
    hidden_pad = pad_cells(grad_hidden.reshape(row_count, col_count, chans))
    grad_inputs = conv_inward(hidden_pad, w_in, row_count, col_count).astype(jnp.bfloat16)
    grad_w_in = conv_weights(in_pad, grad_hidden, row_count, col_count)
    parts = (grad_w_in, grad_w_out, grad_w_qkv, grad_w_proj)
    flat = jnp.concatenate([part.reshape(-1, chans) for part in parts], axis=0)
    summed = gather_all(scatter_sum(flat).astype(jnp.bfloat16)).astype(jnp.float32)
    ends = [9 * chans, 18 * chans, 21 * chans]
    grad_w_in, grad_w_out, grad_w_qkv, grad_w_proj = (
        piece.reshape(part.shape) for piece, part in zip(jnp.split(summed, ends), parts)
    )
    shape = (row_count, col_count, chans)
    return (
        outputs.reshape(shape),
        grad_inputs.reshape(shape),
        grad_w_in,
        grad_w_out,
        grad_w_qkv,
        grad_w_proj,
    )


def solution(mesh):
    in_specs = (P("lat", "lon", None), P("lat", "lon", None), P(), P(), P(), P())
    out_specs = (P("lat", "lon", None), P("lat", "lon", None), P(), P(), P(), P())
    return jax.shard_map(body, mesh=mesh, in_specs=in_specs, out_specs=out_specs, check_vma=False)
```

```python
import functools

import jax
import jax.numpy as jnp
from jax import lax
from jax.experimental import pallas as pl
from jax.experimental.pallas import tpu as pltpu
from jax.sharding import PartitionSpec as P

HEADS = 2
HEAD_DIM = 64
PATCH = 16
DEVICES = 128
AXES = ("lat", "lon")
EDGE = 8
HIGHEST = lax.Precision.HIGHEST
F32 = jnp.float32
BF16 = jnp.bfloat16
NT = (((1,), (1,)), ((), ()))
TN = (((0,), (0,)), ((), ()))


def call(kernel, outs, scratch=(), flops=0, in_specs=None):
    return pl.pallas_call(
        kernel,
        out_shape=outs,
        **({"in_specs": in_specs} if in_specs else {}),
        scratch_shapes=list(scratch),
        compiler_params=pltpu.CompilerParams(vmem_limit_bytes=48 * 2**20),
        cost_estimate=pl.CostEstimate(flops=flops, bytes_accessed=8 * 2**20, transcendentals=0),
    )


def put_shifted(taps, pair, odd, field):
    chans = field.shape[1]
    width = field.shape[0]
    wide = field.astype(F32)
    base = odd * 3 * chans
    taps[pair, :, base : base + chans] = pltpu.roll(wide, 1, 0).astype(BF16)
    taps[pair, :, base + chans : base + 2 * chans] = field.astype(BF16)
    taps[pair, :, base + 2 * chans : base + 3 * chans] = pltpu.roll(wide, width - 1, 0).astype(BF16)


def pair_conv(taps, pair, weight):
    half = weight.shape[0] // 2
    low = jnp.dot(taps[pair], weight[:half], preferred_element_type=F32)
    return low + jnp.dot(taps[pair + 1], weight[half:], preferred_element_type=F32)


def pair_weight(weight):
    taps = weight.reshape(3, -1, weight.shape[3])
    none = jnp.zeros_like(taps[:1])
    left = jnp.concatenate([taps, none], axis=0)
    right = jnp.concatenate([none, taps], axis=0)
    return jnp.concatenate([left, right], axis=2).reshape(-1, 2 * weight.shape[3])


def flipped(weight):
    return jnp.flip(weight, axis=(0, 1)).transpose(0, 1, 3, 2)


def spread_row(grid_row):
    chans = grid_row.shape[1]
    parts = [jnp.broadcast_to(grid_row[15:16], (EDGE, chans))]
    for col in range(8):
        parts.append(jnp.broadcast_to(grid_row[col : col + 1], (PATCH, chans)))
    parts.append(jnp.broadcast_to(grid_row[8:9], (EDGE, chans)))
    return jnp.concatenate(parts, axis=0)


def patch_sums(field, first):
    sums = []
    for row in range(2):
        total = field[first + row * PATCH].astype(F32)
        for step in range(1, PATCH):
            total = total + field[first + row * PATCH + step].astype(F32)
        inner = total[EDGE : EDGE + 8 * PATCH]
        sums.append(jnp.sum(inner.reshape(8, PATCH, -1), axis=1))
    return jnp.concatenate(sums, axis=0)


def encode_kernel(field, weight, act, slope, tokens, taps):
    pairs = taps.shape[0]
    chans = field.shape[2]
    for pair in range(pairs):
        for odd in range(2):
            put_shifted(taps, pair, odd, field[2 * pair + odd])

    def step(pair, carry):
        both = pair_conv(taps, pair, weight)
        for odd in range(2):
            hidden = both[:, odd * chans : (odd + 1) * chans]
            sigma = jax.nn.sigmoid(hidden)
            act[2 * pair + odd] = (hidden * sigma).astype(BF16)
            slope[2 * pair + odd] = (sigma * (1.0 + hidden * (1.0 - sigma))).astype(BF16)
        return carry

    lax.fori_loop(0, pairs - 1, step, 0)
    tokens[...] = (patch_sums(act, 1) / (PATCH * PATCH)).astype(BF16)


def back_kernel(field, weight, grad, coarse, taps):
    pairs = taps.shape[0]
    chans = field.shape[2]
    for pair in range(pairs):
        for odd in range(2):
            put_shifted(taps, pair, odd, field[2 * pair + odd])

    def step(pair, carry):
        both = pair_conv(taps, pair, weight)
        for odd in range(2):
            grad[2 * pair + odd] = both[:, odd * chans : (odd + 1) * chans]
        return carry

    lax.fori_loop(0, pairs - 1, step, 0)
    coarse[...] = patch_sums(grad, 1)


def near_index(place, shape, dim):
    entry = lax.broadcasted_iota(jnp.int32, shape, dim)
    row = 2 * place[0] + (((entry >> 4) + 1) & 3) - 1
    row = jnp.clip(row, 0, 15)
    col = (8 * place[1] + (((entry & 15) + 4) & 15) - 4) & 127
    device = (row >> 1) * 16 + (col >> 3)
    return device * 16 + (row & 1) * 8 + (col & 7)


def pick_near(place, table):
    count = table.shape[0]
    index = near_index(place, (64, count), 0)
    lane = lax.broadcasted_iota(jnp.int32, (64, count), 1)
    chosen = jnp.where(index == lane, 1.0, 0.0).astype(BF16)
    return jnp.dot(chosen, table, preferred_element_type=F32).astype(BF16)


def by_head(rows):
    lane = lax.broadcasted_iota(jnp.int32, rows.shape, 1)
    wide = rows.astype(F32)
    first = jnp.where(lane < HEAD_DIM, wide, 0.0)
    second = jnp.where(lane < HEAD_DIM, 0.0, wide)
    return jnp.concatenate([first, second], axis=0).astype(BF16)


def join_heads(rows):
    half = rows.shape[0] // 2
    lane = lax.broadcasted_iota(jnp.int32, (half, rows.shape[1]), 1)
    return jnp.where(lane < HEAD_DIM, rows[:half], rows[half:])


def low_dot(a, b):
    return jnp.dot(a, b, preferred_element_type=F32).astype(BF16)


def own_rows(near):
    return jnp.concatenate([near[0:8], near[16:24]], axis=0)


def split_three(value):
    high = value.astype(BF16)
    rest = value - high.astype(F32)
    mid = rest.astype(BF16)
    return high, mid, (rest - mid.astype(F32)).astype(BF16)


def attend_kernel(place, tokens, w_qkv, w_proj, grad_coarse, coarse, message, grad_proj, soft):
    scale = HEAD_DIM**-0.5
    near = pick_near(place, tokens[...])
    keys = low_dot(tokens[...], w_qkv[1])
    values = low_dot(tokens[...], w_qkv[2])
    queries = by_head(low_dot(near, w_qkv[0]))
    scores = lax.dot_general(queries, keys, NT, preferred_element_type=F32) * scale
    top = jnp.max(scores, axis=1, keepdims=True)
    weights = jnp.exp(scores - top)
    total = jnp.sum(weights, axis=1, keepdims=True)
    prob = (weights / total).astype(BF16)
    mixed_wide = join_heads(jnp.dot(prob, values, preferred_element_type=F32))
    mixed = mixed_wide.astype(BF16)
    coarse[...] = near.astype(F32) + jnp.dot(mixed, w_proj[...], preferred_element_type=F32)
    log_sum = top + jnp.log(total)
    soft[...] = log_sum
    coarse_low = grad_coarse[...].astype(BF16)
    grad_proj[...] = lax.dot_general(
        own_rows(mixed), coarse_low, TN, preferred_element_type=F32
    )
    grad_mixed = lax.dot_general(coarse_low, w_proj[...], NT, preferred_element_type=F32)
    product = grad_mixed.astype(BF16).astype(F32) * own_rows(mixed_wide)
    lane = lax.broadcasted_iota(jnp.int32, product.shape, 1)
    inner = [
        jnp.sum(jnp.where(lane < HEAD_DIM, product, 0.0), axis=1, keepdims=True),
        jnp.sum(jnp.where(lane < HEAD_DIM, 0.0, product), axis=1, keepdims=True),
    ]
    logs = [own_rows(log_sum[:64]), own_rows(log_sum[64:])]
    token = lax.broadcasted_iota(jnp.int32, product.shape, 0)
    rows = []
    for pair in (logs, inner):
        row = jnp.zeros((1, 128), F32)
        for head in range(HEADS):
            for part, value in enumerate(split_three(pair[head])):
                slot = (head * 3 + part) * 16
                at = jnp.where(lane == token + slot, value.astype(F32), 0.0)
                row = row + jnp.sum(at, axis=0, keepdims=True)
        rows.append(row)
    blank = jnp.zeros((14, 128), F32)
    message[...] = jnp.concatenate([coarse_low.astype(F32)] + rows + [blank], axis=0).astype(BF16)


def lane_stats(sums, head):
    count = sums.shape[0] * 16
    slot = lax.broadcasted_iota(jnp.int32, (128, count), 0)
    lane = lax.broadcasted_iota(jnp.int32, (128, count), 1)
    part = slot >> 4
    wanted = ((slot & 15) == (lane & 15)) & (part >= 3 * head) & (part < 3 * head + 3)
    chosen = jnp.where(wanted, 1.0, 0.0).astype(BF16)
    tiled = jnp.dot(sums, chosen, preferred_element_type=F32)
    device = lax.broadcasted_iota(jnp.int32, tiled.shape, 0)
    lane = lax.broadcasted_iota(jnp.int32, tiled.shape, 1)
    return jnp.sum(jnp.where(device == (lane >> 4), tiled, 0.0), axis=0, keepdims=True)


def attend_back_kernel(
    place, tokens, coarse_low, logs, inner, soft, grad_coarse, w_qkv, w_proj, grad_tokens, grad_qkv
):
    scale = HEAD_DIM**-0.5
    near = pick_near(place, tokens[...])
    near_low = pick_near(place, coarse_low[...])
    queries = low_dot(tokens[...], w_qkv[0])
    keys = low_dot(tokens[...], w_qkv[1])
    values = low_dot(tokens[...], w_qkv[2])
    mixed = lax.dot_general(
        coarse_low[...], w_proj[...], NT, preferred_element_type=F32
    ).astype(BF16)
    near_mixed = lax.dot_general(
        near_low, w_proj[...], NT, preferred_element_type=F32
    ).astype(BF16)
    near_q = by_head(low_dot(near, w_qkv[0]))
    scores = lax.dot_general(near_q, keys, NT, preferred_element_type=F32) * scale
    prob = jnp.exp(scores - soft[...])
    grad_prob = lax.dot_general(by_head(near_mixed), values, NT, preferred_element_type=F32)
    mean = jnp.sum(prob * grad_prob, axis=1, keepdims=True)
    grad_score = (prob * (grad_prob - mean) * scale).astype(BF16)
    grad_q = join_heads(jnp.dot(grad_score, keys, preferred_element_type=F32))
    near_k = by_head(low_dot(near, w_qkv[1]))
    near_v = by_head(low_dot(near, w_qkv[2]))
    count = tokens.shape[0]

    def both_heads(table):
        first = jnp.broadcast_to(lane_stats(table, 0), (64, count))
        second = jnp.broadcast_to(lane_stats(table, 1), (64, count))
        return jnp.concatenate([first, second], axis=0)

    scores = lax.dot_general(near_k, queries, NT, preferred_element_type=F32) * scale
    prob = jnp.exp(scores - both_heads(logs[...]))
    grad_prob = lax.dot_general(near_v, mixed, NT, preferred_element_type=F32)
    grad_score = (prob * (grad_prob - both_heads(inner[...])) * scale).astype(BF16)
    grad_k = join_heads(jnp.dot(grad_score, queries, preferred_element_type=F32))
    grad_v = join_heads(jnp.dot(prob.astype(BF16), mixed, preferred_element_type=F32))
    own = jnp.concatenate(
        [grad_coarse[0:8], near_low[8:16].astype(F32), grad_coarse[8:16]], axis=0
    )
    result = jnp.concatenate([own, near_low[24:].astype(F32)], axis=0)
    own_tokens = own_rows(near.astype(F32))
    for index, grad in enumerate((grad_q, grad_k, grad_v)):
        wide = w_qkv[index].astype(F32)
        result = result + lax.dot_general(
            grad, wide, NT, precision=HIGHEST, preferred_element_type=F32
        )
        grad_qkv[index] = lax.dot_general(
            own_tokens, own_rows(grad), TN, precision=HIGHEST, preferred_element_type=F32
        )
    grad_tokens[...] = result


def row_of(index):
    if index == 0:
        return 3
    return min((index - 1) // PATCH, 2)


def inside(place, index, rows):
    if index == 0:
        return jnp.where(place[0] == 0, 0.0, 1.0)
    if index == rows - 1:
        return jnp.where(place[0] == 7, 0.0, 1.0)
    return None


def put_products(grads, field, rows):
    chans = field.shape[2]
    width = field.shape[1]
    column = lax.broadcasted_iota(jnp.int32, (width, chans), 0)
    own = (column >= EDGE) & (column < width - EDGE)
    zero = jnp.zeros((width, chans), BF16)
    for row in range(-1, rows + 3):
        kept = zero
        if 0 < row < rows + 1:
            kept = jnp.where(own, field[row].astype(F32), 0.0).astype(BF16)
        for tap in range(3):
            target = row - 1 + tap
            if 0 <= target < rows + 2:
                odd, place = target & 1, target >> 1
                grads[odd, place, :, tap * chans : (tap + 1) * chans] = kept


def weight_grads(taps, grads, starts, result):
    chans = result.shape[2]
    count, width = grads.shape[1], grads.shape[2]
    total = jnp.zeros((3 * chans, 3 * chans), F32)
    for odd in range(2):
        lanes = starts[odd][1] * 3 * chans
        first = starts[odd][0]
        left = taps[first : first + count, :, lanes : lanes + 3 * chans]
        left = left.reshape(count * width, 3 * chans)
        right = grads[odd].reshape(count * width, 3 * chans)
        total = total + lax.dot_general(left, right, TN, preferred_element_type=F32)
    for tap in range(3):
        result[tap] = total[:, tap * chans : (tap + 1) * chans]


def decode_kernel(place, act, coarse, cotangent, weight, outputs, grad_weight, taps, grads):
    rows = act.shape[0]
    chans = act.shape[2]
    grid = [spread_row(coarse[16 * row : 16 * (row + 1)]) for row in range(4)]
    for index in range(rows):
        merged = act[index].astype(F32) + grid[row_of(index)]
        factor = inside(place, index, rows)
        if factor is not None:
            merged = merged * factor
        put_shifted(taps, index >> 1, index & 1, merged.astype(BF16))

    def step(pair, carry):
        both = pair_conv(taps, pair, weight)
        for odd in range(2):
            lanes = both[EDGE : EDGE + 128, odd * chans : (odd + 1) * chans]
            outputs[2 * pair + odd] = lanes.astype(BF16)
        return carry

    lax.fori_loop(0, rows // 2 - 1, step, 0)
    put_products(grads, cotangent, rows - 2)
    weight_grads(taps, grads, ((0, 0), (0, 1)), grad_weight)


def hidden_kernel(place, slope, grad, grad_tokens, field, result, grad_weight, taps, grads):
    rows = slope.shape[0]
    grid = [
        spread_row(grad_tokens[16 * row : 16 * (row + 1)] * (1.0 / (PATCH * PATCH)))
        for row in range(4)
    ]
    for index in range(rows):
        value = (grad[index] + grid[row_of(index)]) * slope[index].astype(F32)
        factor = inside(place, index, rows)
        if factor is not None:
            value = value * factor
        result[index] = value.astype(BF16)
    for pair in range(taps.shape[0]):
        for odd in range(2):
            put_shifted(taps, pair, odd, field[2 * pair + odd])
    put_products(grads, result, rows - 2)
    weight_grads(taps, grads, ((0, 1), (1, 0)), grad_weight)


def inward_kernel(field, weight, result, taps):
    rows = field.shape[0]
    chans = field.shape[2]
    for index in range(rows):
        put_shifted(taps, index >> 1, index & 1, field[index])

    def step(pair, carry):
        both = pair_conv(taps, pair, weight)
        for odd in range(2):
            lanes = both[EDGE : EDGE + 128, odd * chans : (odd + 1) * chans]
            result[2 * pair + odd] = lanes.astype(BF16)
        return carry

    lax.fori_loop(0, rows // 2 - 1, step, 0)


def gather_all(local):
    copies = jnp.broadcast_to(local[None], (DEVICES,) + local.shape)
    copies = copies.reshape((-1,) + local.shape[1:])
    return lax.all_to_all(copies, AXES, 0, 0, tiled=True)


def scatter_sum(partial):
    moved = lax.all_to_all(partial.astype(BF16), AXES, 0, 0, tiled=True)
    moved = moved.reshape(DEVICES, -1, partial.shape[1])
    return jnp.sum(moved.astype(F32), axis=0)


def widen(inputs, cotangent):
    rows, cols, _ = inputs.shape
    lats, lons = lax.axis_size("lat"), lax.axis_size("lon")
    up = [(i, i + 1) for i in range(lats - 1)]
    down = [(i + 1, i) for i in range(lats - 1)]
    last = jnp.concatenate([inputs[rows - 2 :], cotangent[rows - 2 :]], axis=0)
    first = jnp.concatenate([inputs[:2], cotangent[:2]], axis=0)
    before = lax.ppermute(last, "lat", up)
    after = lax.ppermute(first, "lat", down)
    tall = jnp.concatenate(
        [before[:2], inputs, after[:2], before[2:], cotangent, after[2:]], axis=0
    )
    east = [(i, (i + 1) % lons) for i in range(lons)]
    west = [((i + 1) % lons, i) for i in range(lons)]
    left = lax.ppermute(tall[:, cols - EDGE :], "lon", east)
    right = lax.ppermute(tall[:, :EDGE], "lon", west)
    wide = jnp.concatenate([left, tall, right], axis=1)
    return wide[: rows + 4], wide[rows + 4 :]


def body(inputs, cotangent, w_in, w_out, w_qkv, w_proj):
    rows, cols, chans = inputs.shape
    width = cols + 2 * EDGE
    place = jnp.stack([lax.axis_index("lat"), lax.axis_index("lon")]).astype(jnp.int32)
    shape = jax.ShapeDtypeStruct
    whole = pl.BlockSpec(memory_space=pltpu.VMEM)
    scalars = pl.BlockSpec(memory_space=pltpu.SMEM)
    conv_flops = 2 * rows * cols * 9 * chans * chans

    def taps(count):
        return pltpu.VMEM((count // 2, width, 6 * chans), BF16)

    def grads():
        return pltpu.VMEM((2, rows // 2 + 1, width, 3 * chans), BF16)

    in_wide, cot_wide = widen(inputs, cotangent)
    act, slope, tokens = call(
        encode_kernel,
        (
            shape((rows + 2, width, chans), BF16),
            shape((rows + 2, width, chans), BF16),
            shape((16, chans), BF16),
        ),
        [taps(rows + 4)],
        conv_flops,
    )(in_wide, pair_weight(w_in))
    tokens_all = gather_all(tokens)
    grad_merged, grad_coarse = call(
        back_kernel,
        (shape((rows + 2, width, chans), F32), shape((16, chans), F32)),
        [taps(rows + 4)],
        conv_flops,
    )(cot_wide, pair_weight(flipped(w_out)))
    coarse, message, grad_w_proj, soft = call(
        attend_kernel,
        (
            shape((64, chans), F32),
            shape((32, chans), BF16),
            shape((chans, chans), F32),
            shape((128, 1), F32),
        ),
        flops=2**28,
        in_specs=[scalars] + [whole] * 4,
    )(place, tokens_all, w_qkv, w_proj, grad_coarse)
    moved = gather_all(message[:18]).reshape(DEVICES, 18, chans)
    coarse_low = moved[:, :16].reshape(-1, chans)
    logs, inner = moved[:, 16], moved[:, 17]
    outputs, grad_w_out = call(
        decode_kernel,
        (shape((rows, cols, chans), BF16), shape((3, 3 * chans, chans), F32)),
        [taps(rows + 2), grads()],
        2 * conv_flops,
        in_specs=[scalars] + [whole] * 4,
    )(place, act, coarse, cot_wide[1 : rows + 3], pair_weight(w_out))
    grad_tokens, grad_w_qkv = call(
        attend_back_kernel,
        (shape((64, chans), F32), shape((3, chans, chans), F32)),
        flops=2**29,
        in_specs=[scalars] + [whole] * 8,
    )(place, tokens_all, coarse_low, logs, inner, soft, grad_coarse, w_qkv, w_proj)
    grad_hidden, grad_w_in = call(
        hidden_kernel,
        (shape((rows + 2, width, chans), BF16), shape((3, 3 * chans, chans), F32)),
        [taps(rows + 4), grads()],
        conv_flops,
        in_specs=[scalars] + [whole] * 4,
    )(place, slope, grad_merged, grad_tokens, in_wide)
    parts = (grad_w_in, grad_w_out, grad_w_qkv, grad_w_proj)
    flat = jnp.concatenate([part.reshape(-1, chans) for part in parts], axis=0)
    share = scatter_sum(flat).astype(BF16)
    grad_inputs = call(
        inward_kernel,
        shape((rows, cols, chans), BF16),
        [taps(rows + 2)],
        conv_flops,
    )(grad_hidden, pair_weight(flipped(w_in)))
    summed = gather_all(share).astype(F32)
    ends = [9 * chans, 18 * chans, 21 * chans]
    shapes = ((3, 3, chans, chans), (3, 3, chans, chans), (3, chans, chans), (chans, chans))
    pieces = [piece.reshape(dims) for piece, dims in zip(jnp.split(summed, ends), shapes)]
    return (outputs, grad_inputs, *pieces)


def solution(mesh):
    in_specs = (P("lat", "lon", None), P("lat", "lon", None), P(), P(), P(), P())
    out_specs = (P("lat", "lon", None), P("lat", "lon", None), P(), P(), P(), P())
    return jax.shard_map(body, mesh=mesh, in_specs=in_specs, out_specs=out_specs, check_vma=False)
```

```python
import jax
import jax.numpy as jnp
from jax import lax
from jax.experimental import pallas as pl
from jax.experimental.pallas import tpu as pltpu
from jax.sharding import PartitionSpec as P

HEADS = 2
HEAD_DIM = 64
PATCH = 16
DEVICES = 128
AXES = ("lat", "lon")
EDGE = 8
HIGHEST = lax.Precision.HIGHEST
F32 = jnp.float32
BF16 = jnp.bfloat16
NT = (((1,), (1,)), ((), ()))
TN = (((0,), (0,)), ((), ()))


def call(kernel, outs, scratch=(), flops=0, in_specs=None):
    return pl.pallas_call(
        kernel,
        out_shape=outs,
        **({"in_specs": in_specs} if in_specs else {}),
        scratch_shapes=list(scratch),
        compiler_params=pltpu.CompilerParams(vmem_limit_bytes=48 * 2**20),
        cost_estimate=pl.CostEstimate(flops=flops, bytes_accessed=8 * 2**20, transcendentals=0),
    )


def put_shifted(taps, pair, odd, wide):
    width, chans = wide.shape
    base = odd * 3 * chans
    taps[pair, :, base : base + chans] = pltpu.roll(wide, 1, 0).astype(BF16)
    taps[pair, :, base + chans : base + 2 * chans] = wide.astype(BF16)
    taps[pair, :, base + 2 * chans : base + 3 * chans] = pltpu.roll(wide, width - 1, 0).astype(BF16)


def wide_row(field, left, right, index, offset):
    parts = (left[offset + index], field[index], right[offset + index])
    return jnp.concatenate([part.astype(F32) for part in parts], axis=0)


def put_field(taps, field, left, right, first, offset):
    for index in range(field.shape[0]):
        row = wide_row(field, left, right, index, offset)
        put_shifted(taps, first + (index >> 1), index & 1, row)


def put_pair(taps, pair, field, offset):
    for odd in range(2):
        put_shifted(taps, pair, odd, field[offset + odd].astype(F32))


def put_weight(packed, weight, inward):
    chans = weight.shape[2]
    none = jnp.zeros((chans, chans), BF16)
    for col in range(3):
        blocks = []
        for row in range(3):
            if inward:
                blocks.append(weight[2 - row, 2 - col].astype(F32).T.astype(BF16))
            else:
                blocks.append(weight[row, col])
        for source in range(4):
            for target in range(2):
                row = source - target
                block = blocks[row] if 0 <= row < 3 else none
                start = (source * 3 + col) * chans
                packed[start : start + chans, target * chans : (target + 1) * chans] = block


def pair_conv(taps, pair, weight):
    half = weight.shape[0] // 2
    low = jnp.dot(taps[pair], weight[:half], preferred_element_type=F32)
    return low + jnp.dot(taps[pair + 1], weight[half:], preferred_element_type=F32)


def spread_row(grid_row):
    chans = grid_row.shape[1]
    parts = [jnp.broadcast_to(grid_row[15:16], (EDGE, chans))]
    for col in range(8):
        parts.append(jnp.broadcast_to(grid_row[col : col + 1], (PATCH, chans)))
    parts.append(jnp.broadcast_to(grid_row[8:9], (EDGE, chans)))
    return jnp.concatenate(parts, axis=0)


def column_sums(total):
    inner = total[EDGE : EDGE + 8 * PATCH]
    return jnp.sum(inner.reshape(8, PATCH, -1), axis=1)


def patch_sums(rows):
    total = rows[0].astype(F32)
    for row in rows[1:]:
        total = total + row.astype(F32)
    return column_sums(total)


def activate(hidden):
    sigma = jax.nn.sigmoid(hidden)
    act = (hidden * sigma).astype(BF16)
    return act, (sigma * (1.0 + hidden * (1.0 - sigma))).astype(BF16)


def inner_kernel(field, left, right, weight, act, slope, sums, taps, packed):
    chans = field.shape[2]
    rows = act.shape[0]
    put_weight(packed, weight, False)
    put_field(taps, field, left, right, 0, 0)
    for pair in range(rows // 2):
        both = pair_conv(taps, pair, packed)
        for odd in range(2):
            hidden = both[:, odd * chans : (odd + 1) * chans]
            act[2 * pair + odd], slope[2 * pair + odd] = activate(hidden)
    half = rows // 2
    sums[0:8] = patch_sums([act[row] for row in range(half)])
    sums[8:16] = patch_sums([act[row] for row in range(half, rows)])


def edge_kernel(first, last, top, bottom, weight, sums, act, slope, copies, taps, packed):
    chans = first.shape[2]
    put_weight(packed, weight, False)
    for pair, field in enumerate((top, first, last, bottom)):
        put_pair(taps, pair, field, 0)
    for side in range(2):
        both = pair_conv(taps, 2 * side, packed)
        for odd in range(2):
            hidden = both[:, odd * chans : (odd + 1) * chans]
            act[2 * side + odd], slope[2 * side + odd] = activate(hidden)
    total = jnp.concatenate([patch_sums([act[1]]), patch_sums([act[2]])], axis=0)
    tokens = ((sums[...] + total) / (PATCH * PATCH)).astype(BF16)
    for device in range(DEVICES):
        copies[16 * device : 16 * (device + 1)] = tokens


def back_kernel(field, left, right, top, bottom, weight, grad, coarse, taps, packed):
    pairs = taps.shape[0]
    chans = field.shape[2]
    rows = field.shape[0]
    put_weight(packed, weight, True)
    put_pair(taps, 0, top, 2)
    put_field(taps, field, left, right, 1, rows)
    put_pair(taps, pairs - 1, bottom, 2)
    for pair in range(pairs - 1):
        both = pair_conv(taps, pair, packed)
        for odd in range(2):
            grad[2 * pair + odd] = both[:, odd * chans : (odd + 1) * chans]
    half = rows // 2
    coarse[0:8] = patch_sums([grad[1 + row] for row in range(half)])
    coarse[8:16] = patch_sums([grad[1 + row] for row in range(half, rows)])


def near_index(place, shape, dim):
    entry = lax.broadcasted_iota(jnp.int32, shape, dim)
    row = 2 * place[0] + (((entry >> 4) + 1) & 3) - 1
    row = jnp.clip(row, 0, 15)
    col = (8 * place[1] + (((entry & 15) + 4) & 15) - 4) & 127
    device = (row >> 1) * 16 + (col >> 3)
    return device * 16 + (row & 1) * 8 + (col & 7)


def pick_near(place, table):
    count = table.shape[0]
    index = near_index(place, (64, count), 0)
    lane = lax.broadcasted_iota(jnp.int32, (64, count), 1)
    chosen = jnp.where(index == lane, 1.0, 0.0).astype(BF16)
    return jnp.dot(chosen, table, preferred_element_type=F32).astype(BF16)


def by_head(rows):
    lane = lax.broadcasted_iota(jnp.int32, rows.shape, 1)
    wide = rows.astype(F32)
    first = jnp.where(lane < HEAD_DIM, wide, 0.0)
    second = jnp.where(lane < HEAD_DIM, 0.0, wide)
    return jnp.concatenate([first, second], axis=0).astype(BF16)


def join_heads(rows):
    half = rows.shape[0] // 2
    lane = lax.broadcasted_iota(jnp.int32, (half, rows.shape[1]), 1)
    return jnp.where(lane < HEAD_DIM, rows[:half], rows[half:])


def low_dot(a, b):
    return jnp.dot(a, b, preferred_element_type=F32).astype(BF16)


def own_rows(near):
    return jnp.concatenate([near[0:8], near[16:24]], axis=0)


def split_three(value):
    high = value.astype(BF16)
    rest = value - high.astype(F32)
    mid = rest.astype(BF16)
    return high, mid, (rest - mid.astype(F32)).astype(BF16)


def attend_kernel(place, tokens, w_qkv, w_proj, grad_coarse, coarse, message, grad_proj, soft):
    scale = HEAD_DIM**-0.5
    near = pick_near(place, tokens[...])
    keys = low_dot(tokens[...], w_qkv[1])
    values = low_dot(tokens[...], w_qkv[2])
    queries = by_head(low_dot(near, w_qkv[0]))
    scores = lax.dot_general(queries, keys, NT, preferred_element_type=F32) * scale
    top = jnp.max(scores, axis=1, keepdims=True)
    weights = jnp.exp(scores - top)
    total = jnp.sum(weights, axis=1, keepdims=True)
    prob = (weights / total).astype(BF16)
    mixed_wide = join_heads(jnp.dot(prob, values, preferred_element_type=F32))
    mixed = mixed_wide.astype(BF16)
    coarse[...] = near.astype(F32) + jnp.dot(mixed, w_proj[...], preferred_element_type=F32)
    log_sum = top + jnp.log(total)
    soft[...] = log_sum
    coarse_low = grad_coarse[...].astype(BF16)
    grad_proj[...] = lax.dot_general(
        own_rows(mixed), coarse_low, TN, preferred_element_type=F32
    )
    grad_mixed = lax.dot_general(coarse_low, w_proj[...], NT, preferred_element_type=F32)
    product = grad_mixed.astype(BF16).astype(F32) * own_rows(mixed_wide)
    lane = lax.broadcasted_iota(jnp.int32, product.shape, 1)
    inner = [
        jnp.sum(jnp.where(lane < HEAD_DIM, product, 0.0), axis=1, keepdims=True),
        jnp.sum(jnp.where(lane < HEAD_DIM, 0.0, product), axis=1, keepdims=True),
    ]
    logs = [own_rows(log_sum[:64]), own_rows(log_sum[64:])]
    token = lax.broadcasted_iota(jnp.int32, product.shape, 0)
    rows = []
    for pair in (logs, inner):
        row = jnp.zeros((1, 128), F32)
        for head in range(HEADS):
            for part, value in enumerate(split_three(pair[head])):
                slot = (head * 3 + part) * 16
                at = jnp.where(lane == token + slot, value.astype(F32), 0.0)
                row = row + jnp.sum(at, axis=0, keepdims=True)
        rows.append(row)
    text = jnp.concatenate([coarse_low.astype(F32)] + rows, axis=0).astype(BF16)
    for device in range(DEVICES):
        message[device] = text


def lane_stats(sums, head):
    count = sums.shape[0] * 16
    slot = lax.broadcasted_iota(jnp.int32, (128, count), 0)
    lane = lax.broadcasted_iota(jnp.int32, (128, count), 1)
    part = slot >> 4
    wanted = ((slot & 15) == (lane & 15)) & (part >= 3 * head) & (part < 3 * head + 3)
    chosen = jnp.where(wanted, 1.0, 0.0).astype(BF16)
    tiled = jnp.dot(sums, chosen, preferred_element_type=F32)
    device = lax.broadcasted_iota(jnp.int32, tiled.shape, 0)
    lane = lax.broadcasted_iota(jnp.int32, tiled.shape, 1)
    return jnp.sum(jnp.where(device == (lane >> 4), tiled, 0.0), axis=0, keepdims=True)


def attend_back_kernel(
    place, tokens, coarse_low, logs, inner, soft, grad_coarse, w_qkv, w_proj, grad_tokens, grad_qkv
):
    scale = HEAD_DIM**-0.5
    near = pick_near(place, tokens[...])
    near_low = pick_near(place, coarse_low[...])
    queries = low_dot(tokens[...], w_qkv[0])
    keys = low_dot(tokens[...], w_qkv[1])
    values = low_dot(tokens[...], w_qkv[2])
    mixed = lax.dot_general(
        coarse_low[...], w_proj[...], NT, preferred_element_type=F32
    ).astype(BF16)
    near_mixed = lax.dot_general(
        near_low, w_proj[...], NT, preferred_element_type=F32
    ).astype(BF16)
    near_q = by_head(low_dot(near, w_qkv[0]))
    scores = lax.dot_general(near_q, keys, NT, preferred_element_type=F32) * scale
    prob = jnp.exp(scores - soft[...])
    grad_prob = lax.dot_general(by_head(near_mixed), values, NT, preferred_element_type=F32)
    mean = jnp.sum(prob * grad_prob, axis=1, keepdims=True)
    grad_score = (prob * (grad_prob - mean) * scale).astype(BF16)
    grad_q = join_heads(jnp.dot(grad_score, keys, preferred_element_type=F32))
    near_k = by_head(low_dot(near, w_qkv[1]))
    near_v = by_head(low_dot(near, w_qkv[2]))
    count = tokens.shape[0]

    def both_heads(table):
        first = jnp.broadcast_to(lane_stats(table, 0), (64, count))
        second = jnp.broadcast_to(lane_stats(table, 1), (64, count))
        return jnp.concatenate([first, second], axis=0)

    scores = lax.dot_general(near_k, queries, NT, preferred_element_type=F32) * scale
    prob = jnp.exp(scores - both_heads(logs[...]))
    grad_prob = lax.dot_general(near_v, mixed, NT, preferred_element_type=F32)
    grad_score = (prob * (grad_prob - both_heads(inner[...])) * scale).astype(BF16)
    grad_k = join_heads(jnp.dot(grad_score, queries, preferred_element_type=F32))
    grad_v = join_heads(jnp.dot(prob.astype(BF16), mixed, preferred_element_type=F32))
    own = jnp.concatenate(
        [grad_coarse[0:8], near_low[8:16].astype(F32), grad_coarse[8:16]], axis=0
    )
    result = jnp.concatenate([own, near_low[24:].astype(F32)], axis=0)
    own_tokens = own_rows(near.astype(F32))
    for index, grad in enumerate((grad_q, grad_k, grad_v)):
        wide = w_qkv[index].astype(F32)
        result = result + lax.dot_general(
            grad, wide, NT, precision=HIGHEST, preferred_element_type=F32
        )
        grad_qkv[index] = lax.dot_general(
            own_tokens, own_rows(grad), TN, precision=HIGHEST, preferred_element_type=F32
        )
    grad_tokens[...] = result


def row_of(index):
    if index == 0:
        return 3
    return min((index - 1) // PATCH, 2)


def inside(place, index, rows):
    if index == 0:
        return jnp.where(place[0] == 0, 0.0, 1.0)
    if index == rows - 1:
        return jnp.where(place[0] == 7, 0.0, 1.0)
    return None


def put_products(grads, rows_of):
    chans = grads.shape[3] // 3
    rows = 2 * grads.shape[1] - 2
    zero = jnp.zeros((grads.shape[2], chans), BF16)
    for row in range(-1, rows + 3):
        kept = rows_of(row - 1) if 0 < row < rows + 1 else zero
        for tap in range(3):
            target = row - 1 + tap
            if 0 <= target < rows + 2:
                odd, place = target & 1, target >> 1
                grads[odd, place, :, tap * chans : (tap + 1) * chans] = kept


def weight_grads(taps, grads, starts, result):
    chans = result.shape[2]
    count, width = grads.shape[1], grads.shape[2]
    total = jnp.zeros((3 * chans, 3 * chans), F32)
    for odd in range(2):
        lanes = starts[odd][1] * 3 * chans
        first = starts[odd][0]
        left = taps[first : first + count, :, lanes : lanes + 3 * chans]
        left = left.reshape(count * width, 3 * chans)
        right = grads[odd].reshape(count * width, 3 * chans)
        total = total + lax.dot_general(left, right, TN, preferred_element_type=F32)
    for tap in range(3):
        result[tap] = total[:, tap * chans : (tap + 1) * chans]


def pick(inner, edge, index):
    rows = inner.shape[0]
    if index < 2:
        return edge[index]
    return inner[index - 2] if index < rows + 2 else edge[index - rows]


def decode_kernel(
    place, act, edge, coarse, cotangent, weight, outputs, grad_weight, taps, grads, packed
):
    rows = act.shape[0] + 4
    chans = act.shape[2]
    put_weight(packed, weight, False)
    grid = [spread_row(coarse[16 * row : 16 * (row + 1)]) for row in range(4)]
    for index in range(rows):
        merged = pick(act, edge, index).astype(F32) + grid[row_of(index)]
        factor = inside(place, index, rows)
        if factor is not None:
            merged = merged * factor
        put_shifted(taps, index >> 1, index & 1, merged)
    for pair in range(rows // 2 - 1):
        both = pair_conv(taps, pair, packed)
        for odd in range(2):
            lanes = both[EDGE : EDGE + 128, odd * chans : (odd + 1) * chans]
            outputs[2 * pair + odd] = lanes.astype(BF16)
    side = jnp.zeros((EDGE, chans), F32)

    def rows_of(row):
        parts = [side, cotangent[row].astype(F32), side]
        return jnp.concatenate(parts, axis=0).astype(BF16)

    put_products(grads, rows_of)
    weight_grads(taps, grads, ((0, 0), (0, 1)), grad_weight)


def hidden_kernel(
    place, slope, edge, grad, grad_tokens, field, left, right, top, bottom,
    result, grad_weight, taps, grads,
):
    rows, width, chans = grad.shape
    grid = [
        spread_row(grad_tokens[16 * row : 16 * (row + 1)] * (1.0 / (PATCH * PATCH)))
        for row in range(4)
    ]
    for index in range(rows):
        value = (grad[index] + grid[row_of(index)]) * pick(slope, edge, index).astype(F32)
        factor = inside(place, index, rows)
        if factor is not None:
            value = value * factor
        result[index] = value.astype(BF16)
    put_pair(taps, 0, top, 0)
    put_field(taps, field, left, right, 1, 0)
    put_pair(taps, taps.shape[0] - 1, bottom, 0)
    column = lax.broadcasted_iota(jnp.int32, (width, chans), 0)
    own = (column >= EDGE) & (column < width - EDGE)

    def rows_of(row):
        return jnp.where(own, result[row + 1].astype(F32), 0.0).astype(BF16)

    put_products(grads, rows_of)
    weight_grads(taps, grads, ((0, 1), (1, 0)), grad_weight)


def inward_kernel(field, weight, result, taps, packed):
    rows = field.shape[0]
    chans = field.shape[2]
    put_weight(packed, weight, True)
    for index in range(rows):
        put_shifted(taps, index >> 1, index & 1, field[index].astype(F32))
    for pair in range(rows // 2 - 1):
        both = pair_conv(taps, pair, packed)
        for odd in range(2):
            lanes = both[EDGE : EDGE + 128, odd * chans : (odd + 1) * chans]
            result[2 * pair + odd] = lanes.astype(BF16)


def share_kernel(moved, copies):
    total = moved[0].astype(F32)
    for device in range(1, DEVICES):
        total = total + moved[device].astype(F32)
    total = total.astype(BF16)
    for device in range(DEVICES):
        copies[device] = total


def unpack_kernel(moved, *results):
    share = moved.shape[1]
    ends = [0]
    for result in results:
        ends.append(ends[-1] + result.shape[0])
    for device in range(DEVICES):
        start = device * share
        piece = moved[device].astype(F32)
        for index, result in enumerate(results):
            low, high = max(start, ends[index]), min(start + share, ends[index + 1])
            if low < high:
                result[low - ends[index] : high - ends[index]] = piece[low - start : high - start]


def exchange(blocks):
    return lax.all_to_all(blocks, AXES, 0, 0, tiled=True)


def body(inputs, cotangent, w_in, w_out, w_qkv, w_proj):
    rows, cols, chans = inputs.shape
    width = cols + 2 * EDGE
    place = jnp.stack([lax.axis_index("lat"), lax.axis_index("lon")]).astype(jnp.int32)
    shape = jax.ShapeDtypeStruct
    whole = pl.BlockSpec(memory_space=pltpu.VMEM)
    scalars = pl.BlockSpec(memory_space=pltpu.SMEM)
    conv_flops = 2 * rows * cols * 9 * chans * chans
    packed = pltpu.VMEM((12 * chans, 2 * chans), BF16)
    grads = pltpu.VMEM((2, rows // 2 + 1, width, 3 * chans), BF16)

    def taps(count):
        return pltpu.VMEM((count // 2, width, 6 * chans), BF16)

    lats, lons = lax.axis_size("lat"), lax.axis_size("lon")
    up = [(i, i + 1) for i in range(lats - 1)]
    down = [(i + 1, i) for i in range(lats - 1)]
    east = [(i, (i + 1) % lons) for i in range(lons)]
    west = [((i + 1) % lons, i) for i in range(lons)]

    def two(cut):
        return jnp.concatenate([cut(inputs), cut(cotangent)], axis=0)

    left = lax.ppermute(two(lambda field: field[:, cols - EDGE :]), "lon", east)
    right = lax.ppermute(two(lambda field: field[:, :EDGE]), "lon", west)

    def wide_pair(start):
        def cut(side):
            return jnp.concatenate(
                [side[start : start + 2], side[rows + start : rows + start + 2]], axis=0
            )

        own = two(lambda field: field[start : start + 2])
        return jnp.concatenate([cut(left), own, cut(right)], axis=1)

    first, last = wide_pair(0), wide_pair(rows - 2)
    top = lax.ppermute(last, "lat", up)
    bottom = lax.ppermute(first, "lat", down)
    act, slope, sums = call(
        inner_kernel,
        (
            shape((rows - 2, width, chans), BF16),
            shape((rows - 2, width, chans), BF16),
            shape((16, chans), F32),
        ),
        [taps(rows), packed],
        conv_flops,
    )(inputs, left, right, w_in)
    act_edge, slope_edge, copies = call(
        edge_kernel,
        (
            shape((4, width, chans), BF16),
            shape((4, width, chans), BF16),
            shape((DEVICES * 16, chans), BF16),
        ),
        [taps(8), packed],
        conv_flops // 8,
    )(first, last, top, bottom, w_in, sums)
    tokens_all = exchange(copies)
    grad_merged, grad_coarse = call(
        back_kernel,
        (shape((rows + 2, width, chans), F32), shape((16, chans), F32)),
        [taps(rows + 4), packed],
        conv_flops,
    )(cotangent, left, right, top, bottom, w_out)
    coarse, message, grad_w_proj, soft = call(
        attend_kernel,
        (
            shape((64, chans), F32),
            shape((DEVICES, 18, chans), BF16),
            shape((chans, chans), F32),
            shape((128, 1), F32),
        ),
        flops=2**28,
        in_specs=[scalars] + [whole] * 4,
    )(place, tokens_all, w_qkv, w_proj, grad_coarse)
    moved = exchange(message)
    coarse_low = moved[:, :16].reshape(-1, chans)
    logs, inner = moved[:, 16], moved[:, 17]
    outputs, grad_w_out = call(
        decode_kernel,
        (shape((rows, cols, chans), BF16), shape((3, 3 * chans, chans), F32)),
        [taps(rows + 2), grads, packed],
        2 * conv_flops,
        in_specs=[scalars] + [whole] * 5,
    )(place, act, act_edge, coarse, cotangent, w_out)
    grad_tokens, grad_w_qkv = call(
        attend_back_kernel,
        (shape((64, chans), F32), shape((3, chans, chans), F32)),
        flops=2**29,
        in_specs=[scalars] + [whole] * 8,
    )(place, tokens_all, coarse_low, logs, inner, soft, grad_coarse, w_qkv, w_proj)
    grad_hidden, grad_w_in = call(
        hidden_kernel,
        (shape((rows + 2, width, chans), BF16), shape((3, 3 * chans, chans), F32)),
        [taps(rows + 4), grads],
        conv_flops,
        in_specs=[scalars] + [whole] * 9,
    )(place, slope, slope_edge, grad_merged, grad_tokens, inputs, left, right, top, bottom)
    parts = (grad_w_in, grad_w_out, grad_w_qkv, grad_w_proj)
    flat = jnp.concatenate([part.reshape(-1, chans) for part in parts], axis=0)
    share = flat.shape[0] // DEVICES
    partial = exchange(flat.astype(BF16).reshape(DEVICES, share, chans))
    copies = call(share_kernel, shape((DEVICES, share, chans), BF16))(partial)
    grad_inputs = call(
        inward_kernel,
        shape((rows, cols, chans), BF16),
        [taps(rows + 2), packed],
        conv_flops,
    )(grad_hidden, w_in)
    sizes = [part.size // chans for part in parts]
    pieces = call(unpack_kernel, tuple(shape((size, chans), F32) for size in sizes))(
        exchange(copies)
    )
    shapes = (w_in.shape, w_out.shape, w_qkv.shape, w_proj.shape)
    pieces = [piece.reshape(dims) for piece, dims in zip(pieces, shapes)]
    return (outputs, grad_inputs, *pieces)


def solution(mesh):
    in_specs = (P("lat", "lon", None), P("lat", "lon", None), P(), P(), P(), P())
    out_specs = (P("lat", "lon", None), P("lat", "lon", None), P(), P(), P(), P())
    return jax.shard_map(body, mesh=mesh, in_specs=in_specs, out_specs=out_specs, check_vma=False)
```

```python
import jax
import jax.numpy as jnp
from jax import lax
from jax.experimental import pallas as pl
from jax.experimental.pallas import tpu as pltpu
from jax.sharding import PartitionSpec as P

HEADS = 2
HEAD_DIM = 64
PATCH = 16
DEVICES = 128
CHIPS = 64
LON = ("chip", "core")
AXES = ("lat",) + LON
EDGE = 8
HIGHEST = lax.Precision.HIGHEST
F32 = jnp.float32
BF16 = jnp.bfloat16
NT = (((1,), (1,)), ((), ()))
TN = (((0,), (0,)), ((), ()))


def call(kernel, outs, scratch=(), flops=0, in_specs=None):
    return pl.pallas_call(
        kernel,
        out_shape=outs,
        **({"in_specs": in_specs} if in_specs else {}),
        scratch_shapes=list(scratch),
        compiler_params=pltpu.CompilerParams(vmem_limit_bytes=24 * 2**20),
        cost_estimate=pl.CostEstimate(flops=flops, bytes_accessed=8 * 2**20, transcendentals=0),
    )


def put_shifted(taps, pair, odd, wide):
    width, chans = wide.shape
    base = odd * 3 * chans
    taps[pair, :, base : base + chans] = pltpu.roll(wide, 1, 0).astype(BF16)
    taps[pair, :, base + chans : base + 2 * chans] = wide.astype(BF16)
    taps[pair, :, base + 2 * chans : base + 3 * chans] = pltpu.roll(wide, width - 1, 0).astype(BF16)


def wide_row(field, left, right, index, offset):
    parts = (left[offset + index], field[index], right[offset + index])
    return jnp.concatenate([part.astype(F32) for part in parts], axis=0)


def put_field(taps, field, left, right, first, offset):
    for index in range(field.shape[0]):
        row = wide_row(field, left, right, index, offset)
        put_shifted(taps, first + (index >> 1), index & 1, row)


def put_pair(taps, pair, field, offset):
    for odd in range(2):
        put_shifted(taps, pair, odd, field[offset + odd].astype(F32))


def put_weight(packed, weight, inward):
    chans = weight.shape[2]
    none = jnp.zeros((chans, chans), BF16)
    for col in range(3):
        blocks = []
        for row in range(3):
            if inward:
                blocks.append(weight[2 - row, 2 - col].astype(F32).T.astype(BF16))
            else:
                blocks.append(weight[row, col])
        for source in range(4):
            for target in range(2):
                row = source - target
                block = blocks[row] if 0 <= row < 3 else none
                start = (source * 3 + col) * chans
                packed[start : start + chans, target * chans : (target + 1) * chans] = block


def pair_conv(taps, pair, weight):
    half = weight.shape[0] // 2
    low = jnp.dot(taps[pair], weight[:half], preferred_element_type=F32)
    return low + jnp.dot(taps[pair + 1], weight[half:], preferred_element_type=F32)


def spread_row(grid_row):
    chans = grid_row.shape[1]
    parts = [jnp.broadcast_to(grid_row[15:16], (EDGE, chans))]
    for col in range(8):
        parts.append(jnp.broadcast_to(grid_row[col : col + 1], (PATCH, chans)))
    parts.append(jnp.broadcast_to(grid_row[8:9], (EDGE, chans)))
    return jnp.concatenate(parts, axis=0)


def column_sums(total):
    inner = total[EDGE : EDGE + 8 * PATCH]
    return jnp.sum(inner.reshape(8, PATCH, -1), axis=1)


def patch_sums(rows):
    total = rows[0].astype(F32)
    for row in rows[1:]:
        total = total + row.astype(F32)
    return column_sums(total)


def activate(hidden):
    sigma = jax.nn.sigmoid(hidden)
    act = (hidden * sigma).astype(BF16)
    return act, (sigma * (1.0 + hidden * (1.0 - sigma))).astype(BF16)


def inner_kernel(field, left, right, weight, act, slope, sums, taps, packed):
    chans = field.shape[2]
    rows = act.shape[0]
    put_weight(packed, weight, False)
    put_field(taps, field, left, right, 0, 0)
    for pair in range(rows // 2):
        both = pair_conv(taps, pair, packed)
        for odd in range(2):
            hidden = both[:, odd * chans : (odd + 1) * chans]
            act[2 * pair + odd], slope[2 * pair + odd] = activate(hidden)
    half = rows // 2
    sums[0:8] = patch_sums([act[row] for row in range(half)])
    sums[8:16] = patch_sums([act[row] for row in range(half, rows)])


def edge_kernel(first, last, top, bottom, weight, sums, act, slope, copies, taps, packed):
    chans = first.shape[2]
    put_weight(packed, weight, False)
    for pair, field in enumerate((top, first, last, bottom)):
        put_pair(taps, pair, field, 0)
    for side in range(2):
        both = pair_conv(taps, 2 * side, packed)
        for odd in range(2):
            hidden = both[:, odd * chans : (odd + 1) * chans]
            act[2 * side + odd], slope[2 * side + odd] = activate(hidden)
    total = jnp.concatenate([patch_sums([act[1]]), patch_sums([act[2]])], axis=0)
    tokens = ((sums[...] + total) / (PATCH * PATCH)).astype(BF16)
    for device in range(DEVICES):
        copies[16 * device : 16 * (device + 1)] = tokens


def back_kernel(field, left, right, top, bottom, weight, grad, coarse, taps, packed):
    pairs = taps.shape[0]
    chans = field.shape[2]
    rows = field.shape[0]
    put_weight(packed, weight, True)
    put_pair(taps, 0, top, 2)
    put_field(taps, field, left, right, 1, rows)
    put_pair(taps, pairs - 1, bottom, 2)
    for pair in range(pairs - 1):
        both = pair_conv(taps, pair, packed)
        for odd in range(2):
            grad[2 * pair + odd] = both[:, odd * chans : (odd + 1) * chans]
    half = rows // 2
    coarse[0:8] = patch_sums([grad[1 + row] for row in range(half)])
    coarse[8:16] = patch_sums([grad[1 + row] for row in range(half, rows)])


def near_index(place, shape, dim):
    entry = lax.broadcasted_iota(jnp.int32, shape, dim)
    row = 2 * place[0] + (((entry >> 4) + 1) & 3) - 1
    row = jnp.clip(row, 0, 15)
    col = (8 * place[1] + (((entry & 15) + 4) & 15) - 4) & 127
    device = (row >> 1) * 16 + (col >> 3)
    return device * 16 + (row & 1) * 8 + (col & 7)


def pick_near(place, table):
    count = table.shape[0]
    index = near_index(place, (64, count), 0)
    lane = lax.broadcasted_iota(jnp.int32, (64, count), 1)
    chosen = jnp.where(index == lane, 1.0, 0.0).astype(BF16)
    return jnp.dot(chosen, table, preferred_element_type=F32).astype(BF16)


def by_head(rows):
    lane = lax.broadcasted_iota(jnp.int32, rows.shape, 1)
    wide = rows.astype(F32)
    first = jnp.where(lane < HEAD_DIM, wide, 0.0)
    second = jnp.where(lane < HEAD_DIM, 0.0, wide)
    return jnp.concatenate([first, second], axis=0).astype(BF16)


def join_heads(rows):
    half = rows.shape[0] // 2
    lane = lax.broadcasted_iota(jnp.int32, (half, rows.shape[1]), 1)
    return jnp.where(lane < HEAD_DIM, rows[:half], rows[half:])


def low_dot(a, b):
    return jnp.dot(a, b, preferred_element_type=F32).astype(BF16)


def own_rows(near):
    return jnp.concatenate([near[0:8], near[16:24]], axis=0)


def split_three(value):
    high = value.astype(BF16)
    rest = value - high.astype(F32)
    mid = rest.astype(BF16)
    return high, mid, (rest - mid.astype(F32)).astype(BF16)


def attend_kernel(
    place, tokens, w_qkv, w_proj, grad_coarse, coarse, message, grad_proj, soft, near, keys, values
):
    scale = HEAD_DIM**-0.5
    near[...] = pick_near(place, tokens[...])
    keys[...] = low_dot(tokens[...], w_qkv[1])
    values[...] = low_dot(tokens[...], w_qkv[2])
    queries = by_head(low_dot(near[...], w_qkv[0]))
    scores = lax.dot_general(queries, keys[...], NT, preferred_element_type=F32) * scale
    top = jnp.max(scores, axis=1, keepdims=True)
    weights = jnp.exp(scores - top)
    total = jnp.sum(weights, axis=1, keepdims=True)
    prob = (weights / total).astype(BF16)
    mixed_wide = join_heads(jnp.dot(prob, values[...], preferred_element_type=F32))
    mixed = mixed_wide.astype(BF16)
    coarse[...] = near[...].astype(F32) + jnp.dot(
        mixed, w_proj[...], preferred_element_type=F32
    )
    log_sum = top + jnp.log(total)
    soft[...] = log_sum
    coarse_low = grad_coarse[...].astype(BF16)
    grad_proj[...] = lax.dot_general(
        own_rows(mixed), coarse_low, TN, preferred_element_type=F32
    )
    grad_mixed = lax.dot_general(coarse_low, w_proj[...], NT, preferred_element_type=F32)
    product = grad_mixed.astype(BF16).astype(F32) * own_rows(mixed_wide)
    lane = lax.broadcasted_iota(jnp.int32, product.shape, 1)
    inner = [
        jnp.sum(jnp.where(lane < HEAD_DIM, product, 0.0), axis=1, keepdims=True),
        jnp.sum(jnp.where(lane < HEAD_DIM, 0.0, product), axis=1, keepdims=True),
    ]
    logs = [own_rows(log_sum[:64]), own_rows(log_sum[64:])]
    token = lax.broadcasted_iota(jnp.int32, product.shape, 0)
    rows = []
    for pair in (logs, inner):
        row = jnp.zeros((1, 128), F32)
        for head in range(HEADS):
            for part, value in enumerate(split_three(pair[head])):
                slot = (head * 3 + part) * 16
                at = jnp.where(lane == token + slot, value.astype(F32), 0.0)
                row = row + jnp.sum(at, axis=0, keepdims=True)
        rows.append(row)
    text = jnp.concatenate([coarse_low.astype(F32)] + rows, axis=0).astype(BF16)
    for device in range(DEVICES):
        message[device] = text


def lane_stats(sums, head):
    count = sums.shape[0] * 16
    slot = lax.broadcasted_iota(jnp.int32, (128, count), 0)
    lane = lax.broadcasted_iota(jnp.int32, (128, count), 1)
    part = slot >> 4
    wanted = ((slot & 15) == (lane & 15)) & (part >= 3 * head) & (part < 3 * head + 3)
    chosen = jnp.where(wanted, 1.0, 0.0).astype(BF16)
    tiled = jnp.dot(sums, chosen, preferred_element_type=F32)
    device = lax.broadcasted_iota(jnp.int32, tiled.shape, 0)
    lane = lax.broadcasted_iota(jnp.int32, tiled.shape, 1)
    return jnp.sum(jnp.where(device == (lane >> 4), tiled, 0.0), axis=0, keepdims=True)


def prepare_kernel(tokens, near, keys, w_qkv, soft, queries, scores, prob, near_values):
    scale = HEAD_DIM**-0.5
    queries[...] = low_dot(tokens[...], w_qkv[0])
    near_q = by_head(low_dot(near[...], w_qkv[0]))
    near_k = by_head(low_dot(near[...], w_qkv[1]))
    near_values[...] = by_head(low_dot(near[...], w_qkv[2]))
    outward = lax.dot_general(near_q, keys[...], NT, preferred_element_type=F32) * scale
    prob[...] = jnp.exp(outward - soft[...])
    scores[...] = lax.dot_general(near_k, queries[...], NT, preferred_element_type=F32) * scale


def attend_back_kernel(
    place, near, keys, values, queries, scores, prob_out, near_values, moved, grad_coarse,
    w_qkv, w_proj, grad_tokens, grad_qkv,
):
    scale = HEAD_DIM**-0.5
    coarse_low = moved[:, :16, :].reshape(-1, moved.shape[2])
    count = coarse_low.shape[0]
    logs, inner = moved[:, 16, :], moved[:, 17, :]
    near_low = pick_near(place, coarse_low)
    mixed = lax.dot_general(coarse_low, w_proj[...], NT, preferred_element_type=F32).astype(BF16)
    near_mixed = lax.dot_general(
        near_low, w_proj[...], NT, preferred_element_type=F32
    ).astype(BF16)
    grad_prob = lax.dot_general(by_head(near_mixed), values[...], NT, preferred_element_type=F32)
    prob = prob_out[...]
    mean = jnp.sum(prob * grad_prob, axis=1, keepdims=True)
    grad_score = (prob * (grad_prob - mean) * scale).astype(BF16)
    grad_q = join_heads(jnp.dot(grad_score, keys[...], preferred_element_type=F32))

    def both_heads(table):
        first = jnp.broadcast_to(lane_stats(table, 0), (64, count))
        second = jnp.broadcast_to(lane_stats(table, 1), (64, count))
        return jnp.concatenate([first, second], axis=0)

    prob = jnp.exp(scores[...] - both_heads(logs))
    grad_prob = lax.dot_general(near_values[...], mixed, NT, preferred_element_type=F32)
    grad_score = (prob * (grad_prob - both_heads(inner)) * scale).astype(BF16)
    grad_k = join_heads(jnp.dot(grad_score, queries[...], preferred_element_type=F32))
    grad_v = join_heads(jnp.dot(prob.astype(BF16), mixed, preferred_element_type=F32))
    own = jnp.concatenate(
        [grad_coarse[0:8], near_low[8:16].astype(F32), grad_coarse[8:16]], axis=0
    )
    result = jnp.concatenate([own, near_low[24:].astype(F32)], axis=0)
    own_tokens = own_rows(near[...].astype(F32))
    for index, grad in enumerate((grad_q, grad_k, grad_v)):
        wide = w_qkv[index].astype(F32)
        result = result + lax.dot_general(
            grad, wide, NT, precision=HIGHEST, preferred_element_type=F32
        )
        grad_qkv[index] = lax.dot_general(
            own_tokens, own_rows(grad), TN, precision=HIGHEST, preferred_element_type=F32
        )
    grad_tokens[...] = result


def row_of(index):
    if index == 0:
        return 3
    return min((index - 1) // PATCH, 2)


def inside(place, index, rows):
    if index == 0:
        return jnp.where(place[0] == 0, 0.0, 1.0)
    if index == rows - 1:
        return jnp.where(place[0] == 7, 0.0, 1.0)
    return None


def put_products(grads, rows_of):
    chans = grads.shape[3] // 3
    rows = 2 * grads.shape[1] - 2
    zero = jnp.zeros((grads.shape[2], chans), BF16)
    for row in range(-1, rows + 3):
        kept = rows_of(row - 1) if 0 < row < rows + 1 else zero
        for tap in range(3):
            target = row - 1 + tap
            if 0 <= target < rows + 2:
                odd, place = target & 1, target >> 1
                grads[odd, place, :, tap * chans : (tap + 1) * chans] = kept


def weight_grads(taps, grads, starts, result):
    chans = result.shape[1]
    count, width = grads.shape[1], grads.shape[2]
    total = jnp.zeros((3 * chans, 3 * chans), F32)
    for odd in range(2):
        lanes = starts[odd][1] * 3 * chans
        first = starts[odd][0]
        left = taps[first : first + count, :, lanes : lanes + 3 * chans]
        left = left.reshape(count * width, 3 * chans)
        right = grads[odd].reshape(count * width, 3 * chans)
        total = total + lax.dot_general(left, right, TN, preferred_element_type=F32)
    for tap in range(3):
        result[tap * 3 * chans : (tap + 1) * 3 * chans] = total[:, tap * chans : (tap + 1) * chans]


def halve(place, table, keep, send):
    half = keep.shape[0]
    core = place[1] & 1
    keep[...] = table[pl.ds(pl.multiple_of(core * half, 64), half)]
    send[...] = table[pl.ds(pl.multiple_of((1 - core) * half, 64), half)].astype(BF16)


def pick(inner, edge, index):
    rows = inner.shape[0]
    if index < 2:
        return edge[index]
    return inner[index - 2] if index < rows + 2 else edge[index - rows]


def decode_kernel(
    place, act, edge, coarse, cotangent, weight, grad_proj, outputs, keep, send,
    taps, grads, packed, table,
):
    rows = act.shape[0] + 4
    chans = act.shape[2]
    put_weight(packed, weight, False)
    grid = [spread_row(coarse[16 * row : 16 * (row + 1)]) for row in range(4)]
    for index in range(rows):
        merged = pick(act, edge, index).astype(F32) + grid[row_of(index)]
        factor = inside(place, index, rows)
        if factor is not None:
            merged = merged * factor
        put_shifted(taps, index >> 1, index & 1, merged)
    for pair in range(rows // 2 - 1):
        both = pair_conv(taps, pair, packed)
        for odd in range(2):
            lanes = both[EDGE : EDGE + 128, odd * chans : (odd + 1) * chans]
            outputs[2 * pair + odd] = lanes.astype(BF16)
    side = jnp.zeros((EDGE, chans), F32)

    def rows_of(row):
        parts = [side, cotangent[row].astype(F32), side]
        return jnp.concatenate(parts, axis=0).astype(BF16)

    put_products(grads, rows_of)
    weight_grads(taps, grads, ((0, 0), (0, 1)), table)
    table[9 * chans :] = grad_proj[...]
    halve(place, table, keep, send)


def hidden_kernel(
    place, slope, edge, grad, grad_tokens, grad_qkv, field, left, right, top, bottom,
    result, keep, send, taps, grads, table,
):
    rows, width, chans = grad.shape
    grid = [
        spread_row(grad_tokens[16 * row : 16 * (row + 1)] * (1.0 / (PATCH * PATCH)))
        for row in range(4)
    ]
    for index in range(rows):
        value = (grad[index] + grid[row_of(index)]) * pick(slope, edge, index).astype(F32)
        factor = inside(place, index, rows)
        if factor is not None:
            value = value * factor
        result[index] = value.astype(BF16)
    put_pair(taps, 0, top, 0)
    put_field(taps, field, left, right, 1, 0)
    put_pair(taps, taps.shape[0] - 1, bottom, 0)
    column = lax.broadcasted_iota(jnp.int32, (width, chans), 0)
    own = (column >= EDGE) & (column < width - EDGE)

    def rows_of(row):
        return jnp.where(own, result[row + 1].astype(F32), 0.0).astype(BF16)

    put_products(grads, rows_of)
    weight_grads(taps, grads, ((0, 1), (1, 0)), table)
    for index in range(3):
        table[(9 + index) * chans : (10 + index) * chans] = grad_qkv[index]
    halve(place, table, keep, send)


def inward_kernel(field, weight, result, taps, packed):
    rows = field.shape[0]
    chans = field.shape[2]
    put_weight(packed, weight, True)
    for index in range(rows):
        put_shifted(taps, index >> 1, index & 1, field[index].astype(F32))
    for pair in range(rows // 2 - 1):
        both = pair_conv(taps, pair, packed)
        for odd in range(2):
            lanes = both[EDGE : EDGE + 128, odd * chans : (odd + 1) * chans]
            result[2 * pair + odd] = lanes.astype(BF16)


def cut(tables, starts, start, stop):
    pieces = []
    for index, table in enumerate(tables):
        low, high = max(start, starts[index]), min(stop, starts[index + 1])
        if low < high:
            pieces.append((table, low - starts[index], high - starts[index], low - start))
    return pieces


def row_starts(tables):
    starts = [0]
    for table in tables:
        starts.append(starts[-1] + table.shape[0])
    return starts


def chip_sum_kernel(keep_a, keep_b, got_a, got_b, blocks, sum_a, sum_b):
    sum_a[...] = keep_a[...] + got_a[...].astype(F32)
    sum_b[...] = keep_b[...] + got_b[...].astype(F32)
    tables = (sum_a, sum_b)
    starts = row_starts(tables)
    share = blocks.shape[1]
    for chip in range(CHIPS):
        pieces = cut(tables, starts, chip * share, (chip + 1) * share)
        rows = [table[low:high] for table, low, high, _ in pieces]
        blocks[chip] = (rows[0] if len(rows) == 1 else jnp.concatenate(rows, axis=0)).astype(BF16)


def share_kernel(moved, copies):
    total = moved[0].astype(F32)
    for chip in range(1, CHIPS):
        total = total + moved[chip].astype(F32)
    total = total.astype(BF16)
    for chip in range(CHIPS):
        copies[chip] = total


def unpack_kernel(place, own, other, *rest):
    results, (sum_a, sum_b) = rest[:4], rest[4:]
    share = own.shape[1]
    core = place[1] & 1
    tables = (sum_a, sum_b)
    starts = [0, sum_a.shape[0] // 2, sum_a.shape[0] // 2 + sum_b.shape[0] // 2]
    for source, at in ((own, core), (other, 1 - core)):
        for chip in range(CHIPS):
            piece = source[chip].astype(F32)
            for table, low, high, offset in cut(tables, starts, chip * share, (chip + 1) * share):
                base = pl.multiple_of(at * (table.shape[0] // 2), 64)
                table[pl.ds(base + low, high - low)] = piece[offset : offset + high - low]
    size = results[0].shape[0]
    results[0][...] = sum_a[:size]
    results[2][...] = sum_a[size:]
    results[1][...] = sum_b[:size]
    results[3][...] = sum_b[size:]


def exchange(blocks, axes):
    return lax.all_to_all(blocks, axes, 0, 0, tiled=True)


def body(inputs, cotangent, w_in, w_out, w_qkv, w_proj):
    rows, cols, chans = inputs.shape
    width = cols + 2 * EDGE
    place = jnp.stack([lax.axis_index("lat"), lax.axis_index(LON)]).astype(jnp.int32)
    shape = jax.ShapeDtypeStruct
    whole = pl.BlockSpec(memory_space=pltpu.VMEM)
    scalars = pl.BlockSpec(memory_space=pltpu.SMEM)
    conv_flops = 2 * rows * cols * 9 * chans * chans
    packed = pltpu.VMEM((12 * chans, 2 * chans), BF16)
    grads = pltpu.VMEM((2, rows // 2 + 1, width, 3 * chans), BF16)

    def taps(count):
        return pltpu.VMEM((count // 2, width, 6 * chans), BF16)

    lats, lons = lax.axis_size("lat"), lax.axis_size("chip") * lax.axis_size("core")
    up = [(i, i + 1) for i in range(lats - 1)]
    down = [(i + 1, i) for i in range(lats - 1)]
    east = [(i, (i + 1) % lons) for i in range(lons)]
    west = [((i + 1) % lons, i) for i in range(lons)]

    def two(cut):
        return jnp.concatenate([cut(inputs), cut(cotangent)], axis=0)

    left = lax.ppermute(two(lambda field: field[:, cols - EDGE :]), LON, east)
    right = lax.ppermute(two(lambda field: field[:, :EDGE]), LON, west)

    def wide_pair(start):
        def cut(side):
            return jnp.concatenate(
                [side[start : start + 2], side[rows + start : rows + start + 2]], axis=0
            )

        own = two(lambda field: field[start : start + 2])
        return jnp.concatenate([cut(left), own, cut(right)], axis=1)

    first, last = wide_pair(0), wide_pair(rows - 2)
    top = lax.ppermute(last, "lat", up)
    bottom = lax.ppermute(first, "lat", down)
    act, slope, sums = call(
        inner_kernel,
        (
            shape((rows - 2, width, chans), BF16),
            shape((rows - 2, width, chans), BF16),
            shape((16, chans), F32),
        ),
        [taps(rows), packed],
        conv_flops,
    )(inputs, left, right, w_in)
    act_edge, slope_edge, copies = call(
        edge_kernel,
        (
            shape((4, width, chans), BF16),
            shape((4, width, chans), BF16),
            shape((DEVICES * 16, chans), BF16),
        ),
        [taps(8), packed],
        conv_flops // 8,
    )(first, last, top, bottom, w_in, sums)
    tokens_all = exchange(copies, AXES)
    grad_merged, grad_coarse = call(
        back_kernel,
        (shape((rows + 2, width, chans), F32), shape((16, chans), F32)),
        [taps(rows + 4), packed],
        conv_flops,
    )(cotangent, left, right, top, bottom, w_out)
    table = shape((DEVICES * 16, chans), BF16)
    coarse, message, grad_w_proj, soft, near, keys, values = call(
        attend_kernel,
        (
            shape((64, chans), F32),
            shape((DEVICES, 18, chans), BF16),
            shape((chans, chans), F32),
            shape((128, 1), F32),
            shape((64, chans), BF16),
            table,
            table,
        ),
        flops=2**28,
        in_specs=[scalars] + [whole] * 4,
    )(place, tokens_all, w_qkv, w_proj, grad_coarse)
    moved = exchange(message, AXES)
    outputs, keep_b, send_b = call(
        decode_kernel,
        (
            shape((rows, cols, chans), BF16),
            shape((5 * chans, chans), F32),
            shape((5 * chans, chans), BF16),
        ),
        [taps(rows + 2), grads, packed, pltpu.VMEM((10 * chans, chans), F32)],
        2 * conv_flops,
        in_specs=[scalars] + [whole] * 6,
    )(place, act, act_edge, coarse, cotangent, w_out, grad_w_proj)
    wide = shape((128, DEVICES * 16), F32)
    queries, scores, prob, near_values = call(
        prepare_kernel,
        (table, wide, wide, shape((128, chans), BF16)),
        flops=2**28,
    )(tokens_all, near, keys, w_qkv, soft)
    grad_tokens, grad_w_qkv = call(
        attend_back_kernel,
        (shape((64, chans), F32), shape((3, chans, chans), F32)),
        flops=2**28,
        in_specs=[scalars] + [whole] * 11,
    )(
        place, near, keys, values, queries, scores, prob, near_values, moved, grad_coarse,
        w_qkv, w_proj,
    )
    swap = [(0, 1), (1, 0)]
    got_b = lax.ppermute(send_b, "core", swap)
    grad_hidden, keep_a, send_a = call(
        hidden_kernel,
        (
            shape((rows + 2, width, chans), BF16),
            shape((6 * chans, chans), F32),
            shape((6 * chans, chans), BF16),
        ),
        [taps(rows + 4), grads, pltpu.VMEM((12 * chans, chans), F32)],
        conv_flops,
        in_specs=[scalars] + [whole] * 10,
    )(
        place, slope, slope_edge, grad_merged, grad_tokens, grad_w_qkv, inputs, left, right,
        top, bottom,
    )
    got_a = lax.ppermute(send_a, "core", swap)
    share = 11 * chans // CHIPS
    blocks = call(
        chip_sum_kernel,
        shape((CHIPS, share, chans), BF16),
        [pltpu.VMEM(keep.shape, F32) for keep in (keep_a, keep_b)],
    )(keep_a, keep_b, got_a, got_b)
    copies = call(share_kernel, shape(blocks.shape, BF16))(exchange(blocks, ("lat", "chip")))
    grad_inputs = call(
        inward_kernel,
        shape((rows, cols, chans), BF16),
        [taps(rows + 2), packed],
        conv_flops,
    )(grad_hidden, w_in)
    own = exchange(copies, ("lat", "chip"))
    other = lax.ppermute(own, "core", swap)
    shapes = (w_in.shape, w_out.shape, w_qkv.shape, w_proj.shape)
    pieces = call(
        unpack_kernel,
        tuple(shape((size * chans, chans), F32) for size in (9, 9, 3, 1)),
        [pltpu.VMEM((size * chans, chans), F32) for size in (12, 10)],
        in_specs=[scalars, whole, whole],
    )(place, own, other)
    pieces = [piece.reshape(dims) for piece, dims in zip(pieces, shapes)]
    return (outputs, grad_inputs, *pieces)


def solution(mesh):
    lats, lons = mesh.devices.shape
    fine = jax.sharding.Mesh(mesh.devices.reshape(lats, lons // 2, 2), AXES)
    field, whole = P("lat", LON, None), P()
    in_specs = (field, field, whole, whole, whole, whole)
    out_specs = (field, field, whole, whole, whole, whole)
    return jax.shard_map(body, mesh=fine, in_specs=in_specs, out_specs=out_specs, check_vma=False)
```

```python
import jax
import jax.numpy as jnp
from jax import lax
from jax.experimental import pallas as pl
from jax.experimental.pallas import tpu as pltpu
from jax.sharding import PartitionSpec as P

HEADS = 2
HEAD_DIM = 64
PATCH = 16
DEVICES = 128
CHIPS = 64
LON = ("chip", "core")
AXES = ("lat",) + LON
EDGE = 8
HIGHEST = lax.Precision.HIGHEST
F32 = jnp.float32
BF16 = jnp.bfloat16
NT = (((1,), (1,)), ((), ()))
TN = (((0,), (0,)), ((), ()))


def call(kernel, outs, scratch=(), flops=0, in_specs=None):
    return pl.pallas_call(
        kernel,
        out_shape=outs,
        **({"in_specs": in_specs} if in_specs else {}),
        scratch_shapes=list(scratch),
        compiler_params=pltpu.CompilerParams(vmem_limit_bytes=24 * 2**20),
        cost_estimate=pl.CostEstimate(flops=flops, bytes_accessed=8 * 2**20, transcendentals=0),
    )


def put_shifted(taps, pair, odd, wide):
    width, chans = wide.shape
    base = odd * 3 * chans
    taps[pair, :, base : base + chans] = pltpu.roll(wide, 1, 0).astype(BF16)
    taps[pair, :, base + chans : base + 2 * chans] = wide.astype(BF16)
    taps[pair, :, base + 2 * chans : base + 3 * chans] = pltpu.roll(wide, width - 1, 0).astype(BF16)


def wide_row(field, left, right, index, offset):
    parts = (left[offset + index], field[index], right[offset + index])
    return jnp.concatenate([part.astype(F32) for part in parts], axis=0)


def put_field(taps, field, left, right, first, offset):
    for index in range(field.shape[0]):
        row = wide_row(field, left, right, index, offset)
        put_shifted(taps, first + (index >> 1), index & 1, row)


def put_pair(taps, pair, field, offset):
    for odd in range(2):
        put_shifted(taps, pair, odd, field[offset + odd].astype(F32))


def put_weight(packed, weight, inward):
    chans = weight.shape[2]
    none = jnp.zeros((chans, chans), BF16)
    for col in range(3):
        blocks = []
        for row in range(3):
            if inward:
                blocks.append(weight[2 - row, 2 - col].astype(F32).T.astype(BF16))
            else:
                blocks.append(weight[row, col])
        for source in range(4):
            for target in range(2):
                row = source - target
                block = blocks[row] if 0 <= row < 3 else none
                start = (source * 3 + col) * chans
                packed[start : start + chans, target * chans : (target + 1) * chans] = block


def pair_conv(taps, pair, weight):
    half = weight.shape[0] // 2
    low = jnp.dot(taps[pair], weight[:half], preferred_element_type=F32)
    return low + jnp.dot(taps[pair + 1], weight[half:], preferred_element_type=F32)


def spread_row(grid_row):
    chans = grid_row.shape[1]
    parts = [jnp.broadcast_to(grid_row[15:16], (EDGE, chans))]
    for col in range(8):
        parts.append(jnp.broadcast_to(grid_row[col : col + 1], (PATCH, chans)))
    parts.append(jnp.broadcast_to(grid_row[8:9], (EDGE, chans)))
    return jnp.concatenate(parts, axis=0)


def column_sums(total):
    inner = total[EDGE : EDGE + 8 * PATCH]
    return jnp.sum(inner.reshape(8, PATCH, -1), axis=1)


def patch_sums(rows):
    total = rows[0].astype(F32)
    for row in rows[1:]:
        total = total + row.astype(F32)
    return column_sums(total)


def activate(hidden):
    sigma = jax.nn.sigmoid(hidden)
    act = (hidden * sigma).astype(BF16)
    return act, (sigma * (1.0 + hidden * (1.0 - sigma))).astype(BF16)


def inner_kernel(field, left, right, weight, act, slope, sums, taps, packed):
    chans = field.shape[2]
    rows = act.shape[0]
    put_weight(packed, weight, False)
    put_field(taps, field, left, right, 0, 0)
    for pair in range(rows // 2):
        both = pair_conv(taps, pair, packed)
        for odd in range(2):
            hidden = both[:, odd * chans : (odd + 1) * chans]
            act[2 * pair + odd], slope[2 * pair + odd] = activate(hidden)
    half = rows // 2
    sums[0:8] = patch_sums([act[row] for row in range(half)])
    sums[8:16] = patch_sums([act[row] for row in range(half, rows)])


def edge_kernel(first, last, top, bottom, weight, sums, act, slope, copies, taps, packed):
    chans = first.shape[2]
    put_weight(packed, weight, False)
    for pair, field in enumerate((top, first, last, bottom)):
        put_pair(taps, pair, field, 0)
    for side in range(2):
        both = pair_conv(taps, 2 * side, packed)
        for odd in range(2):
            hidden = both[:, odd * chans : (odd + 1) * chans]
            act[2 * side + odd], slope[2 * side + odd] = activate(hidden)
    total = jnp.concatenate([patch_sums([act[1]]), patch_sums([act[2]])], axis=0)
    tokens = ((sums[...] + total) / (PATCH * PATCH)).astype(BF16)
    for device in range(DEVICES):
        copies[16 * device : 16 * (device + 1)] = tokens


def back_kernel(field, left, right, top, bottom, weight, grad, coarse, taps, packed):
    pairs = taps.shape[0]
    chans = field.shape[2]
    rows = field.shape[0]
    put_weight(packed, weight, True)
    put_pair(taps, 0, top, 2)
    put_field(taps, field, left, right, 1, rows)
    put_pair(taps, pairs - 1, bottom, 2)
    for pair in range(pairs - 1):
        both = pair_conv(taps, pair, packed)
        for odd in range(2):
            grad[2 * pair + odd] = both[:, odd * chans : (odd + 1) * chans]
    half = rows // 2
    coarse[0:8] = patch_sums([grad[1 + row] for row in range(half)])
    coarse[8:16] = patch_sums([grad[1 + row] for row in range(half, rows)])


def near_index(place, shape, dim):
    entry = lax.broadcasted_iota(jnp.int32, shape, dim)
    row = 2 * place[0] + (((entry >> 4) + 1) & 3) - 1
    row = jnp.clip(row, 0, 15)
    col = (8 * place[1] + (((entry & 15) + 4) & 15) - 4) & 127
    device = (row >> 1) * 16 + (col >> 3)
    return device * 16 + (row & 1) * 8 + (col & 7)


def pick_near(place, table):
    count = table.shape[0]
    index = near_index(place, (64, count), 0)
    lane = lax.broadcasted_iota(jnp.int32, (64, count), 1)
    chosen = jnp.where(index == lane, 1.0, 0.0).astype(BF16)
    return jnp.dot(chosen, table, preferred_element_type=F32).astype(BF16)


def by_head(rows):
    lane = lax.broadcasted_iota(jnp.int32, rows.shape, 1)
    wide = rows.astype(F32)
    first = jnp.where(lane < HEAD_DIM, wide, 0.0)
    second = jnp.where(lane < HEAD_DIM, 0.0, wide)
    return jnp.concatenate([first, second], axis=0).astype(BF16)


def join_heads(rows):
    half = rows.shape[0] // 2
    lane = lax.broadcasted_iota(jnp.int32, (half, rows.shape[1]), 1)
    return jnp.where(lane < HEAD_DIM, rows[:half], rows[half:])


def low_dot(a, b):
    return jnp.dot(a, b, preferred_element_type=F32).astype(BF16)


def own_rows(near):
    return jnp.concatenate([near[0:8], near[16:24]], axis=0)


def split_three(value):
    high = value.astype(BF16)
    rest = value - high.astype(F32)
    mid = rest.astype(BF16)
    return high, mid, (rest - mid.astype(F32)).astype(BF16)


def attend_kernel(
    place, tokens, w_qkv, w_proj, grad_coarse, coarse, message, grad_proj, soft, near, keys, values
):
    scale = HEAD_DIM**-0.5
    near[...] = pick_near(place, tokens[...])
    keys[...] = low_dot(tokens[...], w_qkv[1])
    values[...] = low_dot(tokens[...], w_qkv[2])
    queries = by_head(low_dot(near[...], w_qkv[0]))
    scores = lax.dot_general(queries, keys[...], NT, preferred_element_type=F32) * scale
    top = jnp.max(scores, axis=1, keepdims=True)
    weights = jnp.exp(scores - top)
    total = jnp.sum(weights, axis=1, keepdims=True)
    prob = (weights / total).astype(BF16)
    mixed_wide = join_heads(jnp.dot(prob, values[...], preferred_element_type=F32))
    mixed = mixed_wide.astype(BF16)
    coarse[...] = near[...].astype(F32) + jnp.dot(
        mixed, w_proj[...], preferred_element_type=F32
    )
    log_sum = top + jnp.log(total)
    soft[...] = log_sum
    coarse_low = grad_coarse[...].astype(BF16)
    grad_proj[...] = lax.dot_general(
        own_rows(mixed), coarse_low, TN, preferred_element_type=F32
    )
    grad_mixed = lax.dot_general(coarse_low, w_proj[...], NT, preferred_element_type=F32)
    product = grad_mixed.astype(BF16).astype(F32) * own_rows(mixed_wide)
    lane = lax.broadcasted_iota(jnp.int32, product.shape, 1)
    inner = [
        jnp.sum(jnp.where(lane < HEAD_DIM, product, 0.0), axis=1, keepdims=True),
        jnp.sum(jnp.where(lane < HEAD_DIM, 0.0, product), axis=1, keepdims=True),
    ]
    logs = [own_rows(log_sum[:64]), own_rows(log_sum[64:])]
    token = lax.broadcasted_iota(jnp.int32, product.shape, 0)
    rows = []
    for pair in (logs, inner):
        row = jnp.zeros((1, 128), F32)
        for head in range(HEADS):
            for part, value in enumerate(split_three(pair[head])):
                slot = (head * 3 + part) * 16
                at = jnp.where(lane == token + slot, value.astype(F32), 0.0)
                row = row + jnp.sum(at, axis=0, keepdims=True)
        rows.append(row)
    text = jnp.concatenate([coarse_low.astype(F32)] + rows, axis=0).astype(BF16)
    for device in range(DEVICES):
        message[device] = text


def lane_stats(sums, head):
    count = sums.shape[0] * 16
    slot = lax.broadcasted_iota(jnp.int32, (128, count), 0)
    lane = lax.broadcasted_iota(jnp.int32, (128, count), 1)
    part = slot >> 4
    wanted = ((slot & 15) == (lane & 15)) & (part >= 3 * head) & (part < 3 * head + 3)
    chosen = jnp.where(wanted, 1.0, 0.0).astype(BF16)
    tiled = jnp.dot(sums, chosen, preferred_element_type=F32)
    device = lax.broadcasted_iota(jnp.int32, tiled.shape, 0)
    lane = lax.broadcasted_iota(jnp.int32, tiled.shape, 1)
    return jnp.sum(jnp.where(device == (lane >> 4), tiled, 0.0), axis=0, keepdims=True)


def prepare_kernel(tokens, near, keys, w_qkv, soft, queries, scores, prob, near_values):
    scale = HEAD_DIM**-0.5
    queries[...] = low_dot(tokens[...], w_qkv[0])
    near_q = by_head(low_dot(near[...], w_qkv[0]))
    near_k = by_head(low_dot(near[...], w_qkv[1]))
    near_values[...] = by_head(low_dot(near[...], w_qkv[2]))
    outward = lax.dot_general(near_q, keys[...], NT, preferred_element_type=F32) * scale
    prob[...] = jnp.exp(outward - soft[...])
    scores[...] = lax.dot_general(near_k, queries[...], NT, preferred_element_type=F32) * scale


def attend_back_kernel(
    place, near, keys, values, queries, scores, prob_out, near_values, moved, grad_coarse,
    w_qkv, w_proj, grad_tokens, grad_qkv,
):
    scale = HEAD_DIM**-0.5
    coarse_low = moved[:, :16, :].reshape(-1, moved.shape[2])
    count = coarse_low.shape[0]
    logs, inner = moved[:, 16, :], moved[:, 17, :]
    near_low = pick_near(place, coarse_low)
    mixed = lax.dot_general(coarse_low, w_proj[...], NT, preferred_element_type=F32).astype(BF16)
    near_mixed = lax.dot_general(
        near_low, w_proj[...], NT, preferred_element_type=F32
    ).astype(BF16)
    grad_prob = lax.dot_general(by_head(near_mixed), values[...], NT, preferred_element_type=F32)
    prob = prob_out[...]
    mean = jnp.sum(prob * grad_prob, axis=1, keepdims=True)
    grad_score = (prob * (grad_prob - mean) * scale).astype(BF16)
    grad_q = join_heads(jnp.dot(grad_score, keys[...], preferred_element_type=F32))

    def both_heads(table):
        first = jnp.broadcast_to(lane_stats(table, 0), (64, count))
        second = jnp.broadcast_to(lane_stats(table, 1), (64, count))
        return jnp.concatenate([first, second], axis=0)

    prob = jnp.exp(scores[...] - both_heads(logs))
    grad_prob = lax.dot_general(near_values[...], mixed, NT, preferred_element_type=F32)
    grad_score = (prob * (grad_prob - both_heads(inner)) * scale).astype(BF16)
    grad_k = join_heads(jnp.dot(grad_score, queries[...], preferred_element_type=F32))
    grad_v = join_heads(jnp.dot(prob.astype(BF16), mixed, preferred_element_type=F32))
    own = jnp.concatenate(
        [grad_coarse[0:8], near_low[8:16].astype(F32), grad_coarse[8:16]], axis=0
    )
    result = jnp.concatenate([own, near_low[24:].astype(F32)], axis=0)
    own_tokens = own_rows(near[...].astype(F32))
    for index, grad in enumerate((grad_q, grad_k, grad_v)):
        wide = w_qkv[index].astype(F32)
        result = result + lax.dot_general(
            grad, wide, NT, precision=HIGHEST, preferred_element_type=F32
        )
        grad_qkv[index] = lax.dot_general(
            own_tokens, own_rows(grad), TN, precision=HIGHEST, preferred_element_type=F32
        )
    grad_tokens[...] = result


def row_of(index):
    if index == 0:
        return 3
    return min((index - 1) // PATCH, 2)


def inside(place, index, rows):
    if index == 0:
        return jnp.where(place[0] == 0, 0.0, 1.0)
    if index == rows - 1:
        return jnp.where(place[0] == 7, 0.0, 1.0)
    return None


def put_products(grads, rows_of):
    chans = grads.shape[3] // 3
    rows = 2 * grads.shape[1] - 2
    zero = jnp.zeros((grads.shape[2], chans), BF16)
    for row in range(-1, rows + 3):
        kept = rows_of(row - 1) if 0 < row < rows + 1 else zero
        for tap in range(3):
            target = row - 1 + tap
            if 0 <= target < rows + 2:
                odd, place = target & 1, target >> 1
                grads[odd, place, :, tap * chans : (tap + 1) * chans] = kept


def weight_grads(taps, grads, starts, result):
    chans = result.shape[1]
    count, width = grads.shape[1], grads.shape[2]
    total = jnp.zeros((3 * chans, 3 * chans), F32)
    for odd in range(2):
        lanes = starts[odd][1] * 3 * chans
        first = starts[odd][0]
        left = taps[first : first + count, :, lanes : lanes + 3 * chans]
        left = left.reshape(count * width, 3 * chans)
        right = grads[odd].reshape(count * width, 3 * chans)
        total = total + lax.dot_general(left, right, TN, preferred_element_type=F32)
    for tap in range(3):
        result[tap * 3 * chans : (tap + 1) * 3 * chans] = total[:, tap * chans : (tap + 1) * chans]


def halve(place, table, keep, send):
    half = keep.shape[0]
    core = place[1] & 1
    keep[...] = table[pl.ds(pl.multiple_of(core * half, 64), half)]
    send[...] = table[pl.ds(pl.multiple_of((1 - core) * half, 64), half)].astype(BF16)


def pick(inner, edge, index):
    rows = inner.shape[0]
    if index < 2:
        return edge[index]
    return inner[index - 2] if index < rows + 2 else edge[index - rows]


def decode_kernel(
    place, act, edge, coarse, cotangent, weight, grad_proj, outputs, keep, send,
    taps, grads, packed, table,
):
    rows = act.shape[0] + 4
    chans = act.shape[2]
    put_weight(packed, weight, False)
    grid = [spread_row(coarse[16 * row : 16 * (row + 1)]) for row in range(4)]
    for index in range(rows):
        merged = pick(act, edge, index).astype(F32) + grid[row_of(index)]
        factor = inside(place, index, rows)
        if factor is not None:
            merged = merged * factor
        put_shifted(taps, index >> 1, index & 1, merged)
    for pair in range(rows // 2 - 1):
        both = pair_conv(taps, pair, packed)
        for odd in range(2):
            lanes = both[EDGE : EDGE + 128, odd * chans : (odd + 1) * chans]
            outputs[2 * pair + odd] = lanes.astype(BF16)
    side = jnp.zeros((EDGE, chans), F32)

    def rows_of(row):
        parts = [side, cotangent[row].astype(F32), side]
        return jnp.concatenate(parts, axis=0).astype(BF16)

    put_products(grads, rows_of)
    weight_grads(taps, grads, ((0, 0), (0, 1)), table)
    table[9 * chans :] = grad_proj[...]
    halve(place, table, keep, send)


def hidden_kernel(
    place, slope, edge, grad, grad_tokens, grad_qkv, field, left, right, top, bottom,
    result, keep, send, taps, grads, table,
):
    rows, width, chans = grad.shape
    grid = [
        spread_row(grad_tokens[16 * row : 16 * (row + 1)] * (1.0 / (PATCH * PATCH)))
        for row in range(4)
    ]
    for index in range(rows):
        value = (grad[index] + grid[row_of(index)]) * pick(slope, edge, index).astype(F32)
        factor = inside(place, index, rows)
        if factor is not None:
            value = value * factor
        result[index] = value.astype(BF16)
    put_pair(taps, 0, top, 0)
    put_field(taps, field, left, right, 1, 0)
    put_pair(taps, taps.shape[0] - 1, bottom, 0)
    column = lax.broadcasted_iota(jnp.int32, (width, chans), 0)
    own = (column >= EDGE) & (column < width - EDGE)

    def rows_of(row):
        return jnp.where(own, result[row + 1].astype(F32), 0.0).astype(BF16)

    put_products(grads, rows_of)
    weight_grads(taps, grads, ((0, 1), (1, 0)), table)
    for index in range(3):
        table[(9 + index) * chans : (10 + index) * chans] = grad_qkv[index]
    halve(place, table, keep, send)


def inward_kernel(field, weight, result, taps, packed):
    rows = field.shape[0]
    chans = field.shape[2]
    put_weight(packed, weight, True)
    for index in range(rows):
        put_shifted(taps, index >> 1, index & 1, field[index].astype(F32))
    for pair in range(rows // 2 - 1):
        both = pair_conv(taps, pair, packed)
        for odd in range(2):
            lanes = both[EDGE : EDGE + 128, odd * chans : (odd + 1) * chans]
            result[2 * pair + odd] = lanes.astype(BF16)


def cut(tables, starts, start, stop):
    pieces = []
    for index, table in enumerate(tables):
        low, high = max(start, starts[index]), min(stop, starts[index + 1])
        if low < high:
            pieces.append((table, low - starts[index], high - starts[index], low - start))
    return pieces


def row_starts(tables):
    starts = [0]
    for table in tables:
        starts.append(starts[-1] + table.shape[0])
    return starts


def chip_sum_kernel(keep_a, keep_b, got_a, got_b, blocks, sum_a, sum_b):
    sum_a[...] = keep_a[...] + got_a[...].astype(F32)
    sum_b[...] = keep_b[...] + got_b[...].astype(F32)
    tables = (sum_a, sum_b)
    starts = row_starts(tables)
    share = blocks.shape[1]
    for chip in range(CHIPS):
        pieces = cut(tables, starts, chip * share, (chip + 1) * share)
        rows = [table[low:high] for table, low, high, _ in pieces]
        blocks[chip] = (rows[0] if len(rows) == 1 else jnp.concatenate(rows, axis=0)).astype(BF16)


def share_kernel(moved, copies):
    total = moved[0].astype(F32)
    for chip in range(1, CHIPS):
        total = total + moved[chip].astype(F32)
    total = total.astype(BF16)
    for chip in range(CHIPS):
        copies[chip] = total


def unpack_kernel(place, own, other, *rest):
    results, (sum_a, sum_b) = rest[:4], rest[4:]
    share = own.shape[1]
    core = place[1] & 1
    tables = (sum_a, sum_b)
    starts = [0, sum_a.shape[0] // 2, sum_a.shape[0] // 2 + sum_b.shape[0] // 2]
    for source, at in ((own, core), (other, 1 - core)):
        for chip in range(CHIPS):
            piece = source[chip].astype(F32)
            for table, low, high, offset in cut(tables, starts, chip * share, (chip + 1) * share):
                base = pl.multiple_of(at * (table.shape[0] // 2), 64)
                table[pl.ds(base + low, high - low)] = piece[offset : offset + high - low]
    size = results[0].shape[0]
    results[0][...] = sum_a[:size]
    results[2][...] = sum_a[size:]
    results[1][...] = sum_b[:size]
    results[3][...] = sum_b[size:]


def exchange(blocks, axes):
    return lax.all_to_all(blocks, axes, 0, 0, tiled=True)


def body(inputs, cotangent, w_in, w_out, w_qkv, w_proj):
    rows, cols, chans = inputs.shape
    width = cols + 2 * EDGE
    place = jnp.stack([lax.axis_index("lat"), lax.axis_index(LON)]).astype(jnp.int32)
    shape = jax.ShapeDtypeStruct
    whole = pl.BlockSpec(memory_space=pltpu.VMEM)
    scalars = pl.BlockSpec(memory_space=pltpu.SMEM)
    conv_flops = 2 * rows * cols * 9 * chans * chans
    packed = pltpu.VMEM((12 * chans, 2 * chans), BF16)
    grads = pltpu.VMEM((2, rows // 2 + 1, width, 3 * chans), BF16)

    def taps(count):
        return pltpu.VMEM((count // 2, width, 6 * chans), BF16)

    lats, lons = lax.axis_size("lat"), lax.axis_size("chip") * lax.axis_size("core")
    up = [(i, i + 1) for i in range(lats - 1)]
    down = [(i + 1, i) for i in range(lats - 1)]
    east = [(i, (i + 1) % lons) for i in range(lons)]
    west = [((i + 1) % lons, i) for i in range(lons)]

    def two(cut):
        return jnp.concatenate([cut(inputs), cut(cotangent)], axis=0)

    left = lax.ppermute(two(lambda field: field[:, cols - EDGE :]), LON, east)
    right = lax.ppermute(two(lambda field: field[:, :EDGE]), LON, west)

    def wide_pair(start):
        def cut(side):
            return jnp.concatenate(
                [side[start : start + 2], side[rows + start : rows + start + 2]], axis=0
            )

        own = two(lambda field: field[start : start + 2])
        return jnp.concatenate([cut(left), own, cut(right)], axis=1)

    first, last = wide_pair(0), wide_pair(rows - 2)
    top = lax.ppermute(last, "lat", up)
    bottom = lax.ppermute(first, "lat", down)
    act, slope, sums = call(
        inner_kernel,
        (
            shape((rows - 2, width, chans), BF16),
            shape((rows - 2, width, chans), BF16),
            shape((16, chans), F32),
        ),
        [taps(rows), packed],
        conv_flops,
    )(inputs, left, right, w_in)
    act_edge, slope_edge, copies = call(
        edge_kernel,
        (
            shape((4, width, chans), BF16),
            shape((4, width, chans), BF16),
            shape((DEVICES * 16, chans), BF16),
        ),
        [taps(8), packed],
        conv_flops // 8,
    )(first, last, top, bottom, w_in, sums)
    grad_merged, grad_coarse = call(
        back_kernel,
        (shape((rows + 2, width, chans), F32), shape((16, chans), F32)),
        [taps(rows + 4), packed],
        conv_flops,
    )(cotangent, left, right, top, bottom, w_out)
    copies, grad_coarse, place = lax.optimization_barrier((copies, grad_coarse, place))
    tokens_all = exchange(copies, AXES)
    table = shape((DEVICES * 16, chans), BF16)
    coarse, message, grad_w_proj, soft, near, keys, values = call(
        attend_kernel,
        (
            shape((64, chans), F32),
            shape((DEVICES, 18, chans), BF16),
            shape((chans, chans), F32),
            shape((128, 1), F32),
            shape((64, chans), BF16),
            table,
            table,
        ),
        flops=2**28,
        in_specs=[scalars] + [whole] * 4,
    )(place, tokens_all, w_qkv, w_proj, grad_coarse)
    outputs, keep_b, send_b = call(
        decode_kernel,
        (
            shape((rows, cols, chans), BF16),
            shape((5 * chans, chans), F32),
            shape((5 * chans, chans), BF16),
        ),
        [taps(rows + 2), grads, packed, pltpu.VMEM((10 * chans, chans), F32)],
        2 * conv_flops,
        in_specs=[scalars] + [whole] * 6,
    )(place, act, act_edge, coarse, cotangent, w_out, grad_w_proj)
    wide = shape((128, DEVICES * 16), F32)
    queries, scores, prob, near_values = call(
        prepare_kernel,
        (table, wide, wide, shape((128, chans), BF16)),
        flops=2**28,
    )(tokens_all, near, keys, w_qkv, soft)
    message, send_b, prob = lax.optimization_barrier((message, send_b, prob))
    moved = exchange(message, AXES)
    grad_tokens, grad_w_qkv = call(
        attend_back_kernel,
        (shape((64, chans), F32), shape((3, chans, chans), F32)),
        flops=2**28,
        in_specs=[scalars] + [whole] * 11,
    )(
        place, near, keys, values, queries, scores, prob, near_values, moved, grad_coarse,
        w_qkv, w_proj,
    )
    swap = [(0, 1), (1, 0)]
    got_b = lax.ppermute(send_b, "core", swap)
    grad_hidden, keep_a, send_a = call(
        hidden_kernel,
        (
            shape((rows + 2, width, chans), BF16),
            shape((6 * chans, chans), F32),
            shape((6 * chans, chans), BF16),
        ),
        [taps(rows + 4), grads, pltpu.VMEM((12 * chans, chans), F32)],
        conv_flops,
        in_specs=[scalars] + [whole] * 10,
    )(
        place, slope, slope_edge, grad_merged, grad_tokens, grad_w_qkv, inputs, left, right,
        top, bottom,
    )
    got_a = lax.ppermute(send_a, "core", swap)
    share = 11 * chans // CHIPS
    blocks = call(
        chip_sum_kernel,
        shape((CHIPS, share, chans), BF16),
        [pltpu.VMEM(keep.shape, F32) for keep in (keep_a, keep_b)],
    )(keep_a, keep_b, got_a, got_b)
    partial = exchange(blocks, ("lat", "chip"))
    grad_inputs = call(
        inward_kernel,
        shape((rows, cols, chans), BF16),
        [taps(rows + 2), packed],
        conv_flops,
    )(grad_hidden, w_in)
    partial, grad_inputs = lax.optimization_barrier((partial, grad_inputs))
    copies = call(share_kernel, shape(blocks.shape, BF16))(partial)
    own = exchange(copies, ("lat", "chip"))
    other = lax.ppermute(own, "core", swap)
    shapes = (w_in.shape, w_out.shape, w_qkv.shape, w_proj.shape)
    pieces = call(
        unpack_kernel,
        tuple(shape((size * chans, chans), F32) for size in (9, 9, 3, 1)),
        [pltpu.VMEM((size * chans, chans), F32) for size in (12, 10)],
        in_specs=[scalars, whole, whole],
    )(place, own, other)
    pieces = [piece.reshape(dims) for piece, dims in zip(pieces, shapes)]
    return (outputs, grad_inputs, *pieces)


def solution(mesh):
    lats, lons = mesh.devices.shape
    fine = jax.sharding.Mesh(mesh.devices.reshape(lats, lons // 2, 2), AXES)
    field, whole = P("lat", LON, None), P()
    in_specs = (field, field, whole, whole, whole, whole)
    out_specs = (field, field, whole, whole, whole, whole)
    return jax.shard_map(body, mesh=fine, in_specs=in_specs, out_specs=out_specs, check_vma=False)
```

```python
import jax
import jax.numpy as jnp
from jax import lax
from jax.experimental import pallas as pl
from jax.experimental.pallas import tpu as pltpu
from jax.sharding import PartitionSpec as P

HEADS = 2
HEAD_DIM = 64
PATCH = 16
DEVICES = 128
CHIPS = 64
LON = ("chip", "core")
AXES = ("lat",) + LON
EDGE = 8
HIGHEST = lax.Precision.HIGHEST
F32 = jnp.float32
BF16 = jnp.bfloat16
NT = (((1,), (1,)), ((), ()))
TN = (((0,), (0,)), ((), ()))


def call(kernel, outs, scratch=(), flops=0, in_specs=None):
    return pl.pallas_call(
        kernel,
        out_shape=outs,
        **({"in_specs": in_specs} if in_specs else {}),
        scratch_shapes=list(scratch),
        compiler_params=pltpu.CompilerParams(vmem_limit_bytes=24 * 2**20),
        cost_estimate=pl.CostEstimate(flops=flops, bytes_accessed=8 * 2**20, transcendentals=0),
    )


def put_shifted(taps, pair, odd, wide):
    width, chans = wide.shape
    base = odd * 3 * chans
    taps[pair, :, base : base + chans] = pltpu.roll(wide, 1, 0).astype(BF16)
    taps[pair, :, base + chans : base + 2 * chans] = wide.astype(BF16)
    taps[pair, :, base + 2 * chans : base + 3 * chans] = pltpu.roll(wide, width - 1, 0).astype(BF16)


def wide_row(field, left, right, index, offset):
    parts = (left[offset + index], field[index], right[offset + index])
    return jnp.concatenate([part.astype(F32) for part in parts], axis=0)


def own_and_edges(field, left, right, top, bottom, second):
    rows = field.shape[0]

    def row(index):
        if index < 2:
            return top[2 * second + index].astype(F32)
        if index >= rows + 2:
            return bottom[2 * second + index - rows - 2].astype(F32)
        return wide_row(field, left, right, index - 2, second * rows)

    return row


def put_rows(taps, pair, row):
    for odd in range(2):
        put_shifted(taps, pair, odd, row(2 * pair + odd))


def stream_conv(taps, packed, row, emit):
    put_rows(taps, 0, row)
    for pair in range(taps.shape[0] - 1):
        put_rows(taps, pair + 1, row)
        emit(pair, pair_conv(taps, pair, packed))


def put_weight(packed, weight, inward):
    chans = weight.shape[2]
    none = jnp.zeros((chans, chans), BF16)
    for col in range(3):
        blocks = []
        for row in range(3):
            if inward:
                blocks.append(weight[2 - row, 2 - col].astype(F32).T.astype(BF16))
            else:
                blocks.append(weight[row, col])
        for source in range(4):
            for target in range(2):
                row = source - target
                block = blocks[row] if 0 <= row < 3 else none
                start = (source * 3 + col) * chans
                packed[start : start + chans, target * chans : (target + 1) * chans] = block


def pair_conv(taps, pair, weight):
    half = weight.shape[0] // 2
    low = jnp.dot(taps[pair], weight[:half], preferred_element_type=F32)
    return low + jnp.dot(taps[pair + 1], weight[half:], preferred_element_type=F32)


def spread_row(grid_row):
    chans = grid_row.shape[1]
    parts = [jnp.broadcast_to(grid_row[15:16], (EDGE, chans))]
    for col in range(8):
        parts.append(jnp.broadcast_to(grid_row[col : col + 1], (PATCH, chans)))
    parts.append(jnp.broadcast_to(grid_row[8:9], (EDGE, chans)))
    return jnp.concatenate(parts, axis=0)


def column_sums(total):
    inner = total[EDGE : EDGE + 8 * PATCH]
    return jnp.sum(inner.reshape(8, PATCH, -1), axis=1)


def activate(hidden):
    sigma = jax.nn.sigmoid(hidden)
    act = (hidden * sigma).astype(BF16)
    return act, (sigma * (1.0 + hidden * (1.0 - sigma))).astype(BF16)


def token_sums(rows):
    totals = [None, None]
    for index, row in rows:
        half, value = index // PATCH, row.astype(F32)
        totals[half] = value if totals[half] is None else totals[half] + value
    return jnp.concatenate([column_sums(total) for total in totals], axis=0)


def halves(both):
    chans = both.shape[1] // 2
    return [both[:, :chans], both[:, chans:]]


def inner_kernel(
    inputs, cotangent, left, right, w_in, w_out, act, slope, grad, sums, taps,
    taps_back, packed, packed_back,
):
    rows = inputs.shape[0]
    put_weight(packed, w_in, False)
    put_weight(packed_back, w_out, True)
    acts, grads = [], []

    def emit_act(pair, both):
        for odd, hidden in enumerate(halves(both)):
            index = 2 * pair + odd
            act[index], slope[index] = activate(hidden)
            acts.append((index + 1, act[index]))

    def emit_grad(pair, both):
        for odd, value in enumerate(halves(both)):
            grad[2 * pair + odd] = value.astype(BF16)
            grads.append((2 * pair + odd + 1, value))

    stream_conv(taps, packed, lambda index: wide_row(inputs, left, right, index, 0), emit_act)
    sums[:16] = token_sums(acts)
    stream_conv(
        taps_back, packed_back, lambda index: wide_row(cotangent, left, right, index, rows), emit_grad
    )
    sums[16:] = token_sums(grads)


def edge_kernel(
    first, last, top, bottom, w_in, w_out, sums, act, slope, grad, copies, coarse, taps, packed
):
    fields = (top, first, last, bottom)

    def convolve(weight, second, emit):
        put_weight(packed, weight, second)
        for pair, field in enumerate(fields):
            put_rows(taps, pair, lambda index, field=field: field[2 * second + (index & 1)].astype(F32))
        for side in range(2):
            for odd, value in enumerate(halves(pair_conv(taps, 2 * side, packed))):
                emit(2 * side + odd, value)

    def emit_act(index, hidden):
        act[index], slope[index] = activate(hidden)

    convolve(w_in, 0, emit_act)
    total = sums[:16] + token_sums([(0, act[1]), (31, act[2])])
    tokens = (total / (PATCH * PATCH)).astype(BF16)
    for device in range(DEVICES):
        copies[16 * device : 16 * (device + 1)] = tokens
    values = []

    def emit_grad(index, value):
        grad[index] = value.astype(BF16)
        values.append(value)

    convolve(w_out, 1, emit_grad)
    coarse[...] = sums[16:] + token_sums([(0, values[1]), (31, values[2])])


def near_index(place, shape, dim):
    entry = lax.broadcasted_iota(jnp.int32, shape, dim)
    row = 2 * place[0] + (((entry >> 4) + 1) & 3) - 1
    row = jnp.clip(row, 0, 15)
    col = (8 * place[1] + (((entry & 15) + 4) & 15) - 4) & 127
    device = (row >> 1) * 16 + (col >> 3)
    return device * 16 + (row & 1) * 8 + (col & 7)


def pick_near(place, table):
    count = table.shape[0]
    index = near_index(place, (64, count), 0)
    lane = lax.broadcasted_iota(jnp.int32, (64, count), 1)
    chosen = jnp.where(index == lane, 1.0, 0.0).astype(BF16)
    return jnp.dot(chosen, table, preferred_element_type=F32).astype(BF16)


def by_head(rows):
    lane = lax.broadcasted_iota(jnp.int32, rows.shape, 1)
    wide = rows.astype(F32)
    first = jnp.where(lane < HEAD_DIM, wide, 0.0)
    second = jnp.where(lane < HEAD_DIM, 0.0, wide)
    return jnp.concatenate([first, second], axis=0).astype(BF16)


def join_heads(rows):
    half = rows.shape[0] // 2
    lane = lax.broadcasted_iota(jnp.int32, (half, rows.shape[1]), 1)
    return jnp.where(lane < HEAD_DIM, rows[:half], rows[half:])


def low_dot(a, b):
    return jnp.dot(a, b, preferred_element_type=F32).astype(BF16)


def own_rows(near):
    return jnp.concatenate([near[0:8], near[16:24]], axis=0)


def split_three(value):
    high = value.astype(BF16)
    rest = value - high.astype(F32)
    mid = rest.astype(BF16)
    return high, mid, (rest - mid.astype(F32)).astype(BF16)


def attend_kernel(
    place, tokens, w_qkv, w_proj, grad_coarse, coarse, message, grad_proj, soft, near, keys, values
):
    scale = HEAD_DIM**-0.5
    near[...] = pick_near(place, tokens[...])
    keys[...] = low_dot(tokens[...], w_qkv[1])
    values[...] = low_dot(tokens[...], w_qkv[2])
    queries = by_head(low_dot(near[...], w_qkv[0]))
    scores = lax.dot_general(queries, keys[...], NT, preferred_element_type=F32) * scale
    top = jnp.max(scores, axis=1, keepdims=True)
    weights = jnp.exp(scores - top)
    total = jnp.sum(weights, axis=1, keepdims=True)
    prob = (weights / total).astype(BF16)
    mixed_wide = join_heads(jnp.dot(prob, values[...], preferred_element_type=F32))
    mixed = mixed_wide.astype(BF16)
    coarse[...] = near[...].astype(F32) + jnp.dot(
        mixed, w_proj[...], preferred_element_type=F32
    )
    log_sum = top + jnp.log(total)
    soft[...] = log_sum
    coarse_low = grad_coarse[...].astype(BF16)
    grad_proj[...] = lax.dot_general(
        own_rows(mixed), coarse_low, TN, preferred_element_type=F32
    )
    grad_mixed = lax.dot_general(coarse_low, w_proj[...], NT, preferred_element_type=F32)
    product = grad_mixed.astype(BF16).astype(F32) * own_rows(mixed_wide)
    lane = lax.broadcasted_iota(jnp.int32, product.shape, 1)
    inner = [
        jnp.sum(jnp.where(lane < HEAD_DIM, product, 0.0), axis=1, keepdims=True),
        jnp.sum(jnp.where(lane < HEAD_DIM, 0.0, product), axis=1, keepdims=True),
    ]
    logs = [own_rows(log_sum[:64]), own_rows(log_sum[64:])]
    token = lax.broadcasted_iota(jnp.int32, product.shape, 0)
    rows = []
    for pair in (logs, inner):
        row = jnp.zeros((1, 128), F32)
        for head in range(HEADS):
            for part, value in enumerate(split_three(pair[head])):
                slot = (head * 3 + part) * 16
                at = jnp.where(lane == token + slot, value.astype(F32), 0.0)
                row = row + jnp.sum(at, axis=0, keepdims=True)
        rows.append(row)
    text = jnp.concatenate([coarse_low.astype(F32)] + rows, axis=0).astype(BF16)
    for chip in range(CHIPS):
        message[chip] = text


def lane_stats(sums, head):
    count = sums.shape[0] * 16
    slot = lax.broadcasted_iota(jnp.int32, (128, count), 0)
    lane = lax.broadcasted_iota(jnp.int32, (128, count), 1)
    part = slot >> 4
    wanted = ((slot & 15) == (lane & 15)) & (part >= 3 * head) & (part < 3 * head + 3)
    chosen = jnp.where(wanted, 1.0, 0.0).astype(BF16)
    tiled = jnp.dot(sums, chosen, preferred_element_type=F32)
    entry = lax.broadcasted_iota(jnp.int32, tiled.shape, 0)
    device = ((entry & (CHIPS - 1)) << 1) + (entry >> 6)
    lane = lax.broadcasted_iota(jnp.int32, tiled.shape, 1)
    return jnp.sum(jnp.where(device == (lane >> 4), tiled, 0.0), axis=0, keepdims=True)


def prepare_kernel(tokens, near, keys, w_qkv, soft, queries, scores, prob, near_values):
    scale = HEAD_DIM**-0.5
    queries[...] = low_dot(tokens[...], w_qkv[0])
    near_q = by_head(low_dot(near[...], w_qkv[0]))
    near_k = by_head(low_dot(near[...], w_qkv[1]))
    near_values[...] = by_head(low_dot(near[...], w_qkv[2]))
    outward = lax.dot_general(near_q, keys[...], NT, preferred_element_type=F32) * scale
    prob[...] = jnp.exp(outward - soft[...])
    scores[...] = lax.dot_general(near_k, queries[...], NT, preferred_element_type=F32) * scale


def attend_back_kernel(
    place, near, keys, values, queries, scores, prob_out, near_values, own, other, grad_coarse,
    w_qkv, w_proj, grad_tokens, grad_qkv,
):
    scale = HEAD_DIM**-0.5
    chans = own.shape[2]
    first_core = (place[1] & 1) == 0

    def in_order(cut):
        mine, theirs = cut(own).astype(F32), cut(other).astype(F32)
        return jnp.where(first_core, mine, theirs), jnp.where(first_core, theirs, mine)

    tokens_of = in_order(lambda half: half[:, :16, :])
    coarse_low = jnp.stack(tokens_of, axis=1).reshape(-1, chans).astype(BF16)
    count = coarse_low.shape[0]
    logs, inner = (
        jnp.concatenate(in_order(lambda half: half[:, row, :]), axis=0).astype(BF16)
        for row in (16, 17)
    )
    near_low = pick_near(place, coarse_low)
    mixed = lax.dot_general(coarse_low, w_proj[...], NT, preferred_element_type=F32).astype(BF16)
    near_mixed = lax.dot_general(
        near_low, w_proj[...], NT, preferred_element_type=F32
    ).astype(BF16)
    grad_prob = lax.dot_general(by_head(near_mixed), values[...], NT, preferred_element_type=F32)
    prob = prob_out[...]
    mean = jnp.sum(prob * grad_prob, axis=1, keepdims=True)
    grad_score = (prob * (grad_prob - mean) * scale).astype(BF16)
    grad_q = join_heads(jnp.dot(grad_score, keys[...], preferred_element_type=F32))

    def both_heads(table):
        first = jnp.broadcast_to(lane_stats(table, 0), (64, count))
        second = jnp.broadcast_to(lane_stats(table, 1), (64, count))
        return jnp.concatenate([first, second], axis=0)

    prob = jnp.exp(scores[...] - both_heads(logs))
    grad_prob = lax.dot_general(near_values[...], mixed, NT, preferred_element_type=F32)
    grad_score = (prob * (grad_prob - both_heads(inner)) * scale).astype(BF16)
    grad_k = join_heads(jnp.dot(grad_score, queries[...], preferred_element_type=F32))
    grad_v = join_heads(jnp.dot(prob.astype(BF16), mixed, preferred_element_type=F32))
    nearest = jnp.concatenate(
        [grad_coarse[0:8], near_low[8:16].astype(F32), grad_coarse[8:16]], axis=0
    )
    result = jnp.concatenate([nearest, near_low[24:].astype(F32)], axis=0)
    grads = jnp.concatenate([grad_q, grad_k, grad_v], axis=1)
    wide = jnp.concatenate([w_qkv[index].astype(F32) for index in range(3)], axis=1)
    result = result + lax.dot_general(
        grads, wide, NT, precision=HIGHEST, preferred_element_type=F32
    )
    own_tokens = own_rows(near[...].astype(F32))
    products = lax.dot_general(
        own_tokens, own_rows(grads), TN, precision=HIGHEST, preferred_element_type=F32
    )
    for index in range(3):
        grad_qkv[index] = products[:, index * chans : (index + 1) * chans]
    grad_tokens[...] = result


def row_of(index):
    if index == 0:
        return 3
    return min((index - 1) // PATCH, 2)


def inside(place, index, rows):
    if index == 0:
        return jnp.where(place[0] == 0, 0.0, 1.0)
    if index == rows - 1:
        return jnp.where(place[0] == 7, 0.0, 1.0)
    return None


def put_products(grads, rows_of):
    chans = grads.shape[3] // 3
    rows = 2 * grads.shape[1] - 2
    zero = jnp.zeros((grads.shape[2], chans), BF16)
    for row in range(-1, rows + 3):
        kept = rows_of(row - 1) if 0 < row < rows + 1 else zero
        for tap in range(3):
            target = row - 1 + tap
            if 0 <= target < rows + 2:
                odd, place = target & 1, target >> 1
                grads[odd, place, :, tap * chans : (tap + 1) * chans] = kept


def weight_grads(pieces, grads, result):
    chans = result.shape[1]
    width = grads.shape[2]
    total = jnp.zeros((3 * chans, 3 * chans), F32)
    for taps, first, count, odd, parity, place in pieces:
        left = taps[first : first + count, :, odd * 3 * chans : (odd + 1) * 3 * chans]
        right = grads[parity, place : place + count]
        total = total + lax.dot_general(
            left.reshape(count * width, 3 * chans),
            right.reshape(count * width, 3 * chans),
            TN,
            preferred_element_type=F32,
        )
    for tap in range(3):
        result[tap * 3 * chans : (tap + 1) * 3 * chans] = total[:, tap * chans : (tap + 1) * chans]


def halve(place, table, keep, send):
    half = keep.shape[0]
    core = place[1] & 1
    keep[...] = table[pl.ds(pl.multiple_of(core * half, 64), half)]
    send[...] = table[pl.ds(pl.multiple_of((1 - core) * half, 64), half)].astype(BF16)


def pick(inner, edge, index):
    rows = inner.shape[0]
    if index < 2:
        return edge[index]
    return inner[index - 2] if index < rows + 2 else edge[index - rows]


def products_kernel(cotangent, grads):
    chans = cotangent.shape[2]
    side = jnp.zeros((EDGE, chans), F32)

    def rows_of(row):
        parts = [side, cotangent[row].astype(F32), side]
        return jnp.concatenate(parts, axis=0).astype(BF16)

    put_products(grads, rows_of)


def decode_kernel(place, act, edge, coarse, grads, grad_proj, merged, keep, send, taps, table):
    rows, _, chans = merged.shape
    grid = [spread_row(coarse[16 * row : 16 * (row + 1)]) for row in range(4)]
    for index in range(rows):
        value = pick(act, edge, index).astype(F32) + grid[row_of(index)]
        factor = inside(place, index, rows)
        value = value if factor is None else value * factor
        merged[index] = value.astype(BF16)
        put_shifted(taps, index >> 1, index & 1, value)
    count = rows // 2
    weight_grads([(taps, 0, count, 0, 0, 0), (taps, 0, count, 1, 1, 0)], grads, table)
    table[9 * chans :] = grad_proj[...]
    halve(place, table, keep, send)


def hidden_kernel(
    place, slope, slope_edge, grad, grad_edge, grad_tokens, grad_qkv, taps, top, bottom,
    result, keep, send, ends, grads, table,
):
    rows, width, chans = result.shape
    for pair, field in enumerate((top, bottom)):
        put_rows(ends, pair, lambda index, field=field: field[index & 1].astype(F32))
    grid = [
        spread_row(grad_tokens[16 * row : 16 * (row + 1)] * (1.0 / (PATCH * PATCH)))
        for row in range(4)
    ]
    for index in range(rows):
        value = pick(grad, grad_edge, index).astype(F32) + grid[row_of(index)]
        value = value * pick(slope, slope_edge, index).astype(F32)
        factor = inside(place, index, rows)
        result[index] = (value if factor is None else value * factor).astype(BF16)
    column = lax.broadcasted_iota(jnp.int32, (width, chans), 0)
    own = (column >= EDGE) & (column < width - EDGE)

    def rows_of(row):
        return jnp.where(own, result[row + 1].astype(F32), 0.0).astype(BF16)

    put_products(grads, rows_of)
    count = taps.shape[0]
    pieces = [
        (taps, 0, count, 0, 1, 0), (taps, 0, count, 1, 0, 1),
        (ends, 0, 1, 1, 0, 0), (ends, 1, 1, 0, 1, count),
    ]
    weight_grads(pieces, grads, table)
    for index in range(3):
        table[(9 + index) * chans : (10 + index) * chans] = grad_qkv[index]
    halve(place, table, keep, send)


def last_kernel(hidden, merged, w_in, w_out, grad_inputs, outputs, taps, packed, taps_2, packed_2):
    put_weight(packed, w_in, True)
    put_weight(packed_2, w_out, False)

    def emit_to(result):
        def emit(pair, both):
            for odd, value in enumerate(halves(both)):
                result[2 * pair + odd] = value[EDGE : EDGE + 128].astype(BF16)

        return emit

    stream_conv(taps, packed, lambda index: hidden[index].astype(F32), emit_to(grad_inputs))
    stream_conv(taps_2, packed_2, lambda index: merged[index].astype(F32), emit_to(outputs))


def cut(tables, starts, start, stop):
    pieces = []
    for index, table in enumerate(tables):
        low, high = max(start, starts[index]), min(stop, starts[index + 1])
        if low < high:
            pieces.append((table, low - starts[index], high - starts[index], low - start))
    return pieces


def row_starts(tables):
    starts = [0]
    for table in tables:
        starts.append(starts[-1] + table.shape[0])
    return starts


def chip_sum_kernel(keep_a, keep_b, got_a, got_b, blocks, sum_a, sum_b):
    sum_a[...] = keep_a[...] + got_a[...].astype(F32)
    sum_b[...] = keep_b[...] + got_b[...].astype(F32)
    tables = (sum_a, sum_b)
    starts = row_starts(tables)
    share = blocks.shape[1]
    for chip in range(CHIPS):
        pieces = cut(tables, starts, chip * share, (chip + 1) * share)
        rows = [table[low:high] for table, low, high, _ in pieces]
        blocks[chip] = (rows[0] if len(rows) == 1 else jnp.concatenate(rows, axis=0)).astype(BF16)


def share_kernel(moved, copies):
    total = moved[0].astype(F32)
    for chip in range(1, CHIPS):
        total = total + moved[chip].astype(F32)
    total = total.astype(BF16)
    for chip in range(CHIPS):
        copies[chip] = total


def unpack_kernel(place, own, other, *rest):
    results, (sum_a, sum_b) = rest[:4], rest[4:]
    share = own.shape[1]
    core = place[1] & 1
    tables = (sum_a, sum_b)
    starts = [0, sum_a.shape[0] // 2, sum_a.shape[0] // 2 + sum_b.shape[0] // 2]
    for source, at in ((own, core), (other, 1 - core)):
        for chip in range(CHIPS):
            piece = source[chip].astype(F32)
            for table, low, high, offset in cut(tables, starts, chip * share, (chip + 1) * share):
                base = pl.multiple_of(at * (table.shape[0] // 2), 64)
                table[pl.ds(base + low, high - low)] = piece[offset : offset + high - low]
    size = results[0].shape[0]
    results[0][...] = sum_a[:size]
    results[2][...] = sum_a[size:]
    results[1][...] = sum_b[:size]
    results[3][...] = sum_b[size:]


def exchange(blocks, axes):
    return lax.all_to_all(blocks, axes, 0, 0, tiled=True)


def body(inputs, cotangent, w_in, w_out, w_qkv, w_proj):
    rows, cols, chans = inputs.shape
    width = cols + 2 * EDGE
    place = jnp.stack([lax.axis_index("lat"), lax.axis_index(LON)]).astype(jnp.int32)
    shape = jax.ShapeDtypeStruct
    whole = pl.BlockSpec(memory_space=pltpu.VMEM)
    scalars = pl.BlockSpec(memory_space=pltpu.SMEM)
    conv_flops = 2 * rows * cols * 9 * chans * chans
    packed = pltpu.VMEM((12 * chans, 2 * chans), BF16)
    grads = pltpu.VMEM((2, rows // 2 + 1, width, 3 * chans), BF16)

    def taps(count):
        return pltpu.VMEM((count // 2, width, 6 * chans), BF16)

    lats, lons = lax.axis_size("lat"), lax.axis_size("chip") * lax.axis_size("core")
    up = [(i, i + 1) for i in range(lats - 1)]
    down = [(i + 1, i) for i in range(lats - 1)]
    east = [(i, (i + 1) % lons) for i in range(lons)]
    west = [((i + 1) % lons, i) for i in range(lons)]

    def two(cut):
        return jnp.concatenate([cut(inputs), cut(cotangent)], axis=0)

    left = lax.ppermute(two(lambda field: field[:, cols - EDGE :]), LON, east)
    right = lax.ppermute(two(lambda field: field[:, :EDGE]), LON, west)

    def wide_pair(start):
        def cut(side):
            return jnp.concatenate(
                [side[start : start + 2], side[rows + start : rows + start + 2]], axis=0
            )

        own = two(lambda field: field[start : start + 2])
        return jnp.concatenate([cut(left), own, cut(right)], axis=1)

    first, last = wide_pair(0), wide_pair(rows - 2)
    top = lax.ppermute(last, "lat", up)
    bottom = lax.ppermute(first, "lat", down)
    inner_field = shape((rows - 2, width, chans), BF16)
    edge_field = shape((4, width, chans), BF16)
    field = shape((rows + 2, width, chans), BF16)
    products = call(products_kernel, shape(grads.shape, BF16), flops=2**27)(cotangent)
    act, slope, grad, sums, taps_in = call(
        inner_kernel,
        (
            inner_field,
            inner_field,
            inner_field,
            shape((32, chans), F32),
            shape((rows // 2, width, 6 * chans), BF16),
        ),
        [taps(rows), packed, packed],
        2 * conv_flops,
    )(inputs, cotangent, left, right, w_in, w_out)
    act_edge, slope_edge, grad_edge, copies, grad_coarse = call(
        edge_kernel,
        (
            edge_field,
            edge_field,
            edge_field,
            shape((DEVICES * 16, chans), BF16),
            shape((16, chans), F32),
        ),
        [taps(8), packed],
        conv_flops // 4,
    )(first, last, top, bottom, w_in, w_out, sums)
    copies, products, place = lax.optimization_barrier((copies, products, place))
    tokens_all = exchange(copies, AXES)
    table = shape((DEVICES * 16, chans), BF16)
    coarse, message, grad_w_proj, soft, near, keys, values = call(
        attend_kernel,
        (
            shape((64, chans), F32),
            shape((CHIPS, 18, chans), BF16),
            shape((chans, chans), F32),
            shape((128, 1), F32),
            shape((64, chans), BF16),
            table,
            table,
        ),
        flops=2**28,
        in_specs=[scalars] + [whole] * 4,
    )(place, tokens_all, w_qkv, w_proj, grad_coarse)
    merged, keep_b, send_b = call(
        decode_kernel,
        (field, shape((5 * chans, chans), F32), shape((5 * chans, chans), BF16)),
        [taps(rows + 2), pltpu.VMEM((10 * chans, chans), F32)],
        2 * conv_flops,
        in_specs=[scalars] + [whole] * 5,
    )(place, act, act_edge, coarse, products, grad_w_proj)
    wide = shape((128, DEVICES * 16), F32)
    queries, scores, prob, near_values = call(
        prepare_kernel,
        (table, wide, wide, shape((128, chans), BF16)),
        flops=2**28,
    )(tokens_all, near, keys, w_qkv, soft)
    message, send_b, prob = lax.optimization_barrier((message, send_b, prob))
    swap = [(0, 1), (1, 0)]
    own = exchange(message, ("lat", "chip"))
    other = lax.ppermute(own, "core", swap)
    grad_tokens, grad_w_qkv = call(
        attend_back_kernel,
        (shape((64, chans), F32), shape((3, chans, chans), F32)),
        flops=2**28,
        in_specs=[scalars] + [whole] * 12,
    )(
        place, near, keys, values, queries, scores, prob, near_values, own, other, grad_coarse,
        w_qkv, w_proj,
    )
    got_b = lax.ppermute(send_b, "core", swap)
    grad_hidden, keep_a, send_a = call(
        hidden_kernel,
        (field, shape((6 * chans, chans), F32), shape((6 * chans, chans), BF16)),
        [taps(4), grads, pltpu.VMEM((12 * chans, chans), F32)],
        conv_flops,
        in_specs=[scalars] + [whole] * 9,
    )(
        place, slope, slope_edge, grad, grad_edge, grad_tokens, grad_w_qkv, taps_in, top, bottom
    )
    got_a = lax.ppermute(send_a, "core", swap)
    share = 11 * chans // CHIPS
    blocks = call(
        chip_sum_kernel,
        shape((CHIPS, share, chans), BF16),
        [pltpu.VMEM(keep.shape, F32) for keep in (keep_a, keep_b)],
    )(keep_a, keep_b, got_a, got_b)
    partial = exchange(blocks, ("lat", "chip"))
    grad_inputs, outputs = call(
        last_kernel,
        (shape((rows, cols, chans), BF16), shape((rows, cols, chans), BF16)),
        [taps(rows + 2), packed, taps(rows + 2), packed],
        2 * conv_flops,
    )(grad_hidden, merged, w_in, w_out)
    partial, grad_inputs = lax.optimization_barrier((partial, grad_inputs))
    copies = call(share_kernel, shape(blocks.shape, BF16))(partial)
    own = exchange(copies, ("lat", "chip"))
    other = lax.ppermute(own, "core", swap)
    shapes = (w_in.shape, w_out.shape, w_qkv.shape, w_proj.shape)
    pieces = call(
        unpack_kernel,
        tuple(shape((size * chans, chans), F32) for size in (9, 9, 3, 1)),
        [pltpu.VMEM((size * chans, chans), F32) for size in (12, 10)],
        in_specs=[scalars, whole, whole],
    )(place, own, other)
    pieces = [piece.reshape(dims) for piece, dims in zip(pieces, shapes)]
    return (outputs, grad_inputs, *pieces)


def solution(mesh):
    lats, lons = mesh.devices.shape
    fine = jax.sharding.Mesh(mesh.devices.reshape(lats, lons // 2, 2), AXES)
    field, whole = P("lat", LON, None), P()
    in_specs = (field, field, whole, whole, whole, whole)
    out_specs = (field, field, whole, whole, whole, whole)
    return jax.shard_map(body, mesh=fine, in_specs=in_specs, out_specs=out_specs, check_vma=False)
```

```python
import jax
import jax.numpy as jnp
from jax import lax
from jax.experimental import pallas as pl
from jax.experimental.pallas import tpu as pltpu
from jax.sharding import PartitionSpec as P

HEADS = 2
HEAD_DIM = 64
PATCH = 16
DEVICES = 128
CHIPS = 64
LON = ("chip", "core")
AXES = ("lat",) + LON
EDGE = 8
HALO = 2
HIGHEST = lax.Precision.HIGHEST
F32 = jnp.float32
BF16 = jnp.bfloat16
NT = (((1,), (1,)), ((), ()))
TN = (((0,), (0,)), ((), ()))


def call(kernel, outs, scratch=(), flops=0, in_specs=None):
    return pl.pallas_call(
        kernel,
        out_shape=outs,
        **({"in_specs": in_specs} if in_specs else {}),
        scratch_shapes=list(scratch),
        compiler_params=pltpu.CompilerParams(vmem_limit_bytes=24 * 2**20),
        cost_estimate=pl.CostEstimate(flops=flops, bytes_accessed=8 * 2**20, transcendentals=0),
    )


def put_shifted(taps, pair, odd, wide):
    width, chans = wide.shape
    base = odd * 3 * chans
    taps[pair, :, base : base + chans] = pltpu.roll(wide, 1, 0).astype(BF16)
    taps[pair, :, base + chans : base + 2 * chans] = wide.astype(BF16)
    taps[pair, :, base + 2 * chans : base + 3 * chans] = pltpu.roll(wide, width - 1, 0).astype(BF16)


def wide_row(field, left, right, index, offset):
    blank = jnp.zeros((EDGE - HALO, field.shape[2]), F32)
    parts = [part.astype(F32) for part in (left[offset + index], field[index], right[offset + index])]
    return jnp.concatenate([blank] + parts + [blank], axis=0)


def own_and_edges(field, left, right, top, bottom, second):
    rows = field.shape[0]

    def row(index):
        if index < 2:
            return top[2 * second + index].astype(F32)
        if index >= rows + 2:
            return bottom[2 * second + index - rows - 2].astype(F32)
        return wide_row(field, left, right, index - 2, second * rows)

    return row


def put_rows(taps, pair, row):
    for odd in range(2):
        put_shifted(taps, pair, odd, row(2 * pair + odd))


def stream_conv(taps, packed, row, emit):
    put_rows(taps, 0, row)
    for pair in range(taps.shape[0] - 1):
        put_rows(taps, pair + 1, row)
        emit(pair, pair_conv(taps, pair, packed))


def put_weight(packed, weight, inward):
    chans = weight.shape[2]
    none = jnp.zeros((chans, chans), BF16)
    for col in range(3):
        blocks = []
        for row in range(3):
            if inward:
                blocks.append(weight[2 - row, 2 - col].astype(F32).T.astype(BF16))
            else:
                blocks.append(weight[row, col])
        for source in range(4):
            for target in range(2):
                row = source - target
                block = blocks[row] if 0 <= row < 3 else none
                start = (source * 3 + col) * chans
                packed[start : start + chans, target * chans : (target + 1) * chans] = block


def pair_conv(taps, pair, weight):
    half = weight.shape[0] // 2
    low = jnp.dot(taps[pair], weight[:half], preferred_element_type=F32)
    return low + jnp.dot(taps[pair + 1], weight[half:], preferred_element_type=F32)


def spread_row(grid_row):
    chans = grid_row.shape[1]
    parts = [jnp.broadcast_to(grid_row[15:16], (EDGE, chans))]
    for col in range(8):
        parts.append(jnp.broadcast_to(grid_row[col : col + 1], (PATCH, chans)))
    parts.append(jnp.broadcast_to(grid_row[8:9], (EDGE, chans)))
    return jnp.concatenate(parts, axis=0)


def column_sums(total):
    inner = total[EDGE : EDGE + 8 * PATCH]
    return jnp.sum(inner.reshape(8, PATCH, -1), axis=1)


def activate(hidden):
    sigma = jax.nn.sigmoid(hidden)
    act = (hidden * sigma).astype(BF16)
    return act, (sigma * (1.0 + hidden * (1.0 - sigma))).astype(BF16)


def token_sums(rows):
    totals = [None, None]
    for index, row in rows:
        half, value = index // PATCH, row.astype(F32)
        totals[half] = value if totals[half] is None else totals[half] + value
    return jnp.concatenate([column_sums(total) for total in totals], axis=0)


def halves(both):
    chans = both.shape[1] // 2
    return [both[:, :chans], both[:, chans:]]


def inner_kernel(
    inputs, cotangent, left, right, w_in, w_out, act, slope, grad, sums, taps,
    taps_back, packed, packed_back,
):
    rows = inputs.shape[0]
    put_weight(packed, w_in, False)
    put_weight(packed_back, w_out, True)
    acts, grads = [], []

    def emit_act(pair, both):
        for odd, hidden in enumerate(halves(both)):
            index = 2 * pair + odd
            act[index], slope[index] = activate(hidden)
            acts.append((index + 1, act[index]))

    def emit_grad(pair, both):
        for odd, value in enumerate(halves(both)):
            grad[2 * pair + odd] = value.astype(BF16)
            grads.append((2 * pair + odd + 1, value))

    stream_conv(taps, packed, lambda index: wide_row(inputs, left, right, index, 0), emit_act)
    sums[:16] = token_sums(acts)
    stream_conv(
        taps_back, packed_back, lambda index: wide_row(cotangent, left, right, index, rows), emit_grad
    )
    sums[16:] = token_sums(grads)


def edge_kernel(
    first, last, top, bottom, w_in, w_out, sums, act, slope, grad, copies, coarse, taps, packed
):
    fields = (top, first, last, bottom)

    def convolve(weight, second, emit):
        put_weight(packed, weight, second)
        for pair, field in enumerate(fields):
            put_rows(taps, pair, lambda index, field=field: field[2 * second + (index & 1)].astype(F32))
        for side in range(2):
            for odd, value in enumerate(halves(pair_conv(taps, 2 * side, packed))):
                emit(2 * side + odd, value)

    def emit_act(index, hidden):
        act[index], slope[index] = activate(hidden)

    convolve(w_in, 0, emit_act)
    total = sums[:16] + token_sums([(0, act[1]), (31, act[2])])
    tokens = (total / (PATCH * PATCH)).astype(BF16)
    for device in range(DEVICES):
        copies[16 * device : 16 * (device + 1)] = tokens
    values = []

    def emit_grad(index, value):
        grad[index] = value.astype(BF16)
        values.append(value)

    convolve(w_out, 1, emit_grad)
    coarse[...] = sums[16:] + token_sums([(0, values[1]), (31, values[2])])


def near_index(place, shape, dim):
    entry = lax.broadcasted_iota(jnp.int32, shape, dim)
    row = 2 * place[0] + (((entry >> 4) + 1) & 3) - 1
    row = jnp.clip(row, 0, 15)
    col = (8 * place[1] + (((entry & 15) + 4) & 15) - 4) & 127
    device = (row >> 1) * 16 + (col >> 3)
    return device * 16 + (row & 1) * 8 + (col & 7)


def pick_near(place, table):
    count = table.shape[0]
    index = near_index(place, (64, count), 0)
    lane = lax.broadcasted_iota(jnp.int32, (64, count), 1)
    chosen = jnp.where(index == lane, 1.0, 0.0).astype(BF16)
    return jnp.dot(chosen, table, preferred_element_type=F32).astype(BF16)


def by_head(rows):
    lane = lax.broadcasted_iota(jnp.int32, rows.shape, 1)
    wide = rows.astype(F32)
    first = jnp.where(lane < HEAD_DIM, wide, 0.0)
    second = jnp.where(lane < HEAD_DIM, 0.0, wide)
    return jnp.concatenate([first, second], axis=0).astype(BF16)


def join_heads(rows):
    half = rows.shape[0] // 2
    lane = lax.broadcasted_iota(jnp.int32, (half, rows.shape[1]), 1)
    return jnp.where(lane < HEAD_DIM, rows[:half], rows[half:])


def low_dot(a, b):
    return jnp.dot(a, b, preferred_element_type=F32).astype(BF16)


def own_rows(near):
    return jnp.concatenate([near[0:8], near[16:24]], axis=0)


def split_three(value):
    high = value.astype(BF16)
    rest = value - high.astype(F32)
    mid = rest.astype(BF16)
    return high, mid, (rest - mid.astype(F32)).astype(BF16)


def attend_kernel(
    place, tokens, w_qkv, w_proj, grad_coarse, coarse, message, grad_proj, soft, near, keys, values
):
    scale = HEAD_DIM**-0.5
    near[...] = pick_near(place, tokens[...])
    keys[...] = low_dot(tokens[...], w_qkv[1])
    values[...] = low_dot(tokens[...], w_qkv[2])
    queries = by_head(low_dot(near[...], w_qkv[0]))
    scores = lax.dot_general(queries, keys[...], NT, preferred_element_type=F32) * scale
    top = jnp.max(scores, axis=1, keepdims=True)
    weights = jnp.exp(scores - top)
    total = jnp.sum(weights, axis=1, keepdims=True)
    prob = (weights / total).astype(BF16)
    mixed_wide = join_heads(jnp.dot(prob, values[...], preferred_element_type=F32))
    mixed = mixed_wide.astype(BF16)
    coarse[...] = near[...].astype(F32) + jnp.dot(
        mixed, w_proj[...], preferred_element_type=F32
    )
    log_sum = top + jnp.log(total)
    soft[...] = log_sum
    coarse_low = grad_coarse[...].astype(BF16)
    grad_proj[...] = lax.dot_general(
        own_rows(mixed), coarse_low, TN, preferred_element_type=F32
    )
    grad_mixed = lax.dot_general(coarse_low, w_proj[...], NT, preferred_element_type=F32)
    product = grad_mixed.astype(BF16).astype(F32) * own_rows(mixed_wide)
    lane = lax.broadcasted_iota(jnp.int32, product.shape, 1)
    inner = [
        jnp.sum(jnp.where(lane < HEAD_DIM, product, 0.0), axis=1, keepdims=True),
        jnp.sum(jnp.where(lane < HEAD_DIM, 0.0, product), axis=1, keepdims=True),
    ]
    logs = [own_rows(log_sum[:64]), own_rows(log_sum[64:])]
    token = lax.broadcasted_iota(jnp.int32, product.shape, 0)
    rows = []
    for pair in (logs, inner):
        row = jnp.zeros((1, 128), F32)
        for head in range(HEADS):
            for part, value in enumerate(split_three(pair[head])):
                slot = (head * 3 + part) * 16
                at = jnp.where(lane == token + slot, value.astype(F32), 0.0)
                row = row + jnp.sum(at, axis=0, keepdims=True)
        rows.append(row)
    text = jnp.concatenate([coarse_low.astype(F32)] + rows, axis=0).astype(BF16)
    for chip in range(CHIPS):
        message[chip] = text


def lane_stats(tables):
    count = DEVICES * 16
    part = lax.broadcasted_iota(jnp.int32, (DEVICES, 128), 1) >> 4
    rows = []
    for table in tables:
        wide = table.astype(F32)
        for head in range(HEADS):
            mine = (part >= 3 * head) & (part < 3 * head + 3)
            rows.append(jnp.where(mine, wide, 0.0).astype(BF16))
    slot = lax.broadcasted_iota(jnp.int32, (128, count), 0)
    lane = lax.broadcasted_iota(jnp.int32, (128, count), 1)
    chosen = jnp.where((slot & 15) == (lane & 15), 1.0, 0.0).astype(BF16)
    tiled = jnp.dot(jnp.concatenate(rows, axis=0), chosen, preferred_element_type=F32)
    entry = lax.broadcasted_iota(jnp.int32, (DEVICES, count), 0)
    device = ((entry & (CHIPS - 1)) << 1) + (entry >> 6)
    mine = device == (lax.broadcasted_iota(jnp.int32, (DEVICES, count), 1) >> 4)
    sums = []
    for index in range(len(rows)):
        block = tiled[index * DEVICES : (index + 1) * DEVICES]
        sums.append(jnp.sum(jnp.where(mine, block, 0.0), axis=0, keepdims=True))
    return sums


def prepare_kernel(tokens, near, keys, w_qkv, soft, queries, scores, prob, near_values):
    scale = HEAD_DIM**-0.5
    queries[...] = low_dot(tokens[...], w_qkv[0])
    near_q = by_head(low_dot(near[...], w_qkv[0]))
    near_k = by_head(low_dot(near[...], w_qkv[1]))
    near_values[...] = by_head(low_dot(near[...], w_qkv[2]))
    outward = lax.dot_general(near_q, keys[...], NT, preferred_element_type=F32) * scale
    prob[...] = jnp.exp(outward - soft[...])
    scores[...] = lax.dot_general(near_k, queries[...], NT, preferred_element_type=F32) * scale


def attend_back_kernel(
    place, near, keys, values, queries, scores, prob_out, near_values, own, other, grad_coarse,
    w_qkv, w_proj, grad_tokens, grad_qkv,
):
    scale = HEAD_DIM**-0.5
    chans = own.shape[2]
    first_core = (place[1] & 1) == 0

    def in_order(cut):
        mine, theirs = cut(own).astype(F32), cut(other).astype(F32)
        return jnp.where(first_core, mine, theirs), jnp.where(first_core, theirs, mine)

    tokens_of = in_order(lambda half: half[:, :16, :])
    coarse_low = jnp.stack(tokens_of, axis=1).reshape(-1, chans).astype(BF16)
    count = coarse_low.shape[0]
    logs, inner = (
        jnp.concatenate(in_order(lambda half: half[:, row, :]), axis=0).astype(BF16)
        for row in (16, 17)
    )
    near_low = pick_near(place, coarse_low)
    mixed = lax.dot_general(coarse_low, w_proj[...], NT, preferred_element_type=F32).astype(BF16)
    near_mixed = lax.dot_general(
        near_low, w_proj[...], NT, preferred_element_type=F32
    ).astype(BF16)
    grad_prob = lax.dot_general(by_head(near_mixed), values[...], NT, preferred_element_type=F32)
    prob = prob_out[...]
    mean = jnp.sum(prob * grad_prob, axis=1, keepdims=True)
    grad_score = (prob * (grad_prob - mean) * scale).astype(BF16)
    grad_q = join_heads(jnp.dot(grad_score, keys[...], preferred_element_type=F32))

    stats = lane_stats((logs, inner))

    def both_heads(first, second):
        spread = [jnp.broadcast_to(row, (64, count)) for row in (first, second)]
        return jnp.concatenate(spread, axis=0)

    prob = jnp.exp(scores[...] - both_heads(*stats[:2]))
    grad_prob = lax.dot_general(near_values[...], mixed, NT, preferred_element_type=F32)
    grad_score = (prob * (grad_prob - both_heads(*stats[2:])) * scale).astype(BF16)
    grad_k = join_heads(jnp.dot(grad_score, queries[...], preferred_element_type=F32))
    grad_v = join_heads(jnp.dot(prob.astype(BF16), mixed, preferred_element_type=F32))
    nearest = jnp.concatenate(
        [grad_coarse[0:8], near_low[8:16].astype(F32), grad_coarse[8:16]], axis=0
    )
    result = jnp.concatenate([nearest, near_low[24:].astype(F32)], axis=0)
    grads = jnp.concatenate([grad_q, grad_k, grad_v], axis=1)
    wide = jnp.concatenate([w_qkv[index].astype(F32) for index in range(3)], axis=1)
    result = result + lax.dot_general(
        grads, wide, NT, precision=HIGHEST, preferred_element_type=F32
    )
    own_tokens = own_rows(near[...].astype(F32))
    products = lax.dot_general(
        own_tokens, own_rows(grads), TN, precision=HIGHEST, preferred_element_type=F32
    )
    for index in range(3):
        grad_qkv[index] = products[:, index * chans : (index + 1) * chans]
    grad_tokens[...] = result


def row_of(index):
    if index == 0:
        return 3
    return min((index - 1) // PATCH, 2)


def inside(place, index, rows):
    if index == 0:
        return jnp.where(place[0] == 0, 0.0, 1.0)
    if index == rows - 1:
        return jnp.where(place[0] == 7, 0.0, 1.0)
    return None


def put_products(grads, rows_of):
    chans = grads.shape[3] // 3
    rows = 2 * grads.shape[1] - 2
    zero = jnp.zeros((grads.shape[2], chans), BF16)
    for row in range(-1, rows + 3):
        kept = rows_of(row - 1) if 0 < row < rows + 1 else zero
        for tap in range(3):
            target = row - 1 + tap
            if 0 <= target < rows + 2:
                odd, place = target & 1, target >> 1
                grads[odd, place, :, tap * chans : (tap + 1) * chans] = kept


def weight_grads(pieces, grads, result):
    chans = result.shape[1]
    width = grads.shape[2]
    total = jnp.zeros((3 * chans, 3 * chans), F32)
    for taps, first, count, odd, parity, place in pieces:
        left = taps[first : first + count, :, odd * 3 * chans : (odd + 1) * 3 * chans]
        right = grads[parity, place : place + count]
        total = total + lax.dot_general(
            left.reshape(count * width, 3 * chans),
            right.reshape(count * width, 3 * chans),
            TN,
            preferred_element_type=F32,
        )
    for tap in range(3):
        result[tap * 3 * chans : (tap + 1) * 3 * chans] = total[:, tap * chans : (tap + 1) * chans]


def halve(place, table, keep, send):
    half = keep.shape[0]
    core = place[1] & 1
    keep[...] = table[pl.ds(pl.multiple_of(core * half, 64), half)]
    send[...] = table[pl.ds(pl.multiple_of((1 - core) * half, 64), half)].astype(BF16)


def pick(inner, edge, index):
    rows = inner.shape[0]
    if index < 2:
        return edge[index]
    return inner[index - 2] if index < rows + 2 else edge[index - rows]


def products_kernel(cotangent, grads):
    chans = cotangent.shape[2]
    side = jnp.zeros((EDGE, chans), F32)

    def rows_of(row):
        parts = [side, cotangent[row].astype(F32), side]
        return jnp.concatenate(parts, axis=0).astype(BF16)

    put_products(grads, rows_of)


def decode_kernel(place, act, edge, coarse, grads, grad_proj, merged, keep, send, taps, table):
    rows, _, chans = merged.shape
    grid = [spread_row(coarse[16 * row : 16 * (row + 1)]) for row in range(4)]
    for index in range(rows):
        value = pick(act, edge, index).astype(F32) + grid[row_of(index)]
        factor = inside(place, index, rows)
        value = value if factor is None else value * factor
        merged[index] = value.astype(BF16)
        put_shifted(taps, index >> 1, index & 1, value)
    count = rows // 2
    weight_grads([(taps, 0, count, 0, 0, 0), (taps, 0, count, 1, 1, 0)], grads, table)
    table[9 * chans :] = grad_proj[...]
    halve(place, table, keep, send)


def hidden_kernel(
    place, slope, slope_edge, grad, grad_edge, grad_tokens, grad_qkv, taps, top, bottom,
    result, keep, send, ends, grads, table,
):
    rows, width, chans = result.shape
    for pair, field in enumerate((top, bottom)):
        put_rows(ends, pair, lambda index, field=field: field[index & 1].astype(F32))
    grid = [
        spread_row(grad_tokens[16 * row : 16 * (row + 1)] * (1.0 / (PATCH * PATCH)))
        for row in range(4)
    ]
    for index in range(rows):
        value = pick(grad, grad_edge, index).astype(F32) + grid[row_of(index)]
        value = value * pick(slope, slope_edge, index).astype(F32)
        factor = inside(place, index, rows)
        result[index] = (value if factor is None else value * factor).astype(BF16)
    column = lax.broadcasted_iota(jnp.int32, (width, chans), 0)
    own = (column >= EDGE) & (column < width - EDGE)

    def rows_of(row):
        return jnp.where(own, result[row + 1].astype(F32), 0.0).astype(BF16)

    put_products(grads, rows_of)
    count = taps.shape[0]
    pieces = [
        (taps, 0, count, 0, 1, 0), (taps, 0, count, 1, 0, 1),
        (ends, 0, 1, 1, 0, 0), (ends, 1, 1, 0, 1, count),
    ]
    weight_grads(pieces, grads, table)
    for index in range(3):
        table[(9 + index) * chans : (10 + index) * chans] = grad_qkv[index]
    halve(place, table, keep, send)


def last_kernel(hidden, merged, w_in, w_out, grad_inputs, outputs, taps, packed, taps_2, packed_2):
    put_weight(packed, w_in, True)
    put_weight(packed_2, w_out, False)

    def emit_to(result):
        def emit(pair, both):
            for odd, value in enumerate(halves(both)):
                result[2 * pair + odd] = value[EDGE : EDGE + 128].astype(BF16)

        return emit

    stream_conv(taps, packed, lambda index: hidden[index].astype(F32), emit_to(grad_inputs))
    stream_conv(taps_2, packed_2, lambda index: merged[index].astype(F32), emit_to(outputs))


def cut(tables, starts, start, stop):
    pieces = []
    for index, table in enumerate(tables):
        low, high = max(start, starts[index]), min(stop, starts[index + 1])
        if low < high:
            pieces.append((table, low - starts[index], high - starts[index], low - start))
    return pieces


def row_starts(tables):
    starts = [0]
    for table in tables:
        starts.append(starts[-1] + table.shape[0])
    return starts


def chip_sum_kernel(keep_a, keep_b, got_a, got_b, blocks, sum_a, sum_b):
    sum_a[...] = keep_a[...] + got_a[...].astype(F32)
    sum_b[...] = keep_b[...] + got_b[...].astype(F32)
    tables = (sum_a, sum_b)
    starts = row_starts(tables)
    share = blocks.shape[1]
    for chip in range(CHIPS):
        pieces = cut(tables, starts, chip * share, (chip + 1) * share)
        rows = [table[low:high] for table, low, high, _ in pieces]
        blocks[chip] = (rows[0] if len(rows) == 1 else jnp.concatenate(rows, axis=0)).astype(BF16)


def share_kernel(moved, copies):
    total = moved[0].astype(F32)
    for chip in range(1, CHIPS):
        total = total + moved[chip].astype(F32)
    total = total.astype(BF16)
    for chip in range(CHIPS):
        copies[chip] = total


def unpack_kernel(place, own, other, grad_in, grad_out, grad_qkv, grad_proj):
    share = own.shape[1]
    first_core = (place[1] & 1) == 0
    half_a = (grad_in.shape[0] + grad_qkv.shape[0]) // 2
    half_b = (grad_out.shape[0] + grad_proj.shape[0]) // 2
    for chip in range(CHIPS):
        mine, theirs = own[chip].astype(F32), other[chip].astype(F32)
        cores = (jnp.where(first_core, mine, theirs), jnp.where(first_core, theirs, mine))
        for core, piece in enumerate(cores):
            for half, start, tables in (
                (half_a, 0, (grad_in, grad_qkv)),
                (half_b, half_a, (grad_out, grad_proj)),
            ):
                low = max(chip * share, start)
                high = min((chip + 1) * share, start + half)
                base = core * half - start
                for table, first, last, offset in cut(
                    tables, row_starts(tables), low + base, high + base
                ):
                    offset = offset + low - chip * share
                    table[first:last] = piece[offset : offset + last - first]


def exchange(blocks, axes):
    return lax.all_to_all(blocks, axes, 0, 0, tiled=True)


def body(inputs, cotangent, w_in, w_out, w_qkv, w_proj):
    rows, cols, chans = inputs.shape
    width = cols + 2 * EDGE
    place = jnp.stack([lax.axis_index("lat"), lax.axis_index(LON)]).astype(jnp.int32)
    shape = jax.ShapeDtypeStruct
    whole = pl.BlockSpec(memory_space=pltpu.VMEM)
    scalars = pl.BlockSpec(memory_space=pltpu.SMEM)
    conv_flops = 2 * rows * cols * 9 * chans * chans
    packed = pltpu.VMEM((12 * chans, 2 * chans), BF16)
    grads = pltpu.VMEM((2, rows // 2 + 1, width, 3 * chans), BF16)

    def taps(count):
        return pltpu.VMEM((count // 2, width, 6 * chans), BF16)

    lats, lons = lax.axis_size("lat"), lax.axis_size("chip") * lax.axis_size("core")
    up = [(i, i + 1) for i in range(lats - 1)]
    down = [(i + 1, i) for i in range(lats - 1)]
    east = [(i, (i + 1) % lons) for i in range(lons)]
    west = [((i + 1) % lons, i) for i in range(lons)]

    def two(cut):
        return jnp.concatenate([cut(inputs), cut(cotangent)], axis=0)

    left = lax.ppermute(two(lambda field: field[:, cols - HALO :]), LON, east)
    right = lax.ppermute(two(lambda field: field[:, :HALO]), LON, west)

    def wide_pair(start):
        def cut(side):
            return jnp.concatenate(
                [side[start : start + 2], side[rows + start : rows + start + 2]], axis=0
            )

        own = two(lambda field: field[start : start + 2])
        row = jnp.concatenate([cut(left), own, cut(right)], axis=1)
        return jnp.pad(row, ((0, 0), (EDGE - HALO, EDGE - HALO), (0, 0)))

    first, last = wide_pair(0), wide_pair(rows - 2)
    top = lax.ppermute(last, "lat", up)
    bottom = lax.ppermute(first, "lat", down)
    inner_field = shape((rows - 2, width, chans), BF16)
    edge_field = shape((4, width, chans), BF16)
    field = shape((rows + 2, width, chans), BF16)
    products = call(products_kernel, shape(grads.shape, BF16), flops=2**27)(cotangent)
    act, slope, grad, sums, taps_in = call(
        inner_kernel,
        (
            inner_field,
            inner_field,
            inner_field,
            shape((32, chans), F32),
            shape((rows // 2, width, 6 * chans), BF16),
        ),
        [taps(rows), packed, packed],
        2 * conv_flops,
    )(inputs, cotangent, left, right, w_in, w_out)
    act_edge, slope_edge, grad_edge, copies, grad_coarse = call(
        edge_kernel,
        (
            edge_field,
            edge_field,
            edge_field,
            shape((DEVICES * 16, chans), BF16),
            shape((16, chans), F32),
        ),
        [taps(8), packed],
        conv_flops // 4,
    )(first, last, top, bottom, w_in, w_out, sums)
    copies, products, place = lax.optimization_barrier((copies, products, place))
    tokens_all = exchange(copies, AXES)
    table = shape((DEVICES * 16, chans), BF16)
    coarse, message, grad_w_proj, soft, near, keys, values = call(
        attend_kernel,
        (
            shape((64, chans), F32),
            shape((CHIPS, 18, chans), BF16),
            shape((chans, chans), F32),
            shape((128, 1), F32),
            shape((64, chans), BF16),
            table,
            table,
        ),
        flops=2**28,
        in_specs=[scalars] + [whole] * 4,
    )(place, tokens_all, w_qkv, w_proj, grad_coarse)
    merged, keep_b, send_b = call(
        decode_kernel,
        (field, shape((5 * chans, chans), F32), shape((5 * chans, chans), BF16)),
        [taps(rows + 2), pltpu.VMEM((10 * chans, chans), F32)],
        2 * conv_flops,
        in_specs=[scalars] + [whole] * 5,
    )(place, act, act_edge, coarse, products, grad_w_proj)
    message, send_b = lax.optimization_barrier((message, send_b))
    swap = [(0, 1), (1, 0)]
    own = exchange(message, ("lat", "chip"))
    own, tokens_all = lax.optimization_barrier((own, tokens_all))
    other = lax.ppermute(own, "core", swap)
    wide = shape((128, DEVICES * 16), F32)
    queries, scores, prob, near_values = call(
        prepare_kernel,
        (table, wide, wide, shape((128, chans), BF16)),
        flops=2**28,
    )(tokens_all, near, keys, w_qkv, soft)
    grad_tokens, grad_w_qkv = call(
        attend_back_kernel,
        (shape((64, chans), F32), shape((3, chans, chans), F32)),
        flops=2**28,
        in_specs=[scalars] + [whole] * 12,
    )(
        place, near, keys, values, queries, scores, prob, near_values, own, other, grad_coarse,
        w_qkv, w_proj,
    )
    got_b = lax.ppermute(send_b, "core", swap)
    grad_hidden, keep_a, send_a = call(
        hidden_kernel,
        (field, shape((6 * chans, chans), F32), shape((6 * chans, chans), BF16)),
        [taps(4), grads, pltpu.VMEM((12 * chans, chans), F32)],
        conv_flops,
        in_specs=[scalars] + [whole] * 9,
    )(
        place, slope, slope_edge, grad, grad_edge, grad_tokens, grad_w_qkv, taps_in, top, bottom
    )
    got_a = lax.ppermute(send_a, "core", swap)
    share = 11 * chans // CHIPS
    blocks = call(
        chip_sum_kernel,
        shape((CHIPS, share, chans), BF16),
        [pltpu.VMEM(keep.shape, F32) for keep in (keep_a, keep_b)],
    )(keep_a, keep_b, got_a, got_b)
    partial = exchange(blocks, ("lat", "chip"))
    grad_inputs, outputs = call(
        last_kernel,
        (shape((rows, cols, chans), BF16), shape((rows, cols, chans), BF16)),
        [taps(rows + 2), packed, taps(rows + 2), packed],
        2 * conv_flops,
    )(grad_hidden, merged, w_in, w_out)
    partial, grad_inputs = lax.optimization_barrier((partial, grad_inputs))
    copies = call(share_kernel, shape(blocks.shape, BF16))(partial)
    own = exchange(copies, ("lat", "chip"))
    other = lax.ppermute(own, "core", swap)
    shapes = (w_in.shape, w_out.shape, w_qkv.shape, w_proj.shape)
    pieces = call(
        unpack_kernel,
        tuple(shape((size * chans, chans), F32) for size in (9, 9, 3, 1)),
        in_specs=[scalars, whole, whole],
    )(place, own, other)
    pieces = [piece.reshape(dims) for piece, dims in zip(pieces, shapes)]
    return (outputs, grad_inputs, *pieces)


def solution(mesh):
    lats, lons = mesh.devices.shape
    fine = jax.sharding.Mesh(mesh.devices.reshape(lats, lons // 2, 2), AXES)
    field, whole = P("lat", LON, None), P()
    in_specs = (field, field, whole, whole, whole, whole)
    out_specs = (field, field, whole, whole, whole, whole)
    return jax.shard_map(body, mesh=fine, in_specs=in_specs, out_specs=out_specs, check_vma=False)
```

```python
import jax
import jax.numpy as jnp
from jax import lax
from jax.experimental import pallas as pl
from jax.experimental.pallas import tpu as pltpu
from jax.sharding import PartitionSpec as P

HEADS = 2
HEAD_DIM = 64
PATCH = 16
DEVICES = 128
CHIPS = 64
LON = ("chip", "core")
AXES = ("lat",) + LON
EDGE = 8
HALO = 2
HIGHEST = lax.Precision.HIGHEST
F32 = jnp.float32
BF16 = jnp.bfloat16
NT = (((1,), (1,)), ((), ()))
TN = (((0,), (0,)), ((), ()))


def call(kernel, outs, scratch=(), flops=0, in_specs=None):
    return pl.pallas_call(
        kernel,
        out_shape=outs,
        **({"in_specs": in_specs} if in_specs else {}),
        scratch_shapes=list(scratch),
        compiler_params=pltpu.CompilerParams(vmem_limit_bytes=24 * 2**20),
        cost_estimate=pl.CostEstimate(flops=flops, bytes_accessed=8 * 2**20, transcendentals=0),
    )


def put_shifted(taps, pair, odd, wide):
    width, chans = wide.shape
    base = odd * 3 * chans
    taps[pair, :, base : base + chans] = pltpu.roll(wide, 1, 0).astype(BF16)
    taps[pair, :, base + chans : base + 2 * chans] = wide.astype(BF16)
    taps[pair, :, base + 2 * chans : base + 3 * chans] = pltpu.roll(wide, width - 1, 0).astype(BF16)


def wide_row(field, left, right, index, offset):
    blank = jnp.zeros((EDGE - HALO, field.shape[2]), F32)
    parts = [part.astype(F32) for part in (left[offset + index], field[index], right[offset + index])]
    return jnp.concatenate([blank] + parts + [blank], axis=0)


def own_and_edges(field, left, right, top, bottom, second):
    rows = field.shape[0]

    def row(index):
        if index < 2:
            return top[2 * second + index].astype(F32)
        if index >= rows + 2:
            return bottom[2 * second + index - rows - 2].astype(F32)
        return wide_row(field, left, right, index - 2, second * rows)

    return row


def put_rows(taps, pair, row):
    for odd in range(2):
        put_shifted(taps, pair, odd, row(2 * pair + odd))


def stream_conv(taps, packed, row, emit):
    put_rows(taps, 0, row)
    for pair in range(taps.shape[0] - 1):
        put_rows(taps, pair + 1, row)
        emit(pair, pair_conv(taps, pair, packed))


def put_weight(packed, weight, inward):
    chans = weight.shape[2]
    none = jnp.zeros((chans, chans), BF16)
    for col in range(3):
        blocks = []
        for row in range(3):
            if inward:
                blocks.append(weight[2 - row, 2 - col].astype(F32).T.astype(BF16))
            else:
                blocks.append(weight[row, col])
        for source in range(4):
            for target in range(2):
                row = source - target
                block = blocks[row] if 0 <= row < 3 else none
                start = (source * 3 + col) * chans
                packed[start : start + chans, target * chans : (target + 1) * chans] = block


def pair_conv(taps, pair, weight):
    half = weight.shape[0] // 2
    low = jnp.dot(taps[pair], weight[:half], preferred_element_type=F32)
    return low + jnp.dot(taps[pair + 1], weight[half:], preferred_element_type=F32)


def spread_row(grid_row):
    chans = grid_row.shape[1]
    parts = [jnp.broadcast_to(grid_row[15:16], (EDGE, chans))]
    for col in range(8):
        parts.append(jnp.broadcast_to(grid_row[col : col + 1], (PATCH, chans)))
    parts.append(jnp.broadcast_to(grid_row[8:9], (EDGE, chans)))
    return jnp.concatenate(parts, axis=0)


def column_sums(total):
    inner = total[EDGE : EDGE + 8 * PATCH]
    return jnp.sum(inner.reshape(8, PATCH, -1), axis=1)


def activate(hidden):
    sigma = jax.nn.sigmoid(hidden)
    act = (hidden * sigma).astype(BF16)
    return act, (sigma * (1.0 + hidden * (1.0 - sigma))).astype(BF16)


def token_sums(rows):
    totals = [None, None]
    for index, row in rows:
        half, value = index // PATCH, row.astype(F32)
        totals[half] = value if totals[half] is None else totals[half] + value
    return jnp.concatenate([column_sums(total) for total in totals], axis=0)


def halves(both):
    chans = both.shape[1] // 2
    return [both[:, :chans], both[:, chans:]]


def inner_kernel(
    inputs, cotangent, left, right, w_in, w_out, act, slope, grad, sums, taps,
    taps_back, packed, packed_back,
):
    rows = inputs.shape[0]
    put_weight(packed, w_in, False)
    put_weight(packed_back, w_out, True)
    acts, grads = [], []

    def emit_act(pair, both):
        for odd, hidden in enumerate(halves(both)):
            index = 2 * pair + odd
            act[index], slope[index] = activate(hidden)
            acts.append((index + 1, act[index]))

    def emit_grad(pair, both):
        for odd, value in enumerate(halves(both)):
            grad[2 * pair + odd] = value.astype(BF16)
            grads.append((2 * pair + odd + 1, value))

    stream_conv(taps, packed, lambda index: wide_row(inputs, left, right, index, 0), emit_act)
    sums[:16] = token_sums(acts)
    stream_conv(
        taps_back, packed_back, lambda index: wide_row(cotangent, left, right, index, rows), emit_grad
    )
    sums[16:] = token_sums(grads)


def edge_kernel(
    first, last, top, bottom, w_in, w_out, sums, act, slope, grad, copies, coarse, taps, packed
):
    fields = (top, first, last, bottom)

    def convolve(weight, second, emit):
        put_weight(packed, weight, second)
        for pair, field in enumerate(fields):
            put_rows(taps, pair, lambda index, field=field: field[2 * second + (index & 1)].astype(F32))
        for side in range(2):
            for odd, value in enumerate(halves(pair_conv(taps, 2 * side, packed))):
                emit(2 * side + odd, value)

    def emit_act(index, hidden):
        act[index], slope[index] = activate(hidden)

    convolve(w_in, 0, emit_act)
    total = sums[:16] + token_sums([(0, act[1]), (31, act[2])])
    tokens = (total / (PATCH * PATCH)).astype(BF16)
    for chip in range(CHIPS):
        copies[16 * chip : 16 * (chip + 1)] = tokens
    values = []

    def emit_grad(index, value):
        grad[index] = value.astype(BF16)
        values.append(value)

    convolve(w_out, 1, emit_grad)
    coarse[...] = sums[16:] + token_sums([(0, values[1]), (31, values[2])])


def near_index(place, shape, dim):
    entry = lax.broadcasted_iota(jnp.int32, shape, dim)
    row = 2 * place[0] + (((entry >> 4) + 1) & 3) - 1
    row = jnp.clip(row, 0, 15)
    col = (8 * place[1] + (((entry & 15) + 4) & 15) - 4) & 127
    device = (row >> 1) * 16 + (col >> 3)
    return device * 16 + (row & 1) * 8 + (col & 7)


def pick_near(place, table):
    count = table.shape[0]
    index = near_index(place, (64, count), 0)
    lane = lax.broadcasted_iota(jnp.int32, (64, count), 1)
    chosen = jnp.where(index == lane, 1.0, 0.0).astype(BF16)
    return jnp.dot(chosen, table, preferred_element_type=F32).astype(BF16)


def by_head(rows):
    lane = lax.broadcasted_iota(jnp.int32, rows.shape, 1)
    wide = rows.astype(F32)
    first = jnp.where(lane < HEAD_DIM, wide, 0.0)
    second = jnp.where(lane < HEAD_DIM, 0.0, wide)
    return jnp.concatenate([first, second], axis=0).astype(BF16)


def join_heads(rows):
    half = rows.shape[0] // 2
    lane = lax.broadcasted_iota(jnp.int32, (half, rows.shape[1]), 1)
    return jnp.where(lane < HEAD_DIM, rows[:half], rows[half:])


def low_dot(a, b):
    return jnp.dot(a, b, preferred_element_type=F32).astype(BF16)


def own_rows(near):
    return jnp.concatenate([near[0:8], near[16:24]], axis=0)


def split_three(value):
    high = value.astype(BF16)
    rest = value - high.astype(F32)
    mid = rest.astype(BF16)
    return high, mid, (rest - mid.astype(F32)).astype(BF16)


def in_order(place, own, other):
    first_core = (place[1] & 1) == 0
    mine, theirs = own.astype(F32), other.astype(F32)
    return jnp.where(first_core, mine, theirs), jnp.where(first_core, theirs, mine)


def attend_kernel(
    place, own, other, w_qkv, w_proj, grad_coarse,
    coarse, message, grad_proj, soft, near, keys, values, tokens,
):
    scale = HEAD_DIM**-0.5
    chans = own.shape[1]
    cores = in_order(place, *(half[...].reshape(CHIPS, 16, chans) for half in (own, other)))
    tokens[...] = jnp.stack(cores, axis=1).reshape(-1, chans).astype(BF16)
    near[...] = pick_near(place, tokens[...])
    keys[...] = low_dot(tokens[...], w_qkv[1])
    values[...] = low_dot(tokens[...], w_qkv[2])
    queries = by_head(low_dot(near[...], w_qkv[0]))
    scores = lax.dot_general(queries, keys[...], NT, preferred_element_type=F32) * scale
    top = jnp.max(scores, axis=1, keepdims=True)
    weights = jnp.exp(scores - top)
    total = jnp.sum(weights, axis=1, keepdims=True)
    prob = (weights / total).astype(BF16)
    mixed_wide = join_heads(jnp.dot(prob, values[...], preferred_element_type=F32))
    mixed = mixed_wide.astype(BF16)
    coarse[...] = near[...].astype(F32) + jnp.dot(
        mixed, w_proj[...], preferred_element_type=F32
    )
    log_sum = top + jnp.log(total)
    soft[...] = log_sum
    coarse_low = grad_coarse[...].astype(BF16)
    grad_proj[...] = lax.dot_general(
        own_rows(mixed), coarse_low, TN, preferred_element_type=F32
    )
    grad_mixed = lax.dot_general(coarse_low, w_proj[...], NT, preferred_element_type=F32)
    product = grad_mixed.astype(BF16).astype(F32) * own_rows(mixed_wide)
    lane = lax.broadcasted_iota(jnp.int32, product.shape, 1)
    inner = [
        jnp.sum(jnp.where(lane < HEAD_DIM, product, 0.0), axis=1, keepdims=True),
        jnp.sum(jnp.where(lane < HEAD_DIM, 0.0, product), axis=1, keepdims=True),
    ]
    logs = [own_rows(log_sum[:64]), own_rows(log_sum[64:])]
    token = lax.broadcasted_iota(jnp.int32, product.shape, 0)
    rows = []
    for pair in (logs, inner):
        row = jnp.zeros((1, 128), F32)
        for head in range(HEADS):
            for part, value in enumerate(split_three(pair[head])):
                slot = (head * 3 + part) * 16
                at = jnp.where(lane == token + slot, value.astype(F32), 0.0)
                row = row + jnp.sum(at, axis=0, keepdims=True)
        rows.append(row)
    text = jnp.concatenate([coarse_low.astype(F32)] + rows, axis=0).astype(BF16)
    for chip in range(CHIPS):
        message[chip] = text


def lane_stats(tables):
    count = DEVICES * 16
    part = lax.broadcasted_iota(jnp.int32, (DEVICES, 128), 1) >> 4
    rows = []
    for table in tables:
        wide = table.astype(F32)
        for head in range(HEADS):
            mine = (part >= 3 * head) & (part < 3 * head + 3)
            rows.append(jnp.where(mine, wide, 0.0).astype(BF16))
    slot = lax.broadcasted_iota(jnp.int32, (128, count), 0)
    lane = lax.broadcasted_iota(jnp.int32, (128, count), 1)
    chosen = jnp.where((slot & 15) == (lane & 15), 1.0, 0.0).astype(BF16)
    tiled = jnp.dot(jnp.concatenate(rows, axis=0), chosen, preferred_element_type=F32)
    entry = lax.broadcasted_iota(jnp.int32, (DEVICES, count), 0)
    device = ((entry & (CHIPS - 1)) << 1) + (entry >> 6)
    mine = device == (lax.broadcasted_iota(jnp.int32, (DEVICES, count), 1) >> 4)
    sums = []
    for index in range(len(rows)):
        block = tiled[index * DEVICES : (index + 1) * DEVICES]
        sums.append(jnp.sum(jnp.where(mine, block, 0.0), axis=0, keepdims=True))
    return sums


def prepare_kernel(tokens, near, keys, w_qkv, soft, queries, scores, prob, near_values):
    scale = HEAD_DIM**-0.5
    queries[...] = low_dot(tokens[...], w_qkv[0])
    near_q = by_head(low_dot(near[...], w_qkv[0]))
    near_k = by_head(low_dot(near[...], w_qkv[1]))
    near_values[...] = by_head(low_dot(near[...], w_qkv[2]))
    outward = lax.dot_general(near_q, keys[...], NT, preferred_element_type=F32) * scale
    prob[...] = jnp.exp(outward - soft[...])
    scores[...] = lax.dot_general(near_k, queries[...], NT, preferred_element_type=F32) * scale


def attend_back_kernel(
    place, near, keys, values, queries, scores, prob_out, near_values, own, other, grad_coarse,
    w_qkv, w_proj, grad_tokens, grad_qkv,
):
    scale = HEAD_DIM**-0.5
    chans = own.shape[2]
    cores = in_order(place, own[:, :16, :], other[:, :16, :])
    coarse_low = jnp.stack(cores, axis=1).reshape(-1, chans).astype(BF16)
    count = coarse_low.shape[0]
    logs, inner = (
        jnp.concatenate(in_order(place, own[:, row, :], other[:, row, :]), axis=0).astype(BF16)
        for row in (16, 17)
    )
    near_low = pick_near(place, coarse_low)
    mixed = lax.dot_general(coarse_low, w_proj[...], NT, preferred_element_type=F32).astype(BF16)
    near_mixed = lax.dot_general(
        near_low, w_proj[...], NT, preferred_element_type=F32
    ).astype(BF16)
    grad_prob = lax.dot_general(by_head(near_mixed), values[...], NT, preferred_element_type=F32)
    prob = prob_out[...]
    mean = jnp.sum(prob * grad_prob, axis=1, keepdims=True)
    grad_score = (prob * (grad_prob - mean) * scale).astype(BF16)
    grad_q = join_heads(jnp.dot(grad_score, keys[...], preferred_element_type=F32))

    stats = lane_stats((logs, inner))

    def both_heads(first, second):
        spread = [jnp.broadcast_to(row, (64, count)) for row in (first, second)]
        return jnp.concatenate(spread, axis=0)

    prob = jnp.exp(scores[...] - both_heads(*stats[:2]))
    grad_prob = lax.dot_general(near_values[...], mixed, NT, preferred_element_type=F32)
    grad_score = (prob * (grad_prob - both_heads(*stats[2:])) * scale).astype(BF16)
    grad_k = join_heads(jnp.dot(grad_score, queries[...], preferred_element_type=F32))
    grad_v = join_heads(jnp.dot(prob.astype(BF16), mixed, preferred_element_type=F32))
    nearest = jnp.concatenate(
        [grad_coarse[0:8], near_low[8:16].astype(F32), grad_coarse[8:16]], axis=0
    )
    result = jnp.concatenate([nearest, near_low[24:].astype(F32)], axis=0)
    grads = jnp.concatenate([grad_q, grad_k, grad_v], axis=1)
    wide = jnp.concatenate([w_qkv[index].astype(F32) for index in range(3)], axis=1)
    result = result + lax.dot_general(
        grads, wide, NT, precision=HIGHEST, preferred_element_type=F32
    )
    own_tokens = own_rows(near[...].astype(F32))
    products = lax.dot_general(
        own_tokens, own_rows(grads), TN, precision=HIGHEST, preferred_element_type=F32
    )
    for index in range(3):
        grad_qkv[index] = products[:, index * chans : (index + 1) * chans]
    grad_tokens[...] = result


def row_of(index):
    if index == 0:
        return 3
    return min((index - 1) // PATCH, 2)


def inside(place, index, rows):
    if index == 0:
        return jnp.where(place[0] == 0, 0.0, 1.0)
    if index == rows - 1:
        return jnp.where(place[0] == 7, 0.0, 1.0)
    return None


def put_products(grads, rows_of):
    chans = grads.shape[3] // 3
    rows = 2 * grads.shape[1] - 2
    zero = jnp.zeros((grads.shape[2], chans), BF16)
    for row in range(-1, rows + 3):
        kept = rows_of(row - 1) if 0 < row < rows + 1 else zero
        for tap in range(3):
            target = row - 1 + tap
            if 0 <= target < rows + 2:
                odd, place = target & 1, target >> 1
                grads[odd, place, :, tap * chans : (tap + 1) * chans] = kept


def weight_grads(pieces, grads, result):
    chans = result.shape[1]
    width = grads.shape[2]
    total = jnp.zeros((3 * chans, 3 * chans), F32)
    for taps, first, count, odd, parity, place in pieces:
        left = taps[first : first + count, :, odd * 3 * chans : (odd + 1) * 3 * chans]
        right = grads[parity, place : place + count]
        total = total + lax.dot_general(
            left.reshape(count * width, 3 * chans),
            right.reshape(count * width, 3 * chans),
            TN,
            preferred_element_type=F32,
        )
    for tap in range(3):
        result[tap * 3 * chans : (tap + 1) * 3 * chans] = total[:, tap * chans : (tap + 1) * chans]


def halve(place, table, keep, send):
    half = keep.shape[0]
    core = place[1] & 1
    keep[...] = table[pl.ds(pl.multiple_of(core * half, 64), half)]
    send[...] = table[pl.ds(pl.multiple_of((1 - core) * half, 64), half)].astype(BF16)


def pick(inner, edge, index):
    rows = inner.shape[0]
    if index < 2:
        return edge[index]
    return inner[index - 2] if index < rows + 2 else edge[index - rows]


def products_kernel(cotangent, grads):
    chans = cotangent.shape[2]
    side = jnp.zeros((EDGE, chans), F32)

    def rows_of(row):
        parts = [side, cotangent[row].astype(F32), side]
        return jnp.concatenate(parts, axis=0).astype(BF16)

    put_products(grads, rows_of)


def decode_kernel(place, act, edge, coarse, grads, grad_proj, merged, keep, send, taps, table):
    rows, _, chans = merged.shape
    grid = [spread_row(coarse[16 * row : 16 * (row + 1)]) for row in range(4)]
    for index in range(rows):
        value = pick(act, edge, index).astype(F32) + grid[row_of(index)]
        factor = inside(place, index, rows)
        value = value if factor is None else value * factor
        merged[index] = value.astype(BF16)
        put_shifted(taps, index >> 1, index & 1, value)
    count = rows // 2
    weight_grads([(taps, 0, count, 0, 0, 0), (taps, 0, count, 1, 1, 0)], grads, table)
    table[9 * chans :] = grad_proj[...]
    halve(place, table, keep, send)


def hidden_kernel(
    place, slope, slope_edge, grad, grad_edge, grad_tokens, grad_qkv, taps, top, bottom,
    result, keep, send, ends, grads, table,
):
    rows, width, chans = result.shape
    for pair, field in enumerate((top, bottom)):
        put_rows(ends, pair, lambda index, field=field: field[index & 1].astype(F32))
    grid = [
        spread_row(grad_tokens[16 * row : 16 * (row + 1)] * (1.0 / (PATCH * PATCH)))
        for row in range(4)
    ]
    for index in range(rows):
        value = pick(grad, grad_edge, index).astype(F32) + grid[row_of(index)]
        value = value * pick(slope, slope_edge, index).astype(F32)
        factor = inside(place, index, rows)
        result[index] = (value if factor is None else value * factor).astype(BF16)
    column = lax.broadcasted_iota(jnp.int32, (width, chans), 0)
    own = (column >= EDGE) & (column < width - EDGE)

    def rows_of(row):
        return jnp.where(own, result[row + 1].astype(F32), 0.0).astype(BF16)

    put_products(grads, rows_of)
    count = taps.shape[0]
    pieces = [
        (taps, 0, count, 0, 1, 0), (taps, 0, count, 1, 0, 1),
        (ends, 0, 1, 1, 0, 0), (ends, 1, 1, 0, 1, count),
    ]
    weight_grads(pieces, grads, table)
    for index in range(3):
        table[(9 + index) * chans : (10 + index) * chans] = grad_qkv[index]
    halve(place, table, keep, send)


def last_kernel(hidden, merged, w_in, w_out, grad_inputs, outputs, taps, packed, taps_2, packed_2):
    put_weight(packed, w_in, True)
    put_weight(packed_2, w_out, False)

    def emit_to(result):
        def emit(pair, both):
            for odd, value in enumerate(halves(both)):
                result[2 * pair + odd] = value[EDGE : EDGE + 128].astype(BF16)

        return emit

    stream_conv(taps, packed, lambda index: hidden[index].astype(F32), emit_to(grad_inputs))
    stream_conv(taps_2, packed_2, lambda index: merged[index].astype(F32), emit_to(outputs))


def cut(tables, starts, start, stop):
    pieces = []
    for index, table in enumerate(tables):
        low, high = max(start, starts[index]), min(stop, starts[index + 1])
        if low < high:
            pieces.append((table, low - starts[index], high - starts[index], low - start))
    return pieces


def row_starts(tables):
    starts = [0]
    for table in tables:
        starts.append(starts[-1] + table.shape[0])
    return starts


def chip_sum_kernel(keep_a, keep_b, got_a, got_b, blocks, sum_a, sum_b):
    sum_a[...] = keep_a[...] + got_a[...].astype(F32)
    sum_b[...] = keep_b[...] + got_b[...].astype(F32)
    tables = (sum_a, sum_b)
    starts = row_starts(tables)
    share = blocks.shape[1]
    for chip in range(CHIPS):
        pieces = cut(tables, starts, chip * share, (chip + 1) * share)
        rows = [table[low:high] for table, low, high, _ in pieces]
        blocks[chip] = (rows[0] if len(rows) == 1 else jnp.concatenate(rows, axis=0)).astype(BF16)


def share_kernel(moved, copies):
    total = moved[0].astype(F32)
    for chip in range(1, CHIPS):
        total = total + moved[chip].astype(F32)
    total = total.astype(BF16)
    for chip in range(CHIPS):
        copies[chip] = total


def unpack_kernel(place, own, other, grad_in, grad_out, grad_qkv, grad_proj):
    share = own.shape[1]
    first_core = (place[1] & 1) == 0
    half_a = (grad_in.shape[0] + grad_qkv.shape[0]) // 2
    half_b = (grad_out.shape[0] + grad_proj.shape[0]) // 2
    for chip in range(CHIPS):
        mine, theirs = own[chip].astype(F32), other[chip].astype(F32)
        cores = (jnp.where(first_core, mine, theirs), jnp.where(first_core, theirs, mine))
        for core, piece in enumerate(cores):
            for half, start, tables in (
                (half_a, 0, (grad_in, grad_qkv)),
                (half_b, half_a, (grad_out, grad_proj)),
            ):
                low = max(chip * share, start)
                high = min((chip + 1) * share, start + half)
                base = core * half - start
                for table, first, last, offset in cut(
                    tables, row_starts(tables), low + base, high + base
                ):
                    offset = offset + low - chip * share
                    table[first:last] = piece[offset : offset + last - first]


def exchange(blocks, axes):
    return lax.all_to_all(blocks, axes, 0, 0, tiled=True)


def body(inputs, cotangent, w_in, w_out, w_qkv, w_proj):
    rows, cols, chans = inputs.shape
    width = cols + 2 * EDGE
    place = jnp.stack([lax.axis_index("lat"), lax.axis_index(LON)]).astype(jnp.int32)
    shape = jax.ShapeDtypeStruct
    whole = pl.BlockSpec(memory_space=pltpu.VMEM)
    scalars = pl.BlockSpec(memory_space=pltpu.SMEM)
    conv_flops = 2 * rows * cols * 9 * chans * chans
    packed = pltpu.VMEM((12 * chans, 2 * chans), BF16)
    grads = pltpu.VMEM((2, rows // 2 + 1, width, 3 * chans), BF16)

    def taps(count):
        return pltpu.VMEM((count // 2, width, 6 * chans), BF16)

    lats, lons = lax.axis_size("lat"), lax.axis_size("chip") * lax.axis_size("core")
    up = [(i, i + 1) for i in range(lats - 1)]
    down = [(i + 1, i) for i in range(lats - 1)]
    east = [(i, (i + 1) % lons) for i in range(lons)]
    west = [((i + 1) % lons, i) for i in range(lons)]

    def two(cut):
        return jnp.concatenate([cut(inputs), cut(cotangent)], axis=0)

    left = lax.ppermute(two(lambda field: field[:, cols - HALO :]), LON, east)
    right = lax.ppermute(two(lambda field: field[:, :HALO]), LON, west)

    def wide_pair(start):
        def cut(side):
            return jnp.concatenate(
                [side[start : start + 2], side[rows + start : rows + start + 2]], axis=0
            )

        own = two(lambda field: field[start : start + 2])
        row = jnp.concatenate([cut(left), own, cut(right)], axis=1)
        return jnp.pad(row, ((0, 0), (EDGE - HALO, EDGE - HALO), (0, 0)))

    first, last = wide_pair(0), wide_pair(rows - 2)
    top = lax.ppermute(last, "lat", up)
    bottom = lax.ppermute(first, "lat", down)
    inner_field = shape((rows - 2, width, chans), BF16)
    edge_field = shape((4, width, chans), BF16)
    field = shape((rows + 2, width, chans), BF16)
    products = call(products_kernel, shape(grads.shape, BF16), flops=2**27)(cotangent)
    act, slope, grad, sums, taps_in = call(
        inner_kernel,
        (
            inner_field,
            inner_field,
            inner_field,
            shape((32, chans), F32),
            shape((rows // 2, width, 6 * chans), BF16),
        ),
        [taps(rows), packed, packed],
        2 * conv_flops,
    )(inputs, cotangent, left, right, w_in, w_out)
    act_edge, slope_edge, grad_edge, copies, grad_coarse = call(
        edge_kernel,
        (
            edge_field,
            edge_field,
            edge_field,
            shape((CHIPS * 16, chans), BF16),
            shape((16, chans), F32),
        ),
        [taps(8), packed],
        conv_flops // 4,
    )(first, last, top, bottom, w_in, w_out, sums)
    copies, products, place = lax.optimization_barrier((copies, products, place))
    swap = [(0, 1), (1, 0)]
    tokens_own = exchange(copies, ("lat", "chip"))
    tokens_other = lax.ppermute(tokens_own, "core", swap)
    table = shape((DEVICES * 16, chans), BF16)
    coarse, message, grad_w_proj, soft, near, keys, values, tokens_all = call(
        attend_kernel,
        (
            shape((64, chans), F32),
            shape((CHIPS, 18, chans), BF16),
            shape((chans, chans), F32),
            shape((128, 1), F32),
            shape((64, chans), BF16),
            table,
            table,
            table,
        ),
        flops=2**28,
        in_specs=[scalars] + [whole] * 5,
    )(place, tokens_own, tokens_other, w_qkv, w_proj, grad_coarse)
    merged, keep_b, send_b = call(
        decode_kernel,
        (field, shape((5 * chans, chans), F32), shape((5 * chans, chans), BF16)),
        [taps(rows + 2), pltpu.VMEM((10 * chans, chans), F32)],
        2 * conv_flops,
        in_specs=[scalars] + [whole] * 5,
    )(place, act, act_edge, coarse, products, grad_w_proj)
    message, send_b = lax.optimization_barrier((message, send_b))
    own = exchange(message, ("lat", "chip"))
    own, tokens_all = lax.optimization_barrier((own, tokens_all))
    other = lax.ppermute(own, "core", swap)
    wide = shape((128, DEVICES * 16), F32)
    queries, scores, prob, near_values = call(
        prepare_kernel,
        (table, wide, wide, shape((128, chans), BF16)),
        flops=2**28,
    )(tokens_all, near, keys, w_qkv, soft)
    grad_tokens, grad_w_qkv = call(
        attend_back_kernel,
        (shape((64, chans), F32), shape((3, chans, chans), F32)),
        flops=2**28,
        in_specs=[scalars] + [whole] * 12,
    )(
        place, near, keys, values, queries, scores, prob, near_values, own, other, grad_coarse,
        w_qkv, w_proj,
    )
    got_b = lax.ppermute(send_b, "core", swap)
    grad_hidden, keep_a, send_a = call(
        hidden_kernel,
        (field, shape((6 * chans, chans), F32), shape((6 * chans, chans), BF16)),
        [taps(4), grads, pltpu.VMEM((12 * chans, chans), F32)],
        conv_flops,
        in_specs=[scalars] + [whole] * 9,
    )(
        place, slope, slope_edge, grad, grad_edge, grad_tokens, grad_w_qkv, taps_in, top, bottom
    )
    got_a = lax.ppermute(send_a, "core", swap)
    share = 11 * chans // CHIPS
    blocks = call(
        chip_sum_kernel,
        shape((CHIPS, share, chans), BF16),
        [pltpu.VMEM(keep.shape, F32) for keep in (keep_a, keep_b)],
    )(keep_a, keep_b, got_a, got_b)
    partial = exchange(blocks, ("lat", "chip"))
    grad_inputs, outputs = call(
        last_kernel,
        (shape((rows, cols, chans), BF16), shape((rows, cols, chans), BF16)),
        [taps(rows + 2), packed, taps(rows + 2), packed],
        2 * conv_flops,
    )(grad_hidden, merged, w_in, w_out)
    partial, grad_inputs = lax.optimization_barrier((partial, grad_inputs))
    copies = call(share_kernel, shape(blocks.shape, BF16))(partial)
    own = exchange(copies, ("lat", "chip"))
    other = lax.ppermute(own, "core", swap)
    shapes = (w_in.shape, w_out.shape, w_qkv.shape, w_proj.shape)
    pieces = call(
        unpack_kernel,
        tuple(shape((size * chans, chans), F32) for size in (9, 9, 3, 1)),
        in_specs=[scalars, whole, whole],
    )(place, own, other)
    pieces = [piece.reshape(dims) for piece, dims in zip(pieces, shapes)]
    return (outputs, grad_inputs, *pieces)


def solution(mesh):
    lats, lons = mesh.devices.shape
    fine = jax.sharding.Mesh(mesh.devices.reshape(lats, lons // 2, 2), AXES)
    field, whole = P("lat", LON, None), P()
    in_specs = (field, field, whole, whole, whole, whole)
    out_specs = (field, field, whole, whole, whole, whole)
    return jax.shard_map(body, mesh=fine, in_specs=in_specs, out_specs=out_specs, check_vma=False)
```

```python
import jax
import jax.numpy as jnp
from jax import lax
from jax.experimental import pallas as pl
from jax.experimental.pallas import tpu as pltpu
from jax.sharding import PartitionSpec as P

HEADS = 2
HEAD_DIM = 64
PATCH = 16
DEVICES = 128
CHIPS = 64
LON = ("chip", "core")
AXES = ("lat",) + LON
EDGE = 8
HALO = 2
HIGHEST = lax.Precision.HIGHEST
F32 = jnp.float32
BF16 = jnp.bfloat16
NT = (((1,), (1,)), ((), ()))
TN = (((0,), (0,)), ((), ()))


def call(kernel, outs, scratch=(), flops=0, in_specs=None):
    return pl.pallas_call(
        kernel,
        out_shape=outs,
        **({"in_specs": in_specs} if in_specs else {}),
        scratch_shapes=list(scratch),
        compiler_params=pltpu.CompilerParams(vmem_limit_bytes=24 * 2**20),
        cost_estimate=pl.CostEstimate(flops=flops, bytes_accessed=8 * 2**20, transcendentals=0),
    )


def put_shifted(taps, pair, odd, wide):
    width, chans = wide.shape
    base = odd * 3 * chans
    taps[pair, :, base : base + chans] = pltpu.roll(wide, 1, 0).astype(BF16)
    taps[pair, :, base + chans : base + 2 * chans] = wide.astype(BF16)
    taps[pair, :, base + 2 * chans : base + 3 * chans] = pltpu.roll(wide, width - 1, 0).astype(BF16)


def wide_row(field, left, right, index, offset):
    blank = jnp.zeros((EDGE - HALO, field.shape[2]), F32)
    parts = [part.astype(F32) for part in (left[offset + index], field[index], right[offset + index])]
    return jnp.concatenate([blank] + parts + [blank], axis=0)


def own_and_edges(field, left, right, top, bottom, second):
    rows = field.shape[0]

    def row(index):
        if index < 2:
            return top[2 * second + index].astype(F32)
        if index >= rows + 2:
            return bottom[2 * second + index - rows - 2].astype(F32)
        return wide_row(field, left, right, index - 2, second * rows)

    return row


def put_rows(taps, pair, row):
    for odd in range(2):
        put_shifted(taps, pair, odd, row(2 * pair + odd))


def stream_conv(taps, packed, row, emit):
    put_rows(taps, 0, row)
    for pair in range(taps.shape[0] - 1):
        put_rows(taps, pair + 1, row)
        emit(pair, pair_conv(taps, pair, packed))


def put_weight(packed, weight, inward):
    chans = weight.shape[2]
    none = jnp.zeros((chans, chans), BF16)
    for col in range(3):
        blocks = []
        for row in range(3):
            if inward:
                blocks.append(weight[2 - row, 2 - col].astype(F32).T.astype(BF16))
            else:
                blocks.append(weight[row, col])
        for source in range(4):
            for target in range(2):
                row = source - target
                block = blocks[row] if 0 <= row < 3 else none
                start = (source * 3 + col) * chans
                packed[start : start + chans, target * chans : (target + 1) * chans] = block


def pair_conv(taps, pair, weight):
    half = weight.shape[0] // 2
    low = jnp.dot(taps[pair], weight[:half], preferred_element_type=F32)
    return low + jnp.dot(taps[pair + 1], weight[half:], preferred_element_type=F32)


def spread_row(grid_row):
    chans = grid_row.shape[1]
    parts = [jnp.broadcast_to(grid_row[15:16], (EDGE, chans))]
    for col in range(8):
        parts.append(jnp.broadcast_to(grid_row[col : col + 1], (PATCH, chans)))
    parts.append(jnp.broadcast_to(grid_row[8:9], (EDGE, chans)))
    return jnp.concatenate(parts, axis=0)


def column_sums(total):
    inner = total[EDGE : EDGE + 8 * PATCH]
    return jnp.sum(inner.reshape(8, PATCH, -1), axis=1)


def activate(hidden):
    sigma = jax.nn.sigmoid(hidden)
    act = (hidden * sigma).astype(BF16)
    return act, (sigma * (1.0 + hidden * (1.0 - sigma))).astype(BF16)


def token_sums(rows):
    totals = [None, None]
    for index, row in rows:
        half, value = index // PATCH, row.astype(F32)
        totals[half] = value if totals[half] is None else totals[half] + value
    return jnp.concatenate([column_sums(total) for total in totals], axis=0)


def halves(both):
    chans = both.shape[1] // 2
    return [both[:, :chans], both[:, chans:]]


def inner_kernel(
    inputs, cotangent, left, right, w_in, w_out, act, slope, grad, sums, taps,
    taps_back, packed, packed_back,
):
    rows = inputs.shape[0]
    put_weight(packed, w_in, False)
    put_weight(packed_back, w_out, True)
    acts, grads = [], []

    def emit_act(pair, both):
        for odd, hidden in enumerate(halves(both)):
            index = 2 * pair + odd
            act[index], slope[index] = activate(hidden)
            acts.append((index + 1, act[index]))

    def emit_grad(pair, both):
        for odd, value in enumerate(halves(both)):
            grad[2 * pair + odd] = value.astype(BF16)
            grads.append((2 * pair + odd + 1, value))

    stream_conv(taps, packed, lambda index: wide_row(inputs, left, right, index, 0), emit_act)
    sums[:16] = token_sums(acts)
    stream_conv(
        taps_back, packed_back, lambda index: wide_row(cotangent, left, right, index, rows), emit_grad
    )
    sums[16:] = token_sums(grads)


def edge_kernel(
    first, last, top, bottom, w_in, w_out, sums, act, slope, grad, copies, coarse, taps, packed
):
    fields = (top, first, last, bottom)

    def convolve(weight, second, emit):
        put_weight(packed, weight, second)
        for pair, field in enumerate(fields):
            put_rows(taps, pair, lambda index, field=field: field[2 * second + (index & 1)].astype(F32))
        for side in range(2):
            for odd, value in enumerate(halves(pair_conv(taps, 2 * side, packed))):
                emit(2 * side + odd, value)

    def emit_act(index, hidden):
        act[index], slope[index] = activate(hidden)

    convolve(w_in, 0, emit_act)
    total = sums[:16] + token_sums([(0, act[1]), (31, act[2])])
    tokens = (total / (PATCH * PATCH)).astype(BF16)
    for device in range(DEVICES):
        copies[16 * device : 16 * (device + 1)] = tokens
    values = []

    def emit_grad(index, value):
        grad[index] = value.astype(BF16)
        values.append(value)

    convolve(w_out, 1, emit_grad)
    coarse[...] = sums[16:] + token_sums([(0, values[1]), (31, values[2])])


def near_index(place, shape, dim):
    entry = lax.broadcasted_iota(jnp.int32, shape, dim)
    row = 2 * place[0] + (((entry >> 4) + 1) & 3) - 1
    row = jnp.clip(row, 0, 15)
    col = (8 * place[1] + (((entry & 15) + 4) & 15) - 4) & 127
    device = (row >> 1) * 16 + (col >> 3)
    return device * 16 + (row & 1) * 8 + (col & 7)


def pick_near(place, table):
    count = table.shape[0]
    index = near_index(place, (64, count), 0)
    lane = lax.broadcasted_iota(jnp.int32, (64, count), 1)
    chosen = jnp.where(index == lane, 1.0, 0.0).astype(BF16)
    return jnp.dot(chosen, table, preferred_element_type=F32).astype(BF16)


def by_head(rows):
    lane = lax.broadcasted_iota(jnp.int32, rows.shape, 1)
    wide = rows.astype(F32)
    first = jnp.where(lane < HEAD_DIM, wide, 0.0)
    second = jnp.where(lane < HEAD_DIM, 0.0, wide)
    return jnp.concatenate([first, second], axis=0).astype(BF16)


def join_heads(rows):
    half = rows.shape[0] // 2
    lane = lax.broadcasted_iota(jnp.int32, (half, rows.shape[1]), 1)
    return jnp.where(lane < HEAD_DIM, rows[:half], rows[half:])


def low_dot(a, b):
    return jnp.dot(a, b, preferred_element_type=F32).astype(BF16)


def own_rows(near):
    return jnp.concatenate([near[0:8], near[16:24]], axis=0)


def split_three(value):
    high = value.astype(BF16)
    rest = value - high.astype(F32)
    mid = rest.astype(BF16)
    return high, mid, (rest - mid.astype(F32)).astype(BF16)


def attend_kernel(
    place, tokens, w_qkv, w_proj, grad_coarse, coarse, message, grad_proj, soft, near, keys, values
):
    scale = HEAD_DIM**-0.5
    near[...] = pick_near(place, tokens[...])
    keys[...] = low_dot(tokens[...], w_qkv[1])
    values[...] = low_dot(tokens[...], w_qkv[2])
    queries = by_head(low_dot(near[...], w_qkv[0]))
    scores = lax.dot_general(queries, keys[...], NT, preferred_element_type=F32) * scale
    top = jnp.max(scores, axis=1, keepdims=True)
    weights = jnp.exp(scores - top)
    total = jnp.sum(weights, axis=1, keepdims=True)
    prob = (weights / total).astype(BF16)
    mixed_wide = join_heads(jnp.dot(prob, values[...], preferred_element_type=F32))
    mixed = mixed_wide.astype(BF16)
    coarse[...] = near[...].astype(F32) + jnp.dot(
        mixed, w_proj[...], preferred_element_type=F32
    )
    log_sum = top + jnp.log(total)
    soft[...] = log_sum
    coarse_low = grad_coarse[...].astype(BF16)
    grad_proj[...] = lax.dot_general(
        own_rows(mixed), coarse_low, TN, preferred_element_type=F32
    )
    grad_mixed = lax.dot_general(coarse_low, w_proj[...], NT, preferred_element_type=F32)
    product = grad_mixed.astype(BF16).astype(F32) * own_rows(mixed_wide)
    lane = lax.broadcasted_iota(jnp.int32, product.shape, 1)
    inner = [
        jnp.sum(jnp.where(lane < HEAD_DIM, product, 0.0), axis=1, keepdims=True),
        jnp.sum(jnp.where(lane < HEAD_DIM, 0.0, product), axis=1, keepdims=True),
    ]
    logs = [own_rows(log_sum[:64]), own_rows(log_sum[64:])]
    token = lax.broadcasted_iota(jnp.int32, product.shape, 0)
    rows = []
    for pair in (logs, inner):
        row = jnp.zeros((1, 128), F32)
        for head in range(HEADS):
            for part, value in enumerate(split_three(pair[head])):
                slot = (head * 3 + part) * 16
                at = jnp.where(lane == token + slot, value.astype(F32), 0.0)
                row = row + jnp.sum(at, axis=0, keepdims=True)
        rows.append(row)
    text = jnp.concatenate([coarse_low.astype(F32)] + rows, axis=0).astype(BF16)
    for chip in range(CHIPS):
        message[chip] = text


def lane_stats(tables):
    count = DEVICES * 16
    part = lax.broadcasted_iota(jnp.int32, (DEVICES, 128), 1) >> 4
    rows = []
    for table in tables:
        wide = table.astype(F32)
        for head in range(HEADS):
            mine = (part >= 3 * head) & (part < 3 * head + 3)
            rows.append(jnp.where(mine, wide, 0.0).astype(BF16))
    slot = lax.broadcasted_iota(jnp.int32, (128, count), 0)
    lane = lax.broadcasted_iota(jnp.int32, (128, count), 1)
    chosen = jnp.where((slot & 15) == (lane & 15), 1.0, 0.0).astype(BF16)
    tiled = jnp.dot(jnp.concatenate(rows, axis=0), chosen, preferred_element_type=F32)
    entry = lax.broadcasted_iota(jnp.int32, (DEVICES, count), 0)
    device = ((entry & (CHIPS - 1)) << 1) + (entry >> 6)
    mine = device == (lax.broadcasted_iota(jnp.int32, (DEVICES, count), 1) >> 4)
    sums = []
    for index in range(len(rows)):
        block = tiled[index * DEVICES : (index + 1) * DEVICES]
        sums.append(jnp.sum(jnp.where(mine, block, 0.0), axis=0, keepdims=True))
    return sums


def prepare_kernel(tokens, near, keys, w_qkv, soft, queries, scores, prob, near_values):
    scale = HEAD_DIM**-0.5
    queries[...] = low_dot(tokens[...], w_qkv[0])
    near_q = by_head(low_dot(near[...], w_qkv[0]))
    near_k = by_head(low_dot(near[...], w_qkv[1]))
    near_values[...] = by_head(low_dot(near[...], w_qkv[2]))
    outward = lax.dot_general(near_q, keys[...], NT, preferred_element_type=F32) * scale
    prob[...] = jnp.exp(jnp.minimum(outward - soft[...], 0.0))
    scores[...] = lax.dot_general(near_k, queries[...], NT, preferred_element_type=F32) * scale


def attend_back_kernel(
    place, near, keys, values, queries, scores, prob_out, near_values, own, other, grad_coarse,
    w_qkv, w_proj, grad_tokens, grad_qkv,
):
    scale = HEAD_DIM**-0.5
    chans = own.shape[2]
    first_core = (place[1] & 1) == 0

    def in_order(cut):
        mine, theirs = cut(own).astype(F32), cut(other).astype(F32)
        return jnp.where(first_core, mine, theirs), jnp.where(first_core, theirs, mine)

    tokens_of = in_order(lambda half: half[:, :16, :])
    coarse_low = jnp.stack(tokens_of, axis=1).reshape(-1, chans).astype(BF16)
    count = coarse_low.shape[0]
    logs, inner = (
        jnp.concatenate(in_order(lambda half: half[:, row, :]), axis=0).astype(BF16)
        for row in (16, 17)
    )
    near_low = pick_near(place, coarse_low)
    mixed = lax.dot_general(coarse_low, w_proj[...], NT, preferred_element_type=F32).astype(BF16)
    near_mixed = lax.dot_general(
        near_low, w_proj[...], NT, preferred_element_type=F32
    ).astype(BF16)
    grad_prob = lax.dot_general(by_head(near_mixed), values[...], NT, preferred_element_type=F32)
    prob = prob_out[...]
    mean = jnp.sum(prob * grad_prob, axis=1, keepdims=True)
    grad_score = (prob * (grad_prob - mean) * scale).astype(BF16)
    grad_q = join_heads(jnp.dot(grad_score, keys[...], preferred_element_type=F32))

    stats = lane_stats((logs, inner))

    def both_heads(first, second):
        spread = [jnp.broadcast_to(row, (64, count)) for row in (first, second)]
        return jnp.concatenate(spread, axis=0)

    prob = jnp.exp(jnp.minimum(scores[...] - both_heads(*stats[:2]), 0.0))
    grad_prob = lax.dot_general(near_values[...], mixed, NT, preferred_element_type=F32)
    grad_score = (prob * (grad_prob - both_heads(*stats[2:])) * scale).astype(BF16)
    grad_k = join_heads(jnp.dot(grad_score, queries[...], preferred_element_type=F32))
    grad_v = join_heads(jnp.dot(prob.astype(BF16), mixed, preferred_element_type=F32))
    nearest = jnp.concatenate(
        [grad_coarse[0:8], near_low[8:16].astype(F32), grad_coarse[8:16]], axis=0
    )
    result = jnp.concatenate([nearest, near_low[24:].astype(F32)], axis=0)
    grads = jnp.concatenate([grad_q, grad_k, grad_v], axis=1)
    wide = jnp.concatenate([w_qkv[index].astype(F32) for index in range(3)], axis=1)
    result = result + lax.dot_general(
        grads, wide, NT, precision=HIGHEST, preferred_element_type=F32
    )
    own_tokens = own_rows(near[...].astype(F32))
    products = lax.dot_general(
        own_tokens, own_rows(grads), TN, precision=HIGHEST, preferred_element_type=F32
    )
    for index in range(3):
        grad_qkv[index] = products[:, index * chans : (index + 1) * chans]
    grad_tokens[...] = result


def row_of(index):
    if index == 0:
        return 3
    return min((index - 1) // PATCH, 2)


def inside(place, index, rows):
    if index == 0:
        return jnp.where(place[0] == 0, 0.0, 1.0)
    if index == rows - 1:
        return jnp.where(place[0] == 7, 0.0, 1.0)
    return None


def put_products(grads, rows_of):
    chans = grads.shape[3] // 3
    rows = 2 * grads.shape[1] - 2
    zero = jnp.zeros((grads.shape[2], chans), BF16)
    for row in range(-1, rows + 3):
        kept = rows_of(row - 1) if 0 < row < rows + 1 else zero
        for tap in range(3):
            target = row - 1 + tap
            if 0 <= target < rows + 2:
                odd, place = target & 1, target >> 1
                grads[odd, place, :, tap * chans : (tap + 1) * chans] = kept


def weight_grads(pieces, grads, result):
    chans = result.shape[1]
    width = grads.shape[2]
    total = jnp.zeros((3 * chans, 3 * chans), F32)
    for taps, first, count, odd, parity, place in pieces:
        left = taps[first : first + count, :, odd * 3 * chans : (odd + 1) * 3 * chans]
        right = grads[parity, place : place + count]
        total = total + lax.dot_general(
            left.reshape(count * width, 3 * chans),
            right.reshape(count * width, 3 * chans),
            TN,
            preferred_element_type=F32,
        )
    for tap in range(3):
        result[tap * 3 * chans : (tap + 1) * 3 * chans] = total[:, tap * chans : (tap + 1) * chans]


def halve(place, table, keep, send):
    half = keep.shape[0]
    core = place[1] & 1
    keep[...] = table[pl.ds(pl.multiple_of(core * half, 64), half)]
    send[...] = table[pl.ds(pl.multiple_of((1 - core) * half, 64), half)].astype(BF16)


def pick(inner, edge, index):
    rows = inner.shape[0]
    if index < 2:
        return edge[index]
    return inner[index - 2] if index < rows + 2 else edge[index - rows]


def products_kernel(cotangent, grads):
    chans = cotangent.shape[2]
    side = jnp.zeros((EDGE, chans), F32)

    def rows_of(row):
        parts = [side, cotangent[row].astype(F32), side]
        return jnp.concatenate(parts, axis=0).astype(BF16)

    put_products(grads, rows_of)


def decode_kernel(place, act, edge, coarse, grads, grad_proj, merged, keep, send, taps, table):
    rows, _, chans = merged.shape
    grid = [spread_row(coarse[16 * row : 16 * (row + 1)]) for row in range(4)]
    for index in range(rows):
        value = pick(act, edge, index).astype(F32) + grid[row_of(index)]
        factor = inside(place, index, rows)
        value = value if factor is None else value * factor
        merged[index] = value.astype(BF16)
        put_shifted(taps, index >> 1, index & 1, value)
    count = rows // 2
    weight_grads([(taps, 0, count, 0, 0, 0), (taps, 0, count, 1, 1, 0)], grads, table)
    table[9 * chans :] = grad_proj[...]
    halve(place, table, keep, send)


def hidden_kernel(
    place, slope, slope_edge, grad, grad_edge, grad_tokens, grad_qkv, taps, top, bottom,
    result, keep, send, ends, grads, table,
):
    rows, width, chans = result.shape
    for pair, field in enumerate((top, bottom)):
        put_rows(ends, pair, lambda index, field=field: field[index & 1].astype(F32))
    grid = [
        spread_row(grad_tokens[16 * row : 16 * (row + 1)] * (1.0 / (PATCH * PATCH)))
        for row in range(4)
    ]
    for index in range(rows):
        value = pick(grad, grad_edge, index).astype(F32) + grid[row_of(index)]
        value = value * pick(slope, slope_edge, index).astype(F32)
        factor = inside(place, index, rows)
        result[index] = (value if factor is None else value * factor).astype(BF16)
    column = lax.broadcasted_iota(jnp.int32, (width, chans), 0)
    own = (column >= EDGE) & (column < width - EDGE)

    def rows_of(row):
        return jnp.where(own, result[row + 1].astype(F32), 0.0).astype(BF16)

    put_products(grads, rows_of)
    count = taps.shape[0]
    pieces = [
        (taps, 0, count, 0, 1, 0), (taps, 0, count, 1, 0, 1),
        (ends, 0, 1, 1, 0, 0), (ends, 1, 1, 0, 1, count),
    ]
    weight_grads(pieces, grads, table)
    for index in range(3):
        table[(9 + index) * chans : (10 + index) * chans] = grad_qkv[index]
    halve(place, table, keep, send)


def last_kernel(hidden, merged, w_in, w_out, grad_inputs, outputs, taps, packed, taps_2, packed_2):
    put_weight(packed, w_in, True)
    put_weight(packed_2, w_out, False)

    def emit_to(result):
        def emit(pair, both):
            for odd, value in enumerate(halves(both)):
                result[2 * pair + odd] = value[EDGE : EDGE + 128].astype(BF16)

        return emit

    stream_conv(taps, packed, lambda index: hidden[index].astype(F32), emit_to(grad_inputs))
    stream_conv(taps_2, packed_2, lambda index: merged[index].astype(F32), emit_to(outputs))


def cut(tables, starts, start, stop):
    pieces = []
    for index, table in enumerate(tables):
        low, high = max(start, starts[index]), min(stop, starts[index + 1])
        if low < high:
            pieces.append((table, low - starts[index], high - starts[index], low - start))
    return pieces


def row_starts(tables):
    starts = [0]
    for table in tables:
        starts.append(starts[-1] + table.shape[0])
    return starts


def chip_sum_kernel(keep_a, keep_b, got_a, got_b, blocks, sum_a, sum_b):
    sum_a[...] = keep_a[...] + got_a[...].astype(F32)
    sum_b[...] = keep_b[...] + got_b[...].astype(F32)
    tables = (sum_a, sum_b)
    starts = row_starts(tables)
    share = blocks.shape[1]
    for chip in range(CHIPS):
        pieces = cut(tables, starts, chip * share, (chip + 1) * share)
        rows = [table[low:high] for table, low, high, _ in pieces]
        blocks[chip] = (rows[0] if len(rows) == 1 else jnp.concatenate(rows, axis=0)).astype(BF16)


def share_kernel(moved, copies):
    total = moved[0].astype(F32)
    for chip in range(1, CHIPS):
        total = total + moved[chip].astype(F32)
    total = total.astype(BF16)
    for chip in range(CHIPS):
        copies[chip] = total


def unpack_kernel(place, own, other, grad_in, grad_out, grad_qkv, grad_proj):
    share = own.shape[1]
    first_core = (place[1] & 1) == 0
    half_a = (grad_in.shape[0] + grad_qkv.shape[0]) // 2
    half_b = (grad_out.shape[0] + grad_proj.shape[0]) // 2
    for chip in range(CHIPS):
        mine, theirs = own[chip].astype(F32), other[chip].astype(F32)
        cores = (jnp.where(first_core, mine, theirs), jnp.where(first_core, theirs, mine))
        for core, piece in enumerate(cores):
            for half, start, tables in (
                (half_a, 0, (grad_in, grad_qkv)),
                (half_b, half_a, (grad_out, grad_proj)),
            ):
                low = max(chip * share, start)
                high = min((chip + 1) * share, start + half)
                base = core * half - start
                for table, first, last, offset in cut(
                    tables, row_starts(tables), low + base, high + base
                ):
                    offset = offset + low - chip * share
                    table[first:last] = piece[offset : offset + last - first]


def exchange(blocks, axes):
    return lax.all_to_all(blocks, axes, 0, 0, tiled=True)


def body(inputs, cotangent, w_in, w_out, w_qkv, w_proj):
    rows, cols, chans = inputs.shape
    width = cols + 2 * EDGE
    place = jnp.stack([lax.axis_index("lat"), lax.axis_index(LON)]).astype(jnp.int32)
    shape = jax.ShapeDtypeStruct
    whole = pl.BlockSpec(memory_space=pltpu.VMEM)
    scalars = pl.BlockSpec(memory_space=pltpu.SMEM)
    conv_flops = 2 * rows * cols * 9 * chans * chans
    packed = pltpu.VMEM((12 * chans, 2 * chans), BF16)
    grads = pltpu.VMEM((2, rows // 2 + 1, width, 3 * chans), BF16)

    def taps(count):
        return pltpu.VMEM((count // 2, width, 6 * chans), BF16)

    lats, lons = lax.axis_size("lat"), lax.axis_size("chip") * lax.axis_size("core")
    up = [(i, i + 1) for i in range(lats - 1)]
    down = [(i + 1, i) for i in range(lats - 1)]
    east = [(i, (i + 1) % lons) for i in range(lons)]
    west = [((i + 1) % lons, i) for i in range(lons)]

    def two(cut):
        return jnp.concatenate([cut(inputs), cut(cotangent)], axis=0)

    left = lax.ppermute(two(lambda field: field[:, cols - HALO :]), LON, east)
    right = lax.ppermute(two(lambda field: field[:, :HALO]), LON, west)

    def wide_pair(start):
        def cut(side):
            return jnp.concatenate(
                [side[start : start + 2], side[rows + start : rows + start + 2]], axis=0
            )

        own = two(lambda field: field[start : start + 2])
        row = jnp.concatenate([cut(left), own, cut(right)], axis=1)
        return jnp.pad(row, ((0, 0), (EDGE - HALO, EDGE - HALO), (0, 0)))

    first, last = wide_pair(0), wide_pair(rows - 2)
    top = lax.ppermute(last, "lat", up)
    bottom = lax.ppermute(first, "lat", down)
    inner_field = shape((rows - 2, width, chans), BF16)
    edge_field = shape((4, width, chans), BF16)
    field = shape((rows + 2, width, chans), BF16)
    products = call(products_kernel, shape(grads.shape, BF16), flops=2**27)(cotangent)
    act, slope, grad, sums, taps_in = call(
        inner_kernel,
        (
            inner_field,
            inner_field,
            inner_field,
            shape((32, chans), F32),
            shape((rows // 2, width, 6 * chans), BF16),
        ),
        [taps(rows), packed, packed],
        2 * conv_flops,
    )(inputs, cotangent, left, right, w_in, w_out)
    act_edge, slope_edge, grad_edge, copies, grad_coarse = call(
        edge_kernel,
        (
            edge_field,
            edge_field,
            edge_field,
            shape((DEVICES * 16, chans), BF16),
            shape((16, chans), F32),
        ),
        [taps(8), packed],
        conv_flops // 4,
    )(first, last, top, bottom, w_in, w_out, sums)
    copies, products, place = lax.optimization_barrier((copies, products, place))
    tokens_all = exchange(copies, AXES)
    table = shape((DEVICES * 16, chans), BF16)
    coarse, message, grad_w_proj, soft, near, keys, values = call(
        attend_kernel,
        (
            shape((64, chans), F32),
            shape((CHIPS, 18, chans), BF16),
            shape((chans, chans), F32),
            shape((128, 1), F32),
            shape((64, chans), BF16),
            table,
            table,
        ),
        flops=2**28,
        in_specs=[scalars] + [whole] * 4,
    )(place, tokens_all, w_qkv, w_proj, grad_coarse)
    merged, keep_b, send_b = call(
        decode_kernel,
        (field, shape((5 * chans, chans), F32), shape((5 * chans, chans), BF16)),
        [taps(rows + 2), pltpu.VMEM((10 * chans, chans), F32)],
        2 * conv_flops,
        in_specs=[scalars] + [whole] * 5,
    )(place, act, act_edge, coarse, products, grad_w_proj)
    message, send_b = lax.optimization_barrier((message, send_b))
    swap = [(0, 1), (1, 0)]
    own = exchange(message, ("lat", "chip"))
    own, tokens_all = lax.optimization_barrier((own, tokens_all))
    other = lax.ppermute(own, "core", swap)
    wide = shape((128, DEVICES * 16), F32)
    queries, scores, prob, near_values = call(
        prepare_kernel,
        (table, wide, wide, shape((128, chans), BF16)),
        flops=2**28,
    )(tokens_all, near, keys, w_qkv, soft)
    grad_tokens, grad_w_qkv = call(
        attend_back_kernel,
        (shape((64, chans), F32), shape((3, chans, chans), F32)),
        flops=2**28,
        in_specs=[scalars] + [whole] * 12,
    )(
        place, near, keys, values, queries, scores, prob, near_values, own, other, grad_coarse,
        w_qkv, w_proj,
    )
    got_b = lax.ppermute(send_b, "core", swap)
    grad_hidden, keep_a, send_a = call(
        hidden_kernel,
        (field, shape((6 * chans, chans), F32), shape((6 * chans, chans), BF16)),
        [taps(4), grads, pltpu.VMEM((12 * chans, chans), F32)],
        conv_flops,
        in_specs=[scalars] + [whole] * 9,
    )(
        place, slope, slope_edge, grad, grad_edge, grad_tokens, grad_w_qkv, taps_in, top, bottom
    )
    got_a = lax.ppermute(send_a, "core", swap)
    share = 11 * chans // CHIPS
    blocks = call(
        chip_sum_kernel,
        shape((CHIPS, share, chans), BF16),
        [pltpu.VMEM(keep.shape, F32) for keep in (keep_a, keep_b)],
    )(keep_a, keep_b, got_a, got_b)
    partial = exchange(blocks, ("lat", "chip"))
    grad_inputs, outputs = call(
        last_kernel,
        (shape((rows, cols, chans), BF16), shape((rows, cols, chans), BF16)),
        [taps(rows + 2), packed, taps(rows + 2), packed],
        2 * conv_flops,
    )(grad_hidden, merged, w_in, w_out)
    partial, grad_inputs = lax.optimization_barrier((partial, grad_inputs))
    copies = call(share_kernel, shape(blocks.shape, BF16))(partial)
    own = exchange(copies, ("lat", "chip"))
    other = lax.ppermute(own, "core", swap)
    shapes = (w_in.shape, w_out.shape, w_qkv.shape, w_proj.shape)
    pieces = call(
        unpack_kernel,
        tuple(shape((size * chans, chans), F32) for size in (9, 9, 3, 1)),
        in_specs=[scalars, whole, whole],
    )(place, own, other)
    pieces = [piece.reshape(dims) for piece, dims in zip(pieces, shapes)]
    return (outputs, grad_inputs, *pieces)


def solution(mesh):
    lats, lons = mesh.devices.shape
    fine = jax.sharding.Mesh(mesh.devices.reshape(lats, lons // 2, 2), AXES)
    field, whole = P("lat", LON, None), P()
    in_specs = (field, field, whole, whole, whole, whole)
    out_specs = (field, field, whole, whole, whole, whole)
    return jax.shard_map(body, mesh=fine, in_specs=in_specs, out_specs=out_specs, check_vma=False)
```
